32 devices in a mesh: row: 8 (over z, core), seq: 4 (over y, x).
Axes of the slice: x: 2, y: 2, z: 4, core: 2. Of those that a mesh axis runs over, the one named last changes fastest.
Arguments:
- frames: bfloat16 [8, 2048, 1536], P('row', 'seq'), may hold values from -6 to 6
- context: bfloat16 [8, 128, 768], P('row'), may hold values from -6 to 6
- seg_lengths: int32 [8, 8], P('row'), may hold values from 1 to 2041, as said below
- bucket_ids: int32 [8], replicated, may hold values from 0 to 4, as said below
- timesteps: int32 [5], replicated, may hold values from 0 to 999
- bucket_weights: float32 [5], replicated, may hold values from 0.5 to 2
- w_time_in: bfloat16 [256, 1536], P(('row', 'seq')), may hold values from -0.5 to 0.5
- w_time_out: bfloat16 [1536, 1536], P(('row', 'seq')), may hold values from -0.15625 to 0.15625
- w_mod: bfloat16 [1536, 9216], P(('row', 'seq')), may hold values from -0.15625 to 0.15625
- w_qkv: bfloat16 [1536, 4608], P(('row', 'seq')), may hold values from -0.15625 to 0.15625
- w_attn_out: bfloat16 [1536, 1536], P(('row', 'seq')), may hold values from -0.875 to 0.875
- cross_gain: bfloat16 [1536], P(('row', 'seq')), may hold values from 0.099609375 to 1.8984375
- w_cross_q: bfloat16 [1536, 1536], P(('row', 'seq')), may hold values from -0.15625 to 0.15625
- w_cross_kv: bfloat16 [768, 3072], P(('row', 'seq')), may hold values from -0.21875 to 0.21875
- w_cross_out: bfloat16 [1536, 1536], P(('row', 'seq')), may hold values from -0.4375 to 0.4375
- w_glu: bfloat16 [1536, 12288], P(('row', 'seq')), may hold values from -0.15625 to 0.15625
- w_down: bfloat16 [6144, 1536], P(('row', 'seq')), may hold values from -0.078125 to 0.078125
- cotangent: bfloat16 [8, 2048, 1536], P('row', 'seq'), may hold values from -6 to 6
Outputs:
- out: bfloat16 [8, 2048, 1536], P('row', 'seq')
- grad_frames: float32 [8, 2048, 1536], P('row', 'seq')
- grad_time_in: float32 [256, 1536], P(('row', 'seq'))
- grad_time_out: float32 [1536, 1536], P(('row', 'seq'))
- grad_mod: float32 [1536, 9216], P(('row', 'seq'))
- grad_qkv: float32 [1536, 4608], P(('row', 'seq'))
- grad_attn_out: float32 [1536, 1536], P(('row', 'seq'))
- grad_cross_gain: float32 [1536], P(('row', 'seq'))
- grad_cross_q: float32 [1536, 1536], P(('row', 'seq'))
- grad_cross_kv: float32 [768, 3072], P(('row', 'seq'))
- grad_cross_out: float32 [1536, 1536], P(('row', 'seq'))
- grad_glu: float32 [1536, 12288], P(('row', 'seq'))
- grad_down: float32 [6144, 1536], P(('row', 'seq'))
The draws below stay inside these ranges and needn't reach their ends.
Inputs may be any that keep to these rules, and one draw needn't show every extreme that they name: `seg_lengths`: each row's 8 lengths are positive and sum to 2048; some row holds a clip of exactly 2041 frames. `bucket_ids`: never falling along the rows, and each of the 5 buckets holds at least one row.
All inputs are finite; a program needn't handle non-finite values.
Results may differ from the reference program's by a relative error of at most 0.02.
Values may be sent and summed in bfloat16 or wider, within the bound.
No kernel may reach another device: no remote copies, remote signals or barrier semaphores. Data moves between devices by JAX's collectives and lax.ppermute only.
A program may use at most 640 MiB of HBM per device.

```python
import math
import jax
import jax.numpy as jnp
from jax import lax

D = 1536
HEADS = 24
HEAD_DIM = 64
FF = 6144
CTX_DIM = 768
CTX_LEN = 128
TFREQ = 256
LENGTH = 2048
SEGS = 8
BUCKETS = 5
FRAMES = 512
ROWS = 8


def draw_seg_lengths(key, part):
    key = jax.random.fold_in(key, 11)
    pick_key, size_key, row_key = jax.random.split(key, 3)
    longest = jax.random.randint(pick_key, (ROWS, 1), 0, SEGS)
    shorts = jax.random.randint(size_key, (ROWS, SEGS), 1, FRAMES // SEGS + 1)
    chosen_row = jax.random.randint(row_key, (), 0, ROWS)
    row_index = jnp.arange(ROWS, dtype=jnp.int32)[:, None]
    shorts = jnp.where(row_index == chosen_row, 1, shorts)
    slot_index = jnp.arange(SEGS, dtype=jnp.int32)[None, :]
    others = jnp.where(slot_index == longest, 0, shorts)
    remainder = LENGTH - jnp.sum(others, axis=1, keepdims=True)
    return jnp.where(slot_index == longest, remainder, others).astype(jnp.int32)


def draw_bucket_ids(key, part):
    key = jax.random.fold_in(key, 23)
    cut_rows = jax.random.permutation(key, ROWS - 1)[:BUCKETS - 1] + 1
    marks = (jnp.arange(ROWS, dtype=jnp.int32)[:, None] >= cut_rows[None, :]).astype(jnp.int32)
    return jnp.sum(marks, axis=1).astype(jnp.int32)


def set_ends(result, key, least, largest):
    longest = result.shape.index(max(result.shape))
    spots = []
    for shift in (0, 1):
        where = [jax.random.randint(jax.random.fold_in(key, axis), (), 0, length) for axis, length in enumerate(result.shape)]
        where[longest] = (where[longest] + shift) % result.shape[longest]
        spots.append(tuple(where))
    return result.at[spots[0]].set(least).at[spots[1]].set(largest)


def shard_levels(rng, shape, cuts, least, top_value):
    def one(dim, parts):
        heights = jax.random.uniform(jax.random.fold_in(jax.random.fold_in(rng, 6), dim), (parts,), jnp.float32, least / len(cuts), top_value / len(cuts))
        return jnp.repeat(jnp.exp(heights), shape[dim] // parts).reshape((-1,) + (1,) * (len(shape) - dim - 1))

    gain = one(*cuts[0])
    for cut in cuts[1:]:
        gain = gain * one(*cut)
    return gain


def scatter_about(key, extent, width, reach, cuts=(), held_as=jnp.bfloat16):
    factor_of = shard_levels(key, extent, cuts, -0.22, 0.18) if cuts else 1.0
    result = jax.random.normal(key, extent, jnp.float32) * width * factor_of
    return jnp.minimum(jnp.maximum(result, -reach), reach).astype(held_as)


def setup_inputs(seed: int = 0) -> dict:
    keys = jax.random.split(jax.random.key(seed), 19)
    return {
        "frames": scatter_about(keys[0], (ROWS, LENGTH, D), 1.0, 6.0, ((0, 8), (1, 4))),
        "context": scatter_about(keys[1], (ROWS, CTX_LEN, CTX_DIM), 1.0, 6.0, ((0, 8),)),
        "seg_lengths": draw_seg_lengths(jax.random.fold_in(keys[18], 71), 0),
        "bucket_ids": draw_bucket_ids(jax.random.fold_in(keys[18], 71), 0),
        "timesteps": set_ends(jax.random.randint(keys[4], (BUCKETS,), 0, 1000), jax.random.fold_in(keys[4], 1), 0, 999).astype(jnp.int32),
        "bucket_weights": jnp.clip(jnp.exp(jax.random.uniform(keys[5], (BUCKETS,), jnp.float32, math.log(0.5), math.log(2.0))), 0.5, 2.0),
        "w_time_in": scatter_about(keys[6], (TFREQ, D), (TFREQ // 2) ** -0.5, 0.5, ((0, 32),)),
        "w_time_out": scatter_about(keys[7], (D, D), D ** -0.5, 0.15625, ((0, 32),)),
        "w_mod": scatter_about(keys[8], (D, 6 * D), D ** -0.5, 0.15625, ((0, 32),)),
        "w_qkv": scatter_about(keys[9], (D, 3 * D), D ** -0.5, 0.15625, ((0, 32),)),
        "w_attn_out": scatter_about(keys[10], (D, D), (D // 32) ** -0.5, 0.875, ((0, 32),)),
        "cross_gain": jnp.clip(1.0 + 0.18 * jax.random.normal(keys[11], (D,), jnp.float32), 0.099609375, 1.8984375).astype(jnp.bfloat16),
        "w_cross_q": scatter_about(keys[12], (D, D), D ** -0.5, 0.15625, ((0, 32),)),
        "w_cross_kv": scatter_about(keys[13], (CTX_DIM, 2 * D), CTX_DIM ** -0.5, 0.21875, ((0, 32),)),
        "w_cross_out": scatter_about(keys[14], (D, D), (D // 8) ** -0.5, 0.4375, ((0, 32),)),
        "w_glu": scatter_about(keys[15], (D, 2 * FF), D ** -0.5, 0.15625, ((0, 32),)),
        "w_down": scatter_about(keys[16], (FF, D), FF ** -0.5, 0.078125, ((0, 32),)),
        "cotangent": scatter_about(keys[17], (ROWS, LENGTH, D), 1.0, 6.0, ((0, 8), (1, 4))),
    }


@jax.custom_vjp
def low(v):
    return lax.optimization_barrier(v.astype(jnp.bfloat16)).astype(jnp.float32)

@jax.custom_vjp
def low_back(v):
    return v

def low_keep(v):
    return (low(v), None)

def low_pass(kept, grad):
    return (grad,)

def back_keep(v):
    return (v, None)

def back_low(kept, grad):
    return (low(grad),)
low.defvjp(low_keep, low_pass)
low_back.defvjp(back_keep, back_low)
highest = lax.Precision.HIGHEST

def dense(left, right):
    return jnp.einsum('...i,ij->...j', left, right, precision=highest)

def layer_norm(values):
    center = values - lax.optimization_barrier(jnp.mean(values, axis=-1, keepdims=True))
    return center * lax.rsqrt(lax.optimization_barrier(jnp.mean(center * center, axis=-1, keepdims=True)) + 1e-05)

def angle_tables(positions):
    half_dim = HEAD_DIM // 2
    inverse = jnp.exp(-math.log(10000.0) * jnp.arange(half_dim, dtype=jnp.float32) / half_dim)
    angles = positions[:, None] * inverse[None, :]
    return (jnp.cos(angles)[:, None, :], jnp.sin(angles)[:, None, :])

def rotate(values, cosine, sine_table):
    half_dim = values.shape[-1] // 2
    first_half = values[..., :half_dim]
    second_half = values[..., half_dim:]
    return jnp.concatenate([first_half * cosine - second_half * sine_table, second_half * cosine + first_half * sine_table], axis=-1)

def time_features(times):
    half_dim = TFREQ // 2
    freqs = jnp.exp(-math.log(10000.0) * jnp.arange(half_dim, dtype=jnp.float32) / half_dim)
    angles = times[:, None] * freqs[None, :]
    return jnp.concatenate([jnp.cos(angles), jnp.sin(angles)], axis=-1)

def softmax_block(query_block, key_rows, value_rows, allowed):
    scores = jnp.einsum('qhd,khd->hqk', query_block, key_rows, precision=highest) * 0.125
    scores = low_back(scores)
    scores = jnp.where(allowed[None], scores, -1e+30)
    shifted = jnp.exp(scores - lax.optimization_barrier(jnp.max(scores, axis=-1, keepdims=True)))
    soft_weights = low(shifted / lax.optimization_barrier(jnp.sum(shifted, axis=-1, keepdims=True)))
    return jnp.einsum('hqk,khd->qhd', soft_weights, value_rows, precision=highest)

def attend(queries, key_rows, value_rows, query_ids, key_ids):
    length = queries.shape[0]
    block_rows = min(512, length)
    block_count = length // block_rows
    blocked_queries = queries.reshape(block_count, block_rows, HEADS, HEAD_DIM)
    blocked_ids = query_ids.reshape(block_count, block_rows)

    def block_step(block_inputs):
        query_block, id_block = block_inputs
        return softmax_block(query_block, key_rows, value_rows, id_block[:, None] == key_ids[None, :])
    mixed_blocks = lax.map(jax.checkpoint(block_step), (blocked_queries, blocked_ids))
    return mixed_blocks.reshape(length, HEADS * HEAD_DIM)

def row_forward(frame_rows, context_rows, modulation, segment_ids, weights):
    qkv_w, attn_w, gain_w, crossq_w, crosskv_w, crossout_w, glu_w, down_w = weights
    shift_attn, scale_attn, gate_attn, shift_ffn, scale_ffn, gate_ffn = jnp.split(modulation, 6)
    length = frame_rows.shape[0]
    attn_in = low(layer_norm(frame_rows) * (1.0 + scale_attn) + shift_attn)
    projected = low_back(dense(attn_in, qkv_w))
    query_pre = projected[:, :D].reshape(length, HEADS, HEAD_DIM)
    key_pre = projected[:, D:2 * D].reshape(length, HEADS, HEAD_DIM)
    value_pre = projected[:, 2 * D:].reshape(length, HEADS, HEAD_DIM)
    cosine, sine_table = angle_tables(jnp.arange(length, dtype=jnp.float32))
    queries = low(rotate(query_pre, cosine, sine_table))
    key_rows = low(rotate(key_pre, cosine, sine_table))
    value_rows = low(value_pre)
    attn_mixed = low(low_back(attend(queries, key_rows, value_rows, segment_ids, segment_ids)))
    attn_out = low_back(dense(attn_mixed, attn_w))
    after_attn = frame_rows + gate_attn * attn_out
    cross_in = low(layer_norm(after_attn) * gain_w)
    cross_q = low(low_back(dense(cross_in, crossq_w))).reshape(length, HEADS, HEAD_DIM)
    cross_kv = low(dense(context_rows, crosskv_w))
    cross_k = cross_kv[:, :D].reshape(CTX_LEN, HEADS, HEAD_DIM)
    cross_v = cross_kv[:, D:].reshape(CTX_LEN, HEADS, HEAD_DIM)
    query_zero = jnp.zeros((length,), jnp.int32)
    text_zero = jnp.zeros((CTX_LEN,), jnp.int32)
    cross_mixed = low(low_back(attend(cross_q, cross_k, cross_v, query_zero, text_zero)))
    cross_out = low_back(dense(cross_mixed, crossout_w))
    after_cross = after_attn + cross_out
    ffn_in = low(layer_norm(after_cross) * (1.0 + scale_ffn) + shift_ffn)
    gate_up = low_back(dense(ffn_in, glu_w))
    gate_pre = gate_up[:, :FF]
    up_pre = gate_up[:, FF:]
    hidden = low(jax.nn.silu(gate_pre) * up_pre)
    ffn_out = low_back(dense(hidden, down_w))
    return after_cross + gate_ffn * ffn_out

def reference(frames, context, seg_lengths, bucket_ids, timesteps, bucket_weights, w_time_in, w_time_out, w_mod, w_qkv, w_attn_out, cross_gain, w_cross_q, w_cross_kv, w_cross_out, w_glu, w_down, cotangent):
    context_values = context.astype(jnp.float32)
    bounds = jnp.cumsum(seg_lengths, axis=-1).astype(jnp.int32)
    positions = jnp.arange(LENGTH, dtype=jnp.int32)
    segment_ids = lax.optimization_barrier(jnp.sum((positions[None, :, None] >= bounds[:, None, :]).astype(jnp.int32), axis=-1))
    time_values = timesteps.astype(jnp.float32)

    def forward(frame_all, time_in, time_out, modul, qkv_w, attn_w, gain_w, crossq_w, crosskv_w, crossout_w, glu_w, down_w):
        features = low(time_features(time_values))
        time_hidden = low(jax.nn.silu(dense(features, time_in)))
        time_token = dense(time_hidden, time_out)
        modulation = dense(low(jax.nn.silu(time_token)), modul)
        row_mods = modulation[bucket_ids]
        weights = (qkv_w, attn_w, gain_w, crossq_w, crosskv_w, crossout_w, glu_w, down_w)

        def row_step(row_inputs):
            frame_rows, context_rows, modulation_row, ids_row = row_inputs
            return row_forward(frame_rows, context_rows, modulation_row, ids_row, weights)
        return lax.map(jax.checkpoint(row_step), (frame_all, context_values, row_mods, segment_ids))
    params = jax.tree.map(lambda argument: argument.astype(jnp.float32), (frames, w_time_in, w_time_out, w_mod, w_qkv, w_attn_out, cross_gain, w_cross_q, w_cross_kv, w_cross_out, w_glu, w_down))
    output, pullback = jax.vjp(forward, *params)
    row_scale = bucket_weights.astype(jnp.float32)[bucket_ids]
    grads = pullback(cotangent.astype(jnp.float32) * row_scale[:, None, None])
    return (output.astype(jnp.bfloat16), grads[0], grads[1], grads[2], grads[3], grads[4], grads[5], grads[6], grads[7], grads[8], grads[9], grads[10], grads[11])
```

```python
import functools
import math

import jax
import jax.numpy as jnp
from jax import lax
from jax.experimental import pallas as pl
from jax.experimental.pallas import tpu as pltpu
from jax.sharding import PartitionSpec as P

D = 1536
HEADS = 24
HEAD_DIM = 64
FF = 6144
TFREQ = 256
LENGTH = 2048
BUCKETS = 5
PAIR = 2 * HEAD_DIM
VMEM = 50 * 1024 * 1024
f32 = jnp.float32
bf16 = jnp.bfloat16


def dot_nt(left, right):
    return lax.dot_general(left, right, (((1,), (1,)), ((), ())), preferred_element_type=f32)


def dot_nn(left, right):
    return lax.dot_general(left, right, (((1,), (0,)), ((), ())), preferred_element_type=f32)


def swap_halves(values):
    lane = lax.broadcasted_iota(jnp.int32, values.shape, 1)
    ahead = pltpu.roll(values, PAIR - HEAD_DIM // 2, 1)
    behind = pltpu.roll(values, HEAD_DIM // 2, 1)
    return jnp.where((lane & (HEAD_DIM // 2)) == 0, ahead, behind)


def head_lanes(values, head):
    lane = lax.broadcasted_iota(jnp.int32, values.shape, 1)
    return jnp.where((lane // HEAD_DIM) == head, values, 0.0)


def project_kernel(x_ref, scale_ref, shift_ref, w_ref, cos_ref, sin_ref, in_ref, out_ref):
    values = x_ref[...].astype(f32)
    center = values - jnp.mean(values, axis=-1, keepdims=True)
    inv_std = lax.rsqrt(jnp.mean(center * center, axis=-1, keepdims=True) + 1e-05)
    modulated = (center * inv_std * scale_ref[...] + shift_ref[...]).astype(bf16)
    in_ref[...] = modulated
    projected = dot_nn(modulated, w_ref[...])
    cosine = cos_ref[...]
    sine = sin_ref[...]
    width = out_ref.shape[1]
    for start in range(0, width, PAIR):
        part = projected[:, start : start + PAIR]
        if start < 2 * width // 3:
            part = part * cosine + swap_halves(part) * sine
        out_ref[:, start : start + PAIR] = part.astype(bf16)


def project(x, scale, shift, w, cosine, sine, block=256):
    count, depth = x.shape
    width = w.shape[1]
    row_spec = lambda cols: pl.BlockSpec((block, cols), lambda i: (i, 0))
    whole = lambda a: pl.BlockSpec(a.shape, lambda i: (0, 0))
    return pl.pallas_call(
        project_kernel,
        grid=(count // block,),
        in_specs=[row_spec(depth), whole(scale), whole(shift), whole(w), row_spec(PAIR), row_spec(PAIR)],
        out_specs=[row_spec(depth), row_spec(width)],
        out_shape=[
            jax.ShapeDtypeStruct((count, depth), bf16),
            jax.ShapeDtypeStruct((count, width), bf16),
        ],
        compiler_params=pltpu.CompilerParams(vmem_limit_bytes=VMEM),
        cost_estimate=pl.CostEstimate(
            flops=2 * count * depth * width,
            bytes_accessed=2 * (2 * count * depth + depth * width + count * width),
            transcendentals=count,
        ),
        name="project",
    )(x, scale, shift, w, cosine, sine)


def attend_kernel(masked, *refs):
    if masked:
        q_ref, k_ref, v_ref, qmask_ref, kmask_ref, o_ref, lse_ref, keys, values_t = refs
    else:
        q_ref, k_ref, v_ref, o_ref, lse_ref, keys, values_t = refs

    @pl.when(pl.program_id(1) == 0)
    def _():
        keys[:, :PAIR] = k_ref[...]
        if masked:
            keys[:, PAIR:] = kmask_ref[...]
        values_t[...] = v_ref[...].astype(f32).T.astype(bf16)

    queries = q_ref[...].astype(f32) * 0.125
    mixed = []
    for head in range(2):
        query = head_lanes(queries, head).astype(bf16)
        if masked:
            query = jnp.concatenate([query, qmask_ref[...]], axis=1)
        scores = dot_nt(keys[...], query)
        top = jnp.max(scores, axis=0, keepdims=True)
        shifted = jnp.exp(scores - top)
        total = jnp.sum(shifted, axis=0, keepdims=True)
        own = values_t[head * HEAD_DIM : (head + 1) * HEAD_DIM, :]
        mixed.append(dot_nn(own, shifted.astype(bf16)) / total)
        lse_ref[0, head : head + 1, :] = top + jnp.log(total)
    o_ref[...] = jnp.concatenate(mixed, axis=0).T.astype(bf16)


def attend(q, k, v, q_col, k_col, v_col, pairs, block, masks=None):
    count, keys = q.shape[0], k.shape[0]
    masked = masks is not None
    in_specs = [
        pl.BlockSpec((block, PAIR), lambda p, i: (i, q_col + p)),
        pl.BlockSpec((keys, PAIR), lambda p, i: (0, k_col + p)),
        pl.BlockSpec((keys, PAIR), lambda p, i: (0, v_col + p)),
    ]
    if masked:
        in_specs += [
            pl.BlockSpec((block, PAIR), lambda p, i: (i, 0)),
            pl.BlockSpec((keys, PAIR), lambda p, i: (0, 0)),
        ]
    return pl.pallas_call(
        functools.partial(attend_kernel, masked),
        grid=(pairs, count // block),
        in_specs=in_specs,
        out_specs=[
            pl.BlockSpec((block, PAIR), lambda p, i: (i, p)),
            pl.BlockSpec((1, 2, block), lambda p, i: (p, 0, i)),
        ],
        out_shape=[
            jax.ShapeDtypeStruct((count, pairs * PAIR), bf16),
            jax.ShapeDtypeStruct((pairs, 2, count), f32),
        ],
        scratch_shapes=[
            pltpu.VMEM((keys, (2 if masked else 1) * PAIR), bf16),
            pltpu.VMEM((PAIR, keys), bf16),
        ],
        compiler_params=pltpu.CompilerParams(vmem_limit_bytes=VMEM),
        cost_estimate=pl.CostEstimate(
            flops=16 * pairs * PAIR * count * keys,
            bytes_accessed=2 * pairs * PAIR * (2 * count + 2 * keys),
            transcendentals=2 * pairs * count * keys,
        ),
        name="attend",
    )(q, k, v, *(masks or ()))


def attend_back_kernel(masked, chunk, *refs):
    if masked:
        (q_ref, k_ref, v_ref, do_ref, o_ref, lse_ref, qmask_ref, kmask_ref, qcos_ref, qsin_ref,
         kcos_ref, ksin_ref, dq_ref, dk_ref, dv_ref, keys, keys_t, dk_sum, dv_sum) = refs
    else:
        (q_ref, k_ref, v_ref, do_ref, o_ref, lse_ref,
         dq_ref, dk_ref, dv_ref, keys, keys_t, dk_sum, dv_sum) = refs
    step = pl.program_id(1)
    count = k_ref.shape[0]

    @pl.when(step == 0)
    def _():
        keys[:, :PAIR] = k_ref[...]
        if masked:
            keys[:, PAIR:] = kmask_ref[...]
        keys_t[...] = k_ref[...].astype(f32).T.astype(bf16)
        dk_sum[...] = jnp.zeros_like(dk_sum)
        dv_sum[...] = jnp.zeros_like(dv_sum)

    queries = q_ref[...].astype(f32) * 0.125
    grads = do_ref[...].astype(f32)
    rows_t = (grads * o_ref[...].astype(f32)).T
    parts = []
    for head in range(2):
        lanes = slice(head * HEAD_DIM, (head + 1) * HEAD_DIM)
        delta = jnp.sum(rows_t[lanes, :], axis=0, keepdims=True)
        log_row = lse_ref[0, head : head + 1, :]
        query = head_lanes(queries, head).astype(bf16)
        grad = head_lanes(grads, head).astype(bf16)
        full = jnp.concatenate([query, qmask_ref[...]], axis=1) if masked else query
        total = None
        for start in range(0, count, chunk):
            here = slice(start, start + chunk)
            soft = jnp.exp(dot_nt(keys[here, :], full) - log_row)
            grad_soft = dot_nt(v_ref[here, :], grad)
            grad_scores = (soft * (grad_soft - delta)).astype(bf16)
            dv_sum[here, :] += dot_nn(soft.astype(bf16), grad)
            dk_sum[here, :] += dot_nn(grad_scores, query)
            part = dot_nn(keys_t[lanes, here], grad_scores)
            total = part if total is None else total + part
        parts.append(total)
    dq = jnp.concatenate(parts, axis=0).T * 0.125
    if masked:
        dq = dq * qcos_ref[...] - swap_halves(dq) * qsin_ref[...]
    dq_ref[...] = dq.astype(dq_ref.dtype)

    @pl.when(step == pl.num_programs(1) - 1)
    def _():
        dk = dk_sum[...]
        if masked:
            dk = dk * kcos_ref[...] - swap_halves(dk) * ksin_ref[...]
        dk_ref[...] = dk.astype(dk_ref.dtype)
        dv_ref[...] = dv_sum[...].astype(dv_ref.dtype)


def attend_back(q, k, v, do, o, lse, q_col, k_col, v_col, pairs, block, chunk, masks=None, tables=None):
    count, keys = q.shape[0], k.shape[0]
    masked = masks is not None
    out_type = bf16 if masked else f32
    rows = lambda col: pl.BlockSpec((block, PAIR), lambda p, i: (i, col + p))
    whole = lambda col: pl.BlockSpec((keys, PAIR), lambda p, i: (0, col + p))
    in_specs = [
        rows(q_col), whole(k_col), whole(v_col), rows(0), rows(0),
        pl.BlockSpec((1, 2, block), lambda p, i: (p, 0, i)),
    ]
    operands = [q, k, v, do, o, lse]
    if masked:
        rows_fixed = pl.BlockSpec((block, PAIR), lambda p, i: (i, 0))
        whole_fixed = pl.BlockSpec((keys, PAIR), lambda p, i: (0, 0))
        in_specs += [rows_fixed, whole_fixed, rows_fixed, rows_fixed, whole_fixed, whole_fixed]
        operands += [masks[0], masks[1], tables[0], tables[1], tables[0], tables[1]]
    return pl.pallas_call(
        functools.partial(attend_back_kernel, masked, chunk),
        grid=(pairs, count // block),
        in_specs=in_specs,
        out_specs=[rows(0), whole(0), whole(0)],
        out_shape=[
            jax.ShapeDtypeStruct((count, pairs * PAIR), bf16),
            jax.ShapeDtypeStruct((keys, pairs * PAIR), out_type),
            jax.ShapeDtypeStruct((keys, pairs * PAIR), out_type),
        ],
        scratch_shapes=[
            pltpu.VMEM((keys, (2 if masked else 1) * PAIR), bf16),
            pltpu.VMEM((PAIR, keys), bf16),
            pltpu.VMEM((keys, PAIR), f32),
            pltpu.VMEM((keys, PAIR), f32),
        ],
        compiler_params=pltpu.CompilerParams(vmem_limit_bytes=VMEM),
        cost_estimate=pl.CostEstimate(
            flops=40 * pairs * PAIR * count * keys,
            bytes_accessed=2 * pairs * PAIR * (4 * count + 4 * keys),
            transcendentals=2 * pairs * count * keys,
        ),
        name="attend_back",
    )(*operands)


highest = lax.Precision.HIGHEST


def matmul(left, right):
    return jnp.einsum("...i,ij->...j", left, right, preferred_element_type=jnp.float32)


def matmul_t(left, right):
    return jnp.einsum("...j,ij->...i", left, right, preferred_element_type=jnp.float32)


def outer_sum(left, right):
    return jnp.einsum("rfi,rfj->ij", left, right, preferred_element_type=jnp.float32)


def layer_stats(values):
    center = values - jnp.mean(values, axis=-1, keepdims=True)
    inv_std = lax.rsqrt(jnp.mean(center * center, axis=-1, keepdims=True) + 1e-05)
    return (center * inv_std, inv_std)


def norm_back(grad_normed, normed, inv_std):
    return inv_std * (
        grad_normed
        - jnp.mean(grad_normed, axis=-1, keepdims=True)
        - normed * jnp.mean(grad_normed * normed, axis=-1, keepdims=True)
    )


def silu_slope(values):
    sigmoid_part = jax.nn.sigmoid(values)
    return sigmoid_part * (1.0 + values * (1.0 - sigmoid_part))


def angle_tables(positions):
    half_dim = HEAD_DIM // 2
    inverse = jnp.exp(-math.log(10000.0) * jnp.arange(half_dim, dtype=jnp.float32) / half_dim)
    angles = positions[:, None] * inverse[None, :]
    return (jnp.cos(angles)[:, None, :], jnp.sin(angles)[:, None, :])


def rotate(values, cosine, sine_table):
    half_dim = values.shape[-1] // 2
    first_half = values[..., :half_dim]
    second_half = values[..., half_dim:]
    return jnp.concatenate(
        [
            first_half * cosine - second_half * sine_table,
            second_half * cosine + first_half * sine_table,
        ],
        axis=-1,
    )


def time_features(times):
    half_dim = TFREQ // 2
    freqs = jnp.exp(-math.log(10000.0) * jnp.arange(half_dim, dtype=jnp.float32) / half_dim)
    angles = times[:, None] * freqs[None, :]
    return jnp.concatenate([jnp.cos(angles), jnp.sin(angles)], axis=-1)


def stamp_rows(times, time_in, time_out, modul):
    features = time_features(times).astype(jnp.bfloat16)
    pre_hidden = jnp.dot(features, time_in, preferred_element_type=jnp.float32)
    time_hidden = jax.nn.silu(pre_hidden).astype(jnp.bfloat16)
    time_token = jnp.dot(time_hidden, time_out, preferred_element_type=jnp.float32)
    token_act = jax.nn.silu(time_token).astype(jnp.bfloat16)
    modulation = jnp.dot(token_act, modul, preferred_element_type=jnp.float32)
    return (features, pre_hidden, time_hidden, time_token, token_act, modulation)


def self_forward(row_inputs):
    query_row, key_row, value_row, local_row, whole_row = row_inputs
    allowed = local_row[:, None] == whole_row[None, :]
    scores = (
        jnp.einsum("qhd,khd->hqk", query_row, key_row, preferred_element_type=jnp.float32) * 0.125
    )
    scores = jnp.where(allowed[None], scores, -1e30)
    row_max = jnp.max(scores, axis=-1, keepdims=True)
    shifted = jnp.exp(scores - row_max)
    denominator = jnp.sum(shifted, axis=-1, keepdims=True)
    soft_weights = (shifted / denominator).astype(jnp.bfloat16)
    mixed = jnp.einsum("hqk,khd->qhd", soft_weights, value_row, preferred_element_type=jnp.float32)
    return (mixed.astype(jnp.bfloat16), row_max + jnp.log(denominator))


def self_backward(row_inputs):
    query_row, key_row, value_row, grad_row, log_row, local_row, whole_row = row_inputs
    allowed = local_row[:, None] == whole_row[None, :]
    scores = (
        jnp.einsum("qhd,khd->hqk", query_row, key_row, preferred_element_type=jnp.float32) * 0.125
    )
    soft_again = jnp.exp(jnp.where(allowed[None], scores, -1e30) - log_row)
    grad_soft = jnp.einsum("qhd,khd->hqk", grad_row, value_row, preferred_element_type=jnp.float32)
    grad_scores = (
        soft_again * (grad_soft - jnp.sum(soft_again * grad_soft, axis=-1, keepdims=True))
    ).astype(jnp.bfloat16)
    grad_query = (
        jnp.einsum("hqk,khd->qhd", grad_scores, key_row, preferred_element_type=jnp.float32) * 0.125
    )
    key_part = (
        jnp.einsum("hqk,qhd->khd", grad_scores, query_row, preferred_element_type=jnp.float32)
        * 0.125
    )
    value_part = jnp.einsum(
        "hqk,qhd->khd",
        soft_again.astype(jnp.bfloat16),
        grad_row,
        preferred_element_type=jnp.float32,
    )
    return (grad_query, key_part, value_part)


def on_device(
    frames,
    context,
    seg_lengths,
    bucket_ids,
    timesteps,
    bucket_weights,
    w_time_in,
    w_time_out,
    w_mod,
    w_qkv,
    w_attn_out,
    cross_gain,
    w_cross_q,
    w_cross_kv,
    w_cross_out,
    w_glu,
    w_down,
    cotangent,
):
    fwd_weights = (
        lax.all_gather(w_time_in, ("row", "seq"), axis=0, tiled=True),
        lax.all_gather(w_time_out, ("row", "seq"), axis=0, tiled=True),
        lax.all_gather(w_mod, ("row", "seq"), axis=0, tiled=True),
        lax.all_gather(w_qkv, ("row", "seq"), axis=0, tiled=True),
        lax.all_gather(w_attn_out, ("row", "seq"), axis=0, tiled=True),
        lax.all_gather(cross_gain, ("row", "seq"), axis=0, tiled=True),
        lax.all_gather(w_cross_q, ("row", "seq"), axis=0, tiled=True),
        lax.all_gather(w_cross_kv, ("row", "seq"), axis=0, tiled=True),
        lax.all_gather(w_cross_out, ("row", "seq"), axis=0, tiled=True),
        lax.all_gather(w_glu, ("row", "seq"), axis=0, tiled=True),
        lax.all_gather(w_down, ("row", "seq"), axis=0, tiled=True),
    )
    (
        time_in,
        time_out,
        modul,
        qkv_w,
        attn_w,
        gain_w,
        crossq_w,
        crosskv_w,
        crossout_w,
        glu_w,
        down_w,
    ) = fwd_weights
    rows_here = frames.shape[0]
    frames_here = frames.shape[1]
    text_len = context.shape[1]
    row_start = lax.axis_index("row") * rows_here
    seq_start = lax.axis_index("seq") * frames_here
    my_buckets = lax.dynamic_slice_in_dim(bucket_ids, row_start, rows_here)
    onehot = (my_buckets[:, None] == jnp.arange(BUCKETS, dtype=jnp.int32)[None, :]).astype(
        jnp.float32
    )
    my_times = jnp.dot(onehot, timesteps.astype(jnp.float32), precision=highest)
    features, pre_hidden, time_hidden, time_token, token_act, modulation = stamp_rows(
        my_times, time_in, time_out, modul
    )
    shift_attn = modulation[:, None, 0:D]
    scale_attn = modulation[:, None, D : 2 * D]
    gate_attn = modulation[:, None, 2 * D : 3 * D]
    shift_ffn = modulation[:, None, 3 * D : 4 * D]
    scale_ffn = modulation[:, None, 4 * D : 5 * D]
    gate_ffn = modulation[:, None, 5 * D : 6 * D]
    bounds = jnp.cumsum(seg_lengths, axis=-1)
    all_positions = jnp.arange(LENGTH, dtype=jnp.int32)
    all_ids = jnp.sum(
        (all_positions[None, :, None] >= bounds[:, None, :]).astype(jnp.int32), axis=-1
    )
    local_ids = lax.dynamic_slice_in_dim(all_ids, seq_start, frames_here, 1)
    cosine, sine_table = angle_tables(
        (seq_start + jnp.arange(frames_here, dtype=jnp.int32)).astype(jnp.float32)
    )
    inputs = frames.astype(jnp.float32)
    normed_a, inv_a = layer_stats(inputs)
    attn_in = (normed_a * (1.0 + scale_attn) + shift_attn).astype(jnp.bfloat16)
    projected = matmul(attn_in, qkv_w)
    query_pre = projected[..., :D].reshape(rows_here, frames_here, HEADS, HEAD_DIM)
    key_pre = projected[..., D : 2 * D].reshape(rows_here, frames_here, HEADS, HEAD_DIM)
    value_pre = projected[..., 2 * D :].reshape(rows_here, frames_here, HEADS, HEAD_DIM)
    queries = rotate(query_pre, cosine, sine_table).astype(jnp.bfloat16)
    key_local = rotate(key_pre, cosine, sine_table).astype(jnp.bfloat16)
    value_local = value_pre.astype(jnp.bfloat16)
    key_rows, value_rows = (
        lax.all_gather(key_local, "seq", axis=1, tiled=True),
        lax.all_gather(value_local, "seq", axis=1, tiled=True),
    )
    mixed_rows, log_total = lax.map(
        self_forward, (queries, key_rows, value_rows, local_ids, all_ids)
    )
    attn_mixed = mixed_rows.reshape(rows_here, frames_here, D)
    attn_out = matmul(attn_mixed, attn_w)
    after_attn = inputs + gate_attn * attn_out
    normed_c, inv_c = layer_stats(after_attn)
    gain_values = gain_w.astype(jnp.float32)
    cross_in = (normed_c * gain_values).astype(jnp.bfloat16)
    cross_q = (
        matmul(cross_in, crossq_w)
        .astype(jnp.bfloat16)
        .reshape(rows_here, frames_here, HEADS, HEAD_DIM)
    )
    cross_kv = jnp.einsum(
        "rcm,me->rce", context, crosskv_w, preferred_element_type=jnp.float32
    ).astype(jnp.bfloat16)
    cross_k = cross_kv[..., :D].reshape(rows_here, text_len, HEADS, HEAD_DIM)
    cross_v = cross_kv[..., D:].reshape(rows_here, text_len, HEADS, HEAD_DIM)
    cross_scores = (
        jnp.einsum("rqhd,rchd->rhqc", cross_q, cross_k, preferred_element_type=jnp.float32) * 0.125
    )
    cross_shift = jnp.exp(cross_scores - jnp.max(cross_scores, axis=-1, keepdims=True))
    cross_soft = cross_shift / jnp.sum(cross_shift, axis=-1, keepdims=True)
    cross_soft_low = cross_soft.astype(jnp.bfloat16)
    cross_mixed = (
        jnp.einsum("rhqc,rchd->rqhd", cross_soft_low, cross_v, preferred_element_type=jnp.float32)
        .reshape(rows_here, frames_here, D)
        .astype(jnp.bfloat16)
    )
    cross_out = matmul(cross_mixed, crossout_w)
    after_cross = after_attn + cross_out
    normed_f, inv_f = layer_stats(after_cross)
    ffn_in = (normed_f * (1.0 + scale_ffn) + shift_ffn).astype(jnp.bfloat16)
    gate_up = matmul(ffn_in, glu_w)
    gate_pre = gate_up[..., :FF]
    up_pre = gate_up[..., FF:]
    gate_act = jax.nn.silu(gate_pre)
    hidden = (gate_act * up_pre).astype(jnp.bfloat16)
    ffn_out = matmul(hidden, down_w)
    result = (after_cross + gate_ffn * ffn_out).astype(jnp.bfloat16)
    bwd_weights = (
        lax.all_gather(w_time_in, ("row", "seq"), axis=0, tiled=True),
        lax.all_gather(w_time_out, ("row", "seq"), axis=0, tiled=True),
        lax.all_gather(w_mod, ("row", "seq"), axis=0, tiled=True),
        lax.all_gather(w_qkv, ("row", "seq"), axis=0, tiled=True),
        lax.all_gather(w_attn_out, ("row", "seq"), axis=0, tiled=True),
        lax.all_gather(cross_gain, ("row", "seq"), axis=0, tiled=True),
        lax.all_gather(w_cross_q, ("row", "seq"), axis=0, tiled=True),
        lax.all_gather(w_cross_kv, ("row", "seq"), axis=0, tiled=True),
        lax.all_gather(w_cross_out, ("row", "seq"), axis=0, tiled=True),
        lax.all_gather(w_glu, ("row", "seq"), axis=0, tiled=True),
        lax.all_gather(w_down, ("row", "seq"), axis=0, tiled=True),
    )
    (
        time_in,
        time_out,
        modul,
        qkv_w,
        attn_w,
        gain_w,
        crossq_w,
        crosskv_w,
        crossout_w,
        glu_w,
        down_w,
    ) = bwd_weights
    row_scale = jnp.dot(onehot, bucket_weights, precision=highest)
    grad_out = cotangent.astype(jnp.float32) * row_scale[:, None, None]
    grad_ffn_low = (gate_ffn * grad_out).astype(jnp.bfloat16)
    dgate_ffn = jnp.sum(grad_out * ffn_out, axis=1)
    grad_down = outer_sum(hidden, grad_ffn_low)
    grad_hidden = matmul_t(grad_ffn_low, down_w)
    grad_gate_up = jnp.concatenate(
        [grad_hidden * up_pre * silu_slope(gate_pre), grad_hidden * gate_act], axis=-1
    ).astype(jnp.bfloat16)
    grad_glu = outer_sum(ffn_in, grad_gate_up)
    grad_ffn_in = matmul_t(grad_gate_up, glu_w)
    dshift_ffn = jnp.sum(grad_ffn_in, axis=1)
    dscale_ffn = jnp.sum(grad_ffn_in * normed_f, axis=1)
    grad_cross = grad_out + norm_back(grad_ffn_in * (1.0 + scale_ffn), normed_f, inv_f)
    ffn_grads = (
        lax.psum_scatter(grad_glu, ("row", "seq"), scatter_dimension=0, tiled=True),
        lax.psum_scatter(grad_down, ("row", "seq"), scatter_dimension=0, tiled=True),
    )
    grad_cross_low = grad_cross.astype(jnp.bfloat16)
    grad_crossout = outer_sum(cross_mixed, grad_cross_low)
    grad_cmixed = (
        matmul_t(grad_cross_low, crossout_w)
        .astype(jnp.bfloat16)
        .reshape(rows_here, frames_here, HEADS, HEAD_DIM)
    )
    grad_csoft = jnp.einsum(
        "rqhd,rchd->rhqc", grad_cmixed, cross_v, preferred_element_type=jnp.float32
    )
    grad_cvalue = jnp.einsum(
        "rhqc,rqhd->rchd", cross_soft_low, grad_cmixed, preferred_element_type=jnp.float32
    )
    grad_cscores = (
        cross_soft * (grad_csoft - jnp.sum(cross_soft * grad_csoft, axis=-1, keepdims=True))
    ).astype(jnp.bfloat16)
    grad_cquery = (
        (
            jnp.einsum("rhqc,rchd->rqhd", grad_cscores, cross_k, preferred_element_type=jnp.float32)
            * 0.125
        )
        .reshape(rows_here, frames_here, D)
        .astype(jnp.bfloat16)
    )
    grad_ckey = (
        jnp.einsum("rhqc,rqhd->rchd", grad_cscores, cross_q, preferred_element_type=jnp.float32)
        * 0.125
    )
    grad_ckv = jnp.concatenate(
        [grad_ckey.reshape(rows_here, text_len, D), grad_cvalue.reshape(rows_here, text_len, D)],
        axis=-1,
    )
    grad_crosskv = jnp.einsum(
        "rcm,rce->me", context.astype(jnp.float32), grad_ckv, precision=highest
    )
    grad_crossq = outer_sum(cross_in, grad_cquery)
    grad_cross_in = matmul_t(grad_cquery, crossq_w)
    grad_gain = jnp.sum(grad_cross_in * normed_c, axis=(0, 1))
    grad_attn = grad_cross + norm_back(grad_cross_in * gain_values, normed_c, inv_c)
    grad_attn_low = (gate_attn * grad_attn).astype(jnp.bfloat16)
    dgate_attn = jnp.sum(grad_attn * attn_out, axis=1)
    grad_attnout = outer_sum(attn_mixed, grad_attn_low)
    grad_amixed = (
        matmul_t(grad_attn_low, attn_w)
        .astype(jnp.bfloat16)
        .reshape(rows_here, frames_here, HEADS, HEAD_DIM)
    )
    grad_query, key_part, value_part = lax.map(
        self_backward, (queries, key_rows, value_rows, grad_amixed, log_total, local_ids, all_ids)
    )
    grad_key, grad_value = (
        lax.psum_scatter(
            key_part.astype(jnp.bfloat16), "seq", scatter_dimension=1, tiled=True
        ).astype(jnp.float32),
        lax.psum_scatter(
            value_part.astype(jnp.bfloat16), "seq", scatter_dimension=1, tiled=True
        ).astype(jnp.float32),
    )
    grad_projected = jnp.concatenate(
        [
            rotate(grad_query, cosine, -sine_table).reshape(rows_here, frames_here, D),
            rotate(grad_key, cosine, -sine_table).reshape(rows_here, frames_here, D),
            grad_value.reshape(rows_here, frames_here, D),
        ],
        axis=-1,
    ).astype(jnp.bfloat16)
    grad_qkv = outer_sum(attn_in, grad_projected)
    grad_attn_in = matmul_t(grad_projected, qkv_w)
    dshift_attn = jnp.sum(grad_attn_in, axis=1)
    dscale_attn = jnp.sum(grad_attn_in * normed_a, axis=1)
    grad_frames = grad_attn + norm_back(grad_attn_in * (1.0 + scale_attn), normed_a, inv_a)
    grad_rows = jnp.concatenate(
        [dshift_attn, dscale_attn, dgate_attn, dshift_ffn, dscale_ffn, dgate_ffn], axis=-1
    )
    grad_modul = jnp.dot(token_act.astype(jnp.float32).T, grad_rows, precision=highest)
    grad_token = jnp.dot(grad_rows, modul.astype(jnp.float32).T, precision=highest) * silu_slope(
        time_token
    )
    grad_timeout = jnp.dot(time_hidden.astype(jnp.float32).T, grad_token, precision=highest)
    grad_pre = jnp.dot(grad_token, time_out.astype(jnp.float32).T, precision=highest) * silu_slope(
        pre_hidden
    )
    grad_timein = jnp.dot(features.astype(jnp.float32).T, grad_pre, precision=highest)
    rest_grads = (
        lax.psum_scatter(grad_timein, ("row", "seq"), scatter_dimension=0, tiled=True),
        lax.psum_scatter(grad_timeout, ("row", "seq"), scatter_dimension=0, tiled=True),
        lax.psum_scatter(grad_modul, ("row", "seq"), scatter_dimension=0, tiled=True),
        lax.psum_scatter(grad_qkv, ("row", "seq"), scatter_dimension=0, tiled=True),
        lax.psum_scatter(grad_attnout, ("row", "seq"), scatter_dimension=0, tiled=True),
        lax.psum_scatter(grad_gain, ("row", "seq"), scatter_dimension=0, tiled=True),
        lax.psum_scatter(grad_crossq, ("row", "seq"), scatter_dimension=0, tiled=True),
        lax.psum_scatter(grad_crosskv, ("row", "seq"), scatter_dimension=0, tiled=True),
        lax.psum_scatter(grad_crossout, ("row", "seq"), scatter_dimension=0, tiled=True),
    )
    shard_timein, shard_timeout, shard_modul = (rest_grads[0], rest_grads[1], rest_grads[2])
    block_grads = rest_grads[3:]
    return (
        result,
        grad_frames,
        shard_timein,
        shard_timeout,
        shard_modul,
        block_grads[0],
        block_grads[1],
        block_grads[2],
        block_grads[3],
        block_grads[4],
        block_grads[5],
        ffn_grads[0],
        ffn_grads[1],
    )


def can_split(rows, seqs):
    power = lambda n: n & (n - 1) == 0
    return (
        power(rows)
        and power(seqs)
        and HEADS % (2 * seqs) == 0
        and D % (rows * seqs) == 0
        and FF % (rows * seqs) == 0
        and LENGTH % (seqs * 512) == 0
    )


def on_device_split(
    rows,
    seqs,
    frames,
    context,
    seg_lengths,
    bucket_ids,
    timesteps,
    bucket_weights,
    w_time_in,
    w_time_out,
    w_mod,
    w_qkv,
    w_attn_out,
    cross_gain,
    w_cross_q,
    w_cross_kv,
    w_cross_out,
    w_glu,
    w_down,
    cotangent,
):
    my_row = lax.axis_index("row")
    my_seq = lax.axis_index("seq")
    flat = my_row * seqs + my_seq
    sizes = {"row": rows, "seq": seqs}

    def swap(value, axis, j):
        return lax.ppermute(value, axis, [(i, i ^ j) for i in range(sizes[axis])])

    def sum_over(value, axis):
        j = 1
        while j < sizes[axis]:
            value = value + swap(value, axis, j)
            j *= 2
        return value

    def sum_all(value):
        return sum_over(sum_over(value, "seq"), "row")

    def pick(stack, axis_name, j, dim=0):
        me = my_row if axis_name == "row" else my_seq
        return lax.dynamic_index_in_dim(stack, me ^ j, dim, keepdims=False)

    def natural(slots, axis_name="seq"):
        stack = jnp.stack(slots)
        return jnp.stack([pick(stack, axis_name, t) for t in range(len(slots))])

    def exchange(stack, dim=0, axis_name="seq"):
        pieces = [pick(stack, axis_name, j, dim) for j in range(sizes[axis_name])]
        return [pieces[0]] + [swap(p, axis_name, j) for j, p in enumerate(pieces) if j]

    def spread(value, axis_name="seq"):
        return [value] + [swap(value, axis_name, j) for j in range(1, sizes[axis_name])]

    def mine(values, width):
        return lax.dynamic_slice_in_dim(values, flat * width, width, values.ndim - 1)

    def dot(left, right):
        return jnp.dot(left, right, preferred_element_type=jnp.float32)

    def dot_right_t(left, right):
        return jnp.einsum("fj,ij->fi", left, right, preferred_element_type=jnp.float32)

    def dot_left_t(left, right):
        return jnp.einsum("fi,fj->ij", left, right, preferred_element_type=jnp.float32)

    low = jnp.bfloat16
    frames_here = frames.shape[1]
    text_len, ctx_dim = context.shape[1:]
    local_heads = D // seqs
    depth = w_qkv.shape[0]
    part = FF // (rows * seqs)
    x_own = frames[0]

    x_all = jnp.concatenate(spread(x_own))
    kv_split = w_cross_kv.reshape(w_cross_kv.shape[0], seqs, -1)
    qkv_split = w_qkv.reshape(depth, 3, seqs, local_heads)
    first_pieces = [
        jnp.concatenate(
            [
                pick(qkv_split, "seq", j, 2).reshape(depth, 3 * local_heads),
                pick(kv_split, "seq", j, 1).reshape(depth, -1),
            ],
            axis=1,
        )
        for j in range(seqs)
    ]
    first_slots = [first_pieces[0]] + [swap(p, "seq", j) for j, p in enumerate(first_pieces) if j]
    first_w = natural(first_slots).reshape(seqs * depth, -1)
    first_w = lax.all_gather(first_w, "row", axis=0, tiled=True)
    qkv_w = first_w[:, : 3 * local_heads]
    kv_w = first_w[:, 3 * local_heads :].reshape(ctx_dim, -1)
    wide_w = lax.all_gather(
        jnp.concatenate([w_attn_out, w_cross_q, w_cross_out], axis=1), ("row", "seq"), axis=0, tiled=True
    )
    attn_w, crossq_w, crossout_w = wide_w[:, :D], wide_w[:, D : 2 * D], wide_w[:, 2 * D :]
    glu_slots = exchange(w_glu.reshape(depth, 2, rows, seqs, part), 3)
    glu_w = natural([s.reshape(depth, -1) for s in glu_slots]).reshape(seqs * depth, -1)
    glu_w = lax.all_gather(glu_w, "row", axis=0, tiled=True)
    down_w = lax.all_gather(w_down, "row", axis=0, tiled=True)

    features = time_features(timesteps.astype(jnp.float32)).astype(low)
    pre_part = dot(mine(features, w_time_in.shape[0]), w_time_in)
    gain_part = lax.dynamic_update_slice(
        jnp.zeros((1, D), jnp.float32), cross_gain.astype(jnp.float32)[None], (0, flat * depth)
    )
    pre_hidden = sum_all(jnp.concatenate([pre_part, gain_part]))
    gain_values = pre_hidden[BUCKETS:]
    pre_hidden = pre_hidden[:BUCKETS]
    time_hidden = jax.nn.silu(pre_hidden).astype(low)
    time_token = sum_all(dot(mine(time_hidden, depth), w_time_out))
    token_act = jax.nn.silu(time_token).astype(low)
    mod_part = dot(mine(token_act, depth), w_mod)
    row_part = lambda j: lax.dynamic_index_in_dim(mod_part, bucket_ids[my_row ^ j], 0)
    modulation = row_part(0)
    for j in range(1, rows):
        modulation = modulation + swap(row_part(j), "row", j)
    modulation = sum_over(modulation, "seq")
    shift_attn, scale_attn, gate_attn, shift_ffn, scale_ffn, gate_ffn = jnp.split(modulation, 6, axis=1)

    bounds = jnp.cumsum(seg_lengths[0])
    slot_seq = my_seq ^ jnp.arange(seqs, dtype=jnp.int32)
    positions = (slot_seq[:, None] * frames_here + jnp.arange(frames_here, dtype=jnp.int32)).reshape(-1)
    ids = jnp.sum((positions[:, None] >= bounds[None, :]).astype(jnp.int32), axis=-1)
    lane = jnp.arange(PAIR, dtype=jnp.int32)[None, :]
    same = ids[:, None] == lane
    key_mask = same.astype(low)
    query_mask = jnp.where((lane < seg_lengths.shape[1]) & ~same, -1e30, 0.0).astype(low)
    half_dim = HEAD_DIM // 2
    inverse = jnp.exp(-math.log(10000.0) * jnp.arange(half_dim, dtype=jnp.float32) / half_dim)
    angles = positions.astype(jnp.float32)[:, None] * inverse[None, :]
    cosine = jnp.tile(jnp.cos(angles), (1, PAIR // half_dim))
    sine = jnp.tile(jnp.concatenate([-jnp.sin(angles), jnp.sin(angles)], axis=1), (1, 2))
    masks, tables = (query_mask, key_mask), (cosine, sine)

    pairs = local_heads // PAIR
    attn_in, qkv = project(x_all, 1.0 + scale_attn, shift_attn, qkv_w, cosine, sine)
    mixed_heads, lse = attend(qkv, qkv, qkv, 0, pairs, 2 * pairs, pairs, 512, masks)
    slots = lambda values: values.reshape(seqs, frames_here, -1)
    mixed_slots = slots(mixed_heads)
    mixed_got = [mixed_slots[0]] + [swap(mixed_slots[j], "seq", j) for j in range(1, seqs)]
    attn_mixed = natural(mixed_got).transpose(1, 0, 2).reshape(frames_here, D)
    attn_out = dot(attn_mixed, attn_w)
    inputs = x_own.astype(jnp.float32)
    after_attn = inputs + gate_attn * attn_out

    normed_c, inv_c = layer_stats(after_attn)
    cross_in = (normed_c * gain_values).astype(low)
    cross_q = dot(cross_in, crossq_w).astype(low)
    kv_mine = dot(context[0], kv_w).astype(low)
    cross_kv = natural(spread(kv_mine)).transpose(1, 0, 2).reshape(text_len, 2 * D)
    all_pairs = D // PAIR
    cross_mixed, cross_lse = attend(cross_q, cross_kv, cross_kv, 0, 0, all_pairs, all_pairs, frames_here)
    after_cross = after_attn + dot(cross_mixed, crossout_w)

    normed_f, inv_f = layer_stats(after_cross)
    ffn_in = (normed_f * (1.0 + scale_ffn) + shift_ffn).astype(low)
    ffn_all = jnp.concatenate(spread(ffn_in))
    units = FF // seqs
    gate_up = dot(ffn_all, glu_w)
    gate_pre, up_pre = gate_up[:, :units], gate_up[:, units:]
    gate_act = jax.nn.silu(gate_pre)
    hidden = (gate_act * up_pre).astype(low)

    def return_slots(values):
        stack = slots(values.astype(low))
        total = stack[0].astype(jnp.float32)
        for j in range(1, seqs):
            total = total + swap(stack[j], "seq", j).astype(jnp.float32)
        return total

    ffn_out = return_slots(dot(hidden, down_w))
    result = (after_cross + gate_ffn * ffn_out).astype(low)

    row_scale = lax.dynamic_index_in_dim(bucket_weights, bucket_ids[my_row], 0)
    grad_out = cotangent[0].astype(jnp.float32) * row_scale
    grad_ffn_all = jnp.concatenate(spread((gate_ffn * grad_out).astype(low)))
    dgate_ffn = jnp.sum(grad_out * ffn_out, axis=0)
    grad_hidden = dot_right_t(grad_ffn_all, down_w)
    grad_gate_up = jnp.concatenate(
        [grad_hidden * up_pre * silu_slope(gate_pre), grad_hidden * gate_act], axis=-1
    ).astype(low)
    grad_ffn_in = return_slots(dot_right_t(grad_gate_up, glu_w))
    grad_glu = lax.psum_scatter(
        dot_left_t(ffn_all, grad_gate_up).astype(low), "row", scatter_dimension=0, tiled=True
    )
    grad_down = lax.psum_scatter(
        dot_left_t(hidden, grad_ffn_all).astype(low), "row", scatter_dimension=0, tiled=True
    )
    dshift_ffn = jnp.sum(grad_ffn_in, axis=0)
    dscale_ffn = jnp.sum(grad_ffn_in * normed_f, axis=0)
    grad_cross = grad_out + norm_back(grad_ffn_in * (1.0 + scale_ffn), normed_f, inv_f)

    grad_cross_low = grad_cross.astype(low)
    grad_crossout = dot_left_t(cross_mixed, grad_cross_low)
    grad_cmixed = dot_right_t(grad_cross_low, crossout_w).astype(low)
    grad_cquery, grad_ckey, grad_cvalue = attend_back(
        cross_q, cross_kv, cross_kv, grad_cmixed, cross_mixed, cross_lse,
        0, 0, all_pairs, all_pairs, frames_here, text_len,
    )
    grad_ckv = jnp.concatenate([grad_ckey, grad_cvalue], axis=1).reshape(text_len, seqs, -1)
    grad_ckv = sum(exchange(grad_ckv, 1))
    grad_kv = jnp.einsum(
        "cm,ce->me", context[0].astype(jnp.float32), grad_ckv, precision=highest
    ).astype(low)
    kv_got = exchange(grad_kv.reshape(rows, ctx_dim // rows, -1), 0, "row")
    grad_kv = sum(g.astype(jnp.float32) for g in kv_got)
    grad_kv = natural(exchange(grad_kv.reshape(seqs, ctx_dim // (rows * seqs), -1)))
    grad_crosskv = grad_kv.transpose(1, 0, 2).reshape(ctx_dim // (rows * seqs), 2 * D)
    grad_crossq = dot_left_t(cross_in, grad_cquery)
    grad_cross_in = dot_right_t(grad_cquery, crossq_w)
    grad_gain = jnp.sum(grad_cross_in * normed_c, axis=0)
    grad_attn = grad_cross + norm_back(grad_cross_in * gain_values, normed_c, inv_c)

    grad_attn_low = (gate_attn * grad_attn).astype(low)
    dgate_attn = jnp.sum(grad_attn * attn_out, axis=0)
    grad_attnout = dot_left_t(attn_mixed, grad_attn_low)
    grad_wide = jnp.concatenate([grad_attnout, grad_crossq, grad_crossout], axis=1).astype(low)
    grad_wide = lax.psum_scatter(grad_wide, ("row", "seq"), scatter_dimension=0, tiled=True)
    grad_amixed = dot_right_t(grad_attn_low, attn_w).astype(low)
    grad_heads = jnp.concatenate(exchange(grad_amixed.reshape(frames_here, seqs, local_heads), 1))
    grad_projected = jnp.concatenate(
        attend_back(
            qkv, qkv, qkv, grad_heads, mixed_heads, lse,
            0, pairs, 2 * pairs, pairs, 512, 512, masks, tables,
        ),
        axis=1,
    )
    grad_attn_in = return_slots(dot_right_t(grad_projected, qkv_w))
    grad_qkv = lax.psum_scatter(
        dot_left_t(attn_in, grad_projected).astype(low), "row", scatter_dimension=0, tiled=True
    )
    normed_a, inv_a = layer_stats(inputs)
    dshift_attn = jnp.sum(grad_attn_in, axis=0)
    dscale_attn = jnp.sum(grad_attn_in * normed_a, axis=0)
    grad_frames = grad_attn + norm_back(grad_attn_in * (1.0 + scale_attn), normed_a, inv_a)

    qkv_got = natural(exchange(grad_qkv.reshape(seqs, depth, -1)))
    grad_qkv = qkv_got.reshape(seqs, depth, 3, local_heads).transpose(1, 2, 0, 3).reshape(depth, 3 * D)
    glu_got = natural(exchange(grad_glu.reshape(seqs, depth, -1)))
    grad_glu = (
        glu_got.reshape(seqs, depth, 2, rows, part).transpose(1, 2, 3, 0, 4).reshape(depth, 2 * FF)
    )

    own_sums = sum_over(
        jnp.stack(
            [dshift_attn, dscale_attn, dgate_attn, dshift_ffn, dscale_ffn, dgate_ffn, grad_gain]
        ),
        "seq",
    )
    bucket_list = jnp.arange(BUCKETS, dtype=jnp.int32)
    grad_mods = jnp.zeros((BUCKETS, 6 * D), jnp.float32)
    gain_total = jnp.zeros((D,), jnp.float32)
    for j, sums in enumerate(spread(own_sums, "row")):
        hit = (bucket_list == bucket_ids[my_row ^ j]).astype(jnp.float32)
        grad_mods = grad_mods + hit[:, None] * sums[:6].reshape(1, 6 * D)
        gain_total = gain_total + sums[6]

    def outer(left, right):
        return sum(left[b][:, None] * right[b][None, :] for b in range(BUCKETS))

    def gather_all(own):
        across = natural(spread(own)).transpose(1, 0, 2).reshape(BUCKETS, -1)
        return natural(spread(across, "row"), "row").transpose(1, 0, 2).reshape(BUCKETS, -1)

    grad_modul = outer(mine(token_act, depth).astype(jnp.float32), grad_mods)
    token_own = jnp.dot(grad_mods, w_mod.astype(jnp.float32).T, precision=highest)
    grad_token = gather_all(token_own * silu_slope(mine(time_token, depth)))
    grad_timeout = outer(mine(time_hidden, depth).astype(jnp.float32), grad_token)
    hidden_own = jnp.dot(grad_token, w_time_out.astype(jnp.float32).T, precision=highest)
    grad_pre = gather_all(hidden_own * silu_slope(mine(pre_hidden, depth)))
    grad_timein = outer(mine(features, w_time_in.shape[0]).astype(jnp.float32), grad_pre)

    grad_wide = grad_wide.astype(jnp.float32)
    return (
        result[None],
        grad_frames[None],
        grad_timein,
        grad_timeout,
        grad_modul,
        grad_qkv.astype(jnp.float32),
        grad_wide[:, :D],
        mine(gain_total, depth),
        grad_wide[:, D : 2 * D],
        grad_crosskv,
        grad_wide[:, 2 * D :],
        grad_glu.astype(jnp.float32),
        grad_down.astype(jnp.float32),
    )


def solution(mesh):
    placed = (
        P("row", "seq", None),
        P("row", None, None),
        P("row", None),
        P(),
        P(),
        P(),
        P(("row", "seq"), None),
        P(("row", "seq"), None),
        P(("row", "seq"), None),
        P(("row", "seq"), None),
        P(("row", "seq"), None),
        P(("row", "seq")),
        P(("row", "seq"), None),
        P(("row", "seq"), None),
        P(("row", "seq"), None),
        P(("row", "seq"), None),
        P(("row", "seq"), None),
        P("row", "seq", None),
    )
    rows, seqs = mesh.shape["row"], mesh.shape["seq"]
    plan = functools.partial(on_device_split, rows, seqs) if can_split(rows, seqs) else on_device
    return jax.shard_map(
        plan,
        mesh=mesh,
        in_specs=placed,
        out_specs=(
            P("row", "seq", None),
            P("row", "seq", None),
            P(("row", "seq"), None),
            P(("row", "seq"), None),
            P(("row", "seq"), None),
            P(("row", "seq"), None),
            P(("row", "seq"), None),
            P(("row", "seq")),
            P(("row", "seq"), None),
            P(("row", "seq"), None),
            P(("row", "seq"), None),
            P(("row", "seq"), None),
            P(("row", "seq"), None),
        ),
        check_vma=False,
    )
```

```python
import functools
import math

import jax
import jax.numpy as jnp
from jax import lax
from jax.experimental import pallas as pl
from jax.experimental.pallas import tpu as pltpu
from jax.sharding import PartitionSpec as P

D = 1536
HEADS = 24
HEAD_DIM = 64
FF = 6144
TFREQ = 256
LENGTH = 2048
BUCKETS = 5
PAIR = 2 * HEAD_DIM
VMEM = 50 * 1024 * 1024
f32 = jnp.float32
bf16 = jnp.bfloat16


def dot_nt(left, right):
    return lax.dot_general(left, right, (((1,), (1,)), ((), ())), preferred_element_type=f32)


def dot_nn(left, right):
    return lax.dot_general(left, right, (((1,), (0,)), ((), ())), preferred_element_type=f32)


def swap_halves(values):
    lane = lax.broadcasted_iota(jnp.int32, values.shape, 1)
    ahead = pltpu.roll(values, PAIR - HEAD_DIM // 2, 1)
    behind = pltpu.roll(values, HEAD_DIM // 2, 1)
    return jnp.where((lane & (HEAD_DIM // 2)) == 0, ahead, behind)


def head_lanes(values, head):
    lane = lax.broadcasted_iota(jnp.int32, values.shape, 1)
    return jnp.where((lane // HEAD_DIM) == head, values, 0.0)


def norm_block(x_ref):
    values = x_ref[...].astype(f32)
    center = values - jnp.mean(values, axis=-1, keepdims=True)
    return center * lax.rsqrt(jnp.mean(center * center, axis=-1, keepdims=True) + 1e-05)


def project_kernel(per_slot, *refs):
    x_refs, (scale_ref, shift_ref, w_ref, cos_ref, sin_ref, in_ref, out_ref) = refs[:-7], refs[-7:]

    def run(x_ref):
        modulated = (norm_block(x_ref) * scale_ref[...] + shift_ref[...]).astype(bf16)
        in_ref[...] = modulated
        projected = dot_nn(modulated, w_ref[...])
        cosine = cos_ref[...]
        sine = sin_ref[...]
        width = out_ref.shape[1]
        for start in range(0, width, PAIR):
            part = projected[:, start : start + PAIR]
            if start < 2 * width // 3:
                part = part * cosine + swap_halves(part) * sine
            out_ref[:, start : start + PAIR] = part.astype(bf16)

    for slot, x_ref in enumerate(x_refs):
        pl.when(pl.program_id(0) // per_slot == slot)(functools.partial(run, x_ref))


def slot_specs(x_slots, block):
    per_slot, depth = x_slots[0].shape[0] // block, x_slots[0].shape[1]

    def one(slot):
        return pl.BlockSpec((block, depth), lambda i: (jnp.clip(i - slot * per_slot, 0, per_slot - 1), 0))

    return per_slot, [one(slot) for slot in range(len(x_slots))]


def project(x_slots, scale, shift, w, width, cosine, sine, block=256):
    per_slot, x_specs = slot_specs(x_slots, block)
    depth = x_slots[0].shape[1]
    count = len(x_slots) * x_slots[0].shape[0]
    row_spec = lambda cols: pl.BlockSpec((block, cols), lambda i: (i, 0))
    whole = lambda a: pl.BlockSpec(a.shape, lambda i: (0, 0))

    return pl.pallas_call(
        functools.partial(project_kernel, per_slot),
        grid=(count // block,),
        in_specs=x_specs
        + [
            whole(scale),
            whole(shift),
            pl.BlockSpec((depth, width), lambda i: (0, 0)),
            row_spec(PAIR),
            row_spec(PAIR),
        ],
        out_specs=[row_spec(depth), row_spec(width)],
        out_shape=[
            jax.ShapeDtypeStruct((count, depth), bf16),
            jax.ShapeDtypeStruct((count, width), bf16),
        ],
        compiler_params=pltpu.CompilerParams(vmem_limit_bytes=VMEM),
        cost_estimate=pl.CostEstimate(
            flops=2 * count * depth * width,
            bytes_accessed=2 * (2 * count * depth + depth * width + count * width),
            transcendentals=count,
        ),
        name="project",
    )(*x_slots, scale, shift, w, cosine, sine)


def project_back_kernel(per_slot, *refs):
    x_refs, (grad_ref, w_ref, out_ref, sums_ref) = refs[:-4], refs[-4:]

    @pl.when(pl.program_id(0) == 0)
    def _():
        sums_ref[...] = jnp.zeros_like(sums_ref)

    def run(x_ref):
        part = dot_nt(grad_ref[...], w_ref[...])
        out_ref[...] = part.astype(bf16)
        sums_ref[0:1, :] += jnp.sum(part, axis=0, keepdims=True)
        sums_ref[1:2, :] += jnp.sum(part * norm_block(x_ref), axis=0, keepdims=True)

    for slot, x_ref in enumerate(x_refs):
        pl.when(pl.program_id(0) // per_slot == slot)(functools.partial(run, x_ref))


def project_back(grad, w, x_slots, block=256):
    per_slot, x_specs = slot_specs(x_slots, block)
    count, width = grad.shape
    depth = x_slots[0].shape[1]
    return pl.pallas_call(
        functools.partial(project_back_kernel, per_slot),
        grid=(count // block,),
        in_specs=x_specs
        + [
            pl.BlockSpec((block, width), lambda i: (i, 0)),
            pl.BlockSpec((depth, width), lambda i: (0, 0)),
        ],
        out_specs=[
            pl.BlockSpec((block, depth), lambda i: (i, 0)),
            pl.BlockSpec((2, depth), lambda i: (0, 0)),
        ],
        out_shape=[
            jax.ShapeDtypeStruct((count, depth), bf16),
            jax.ShapeDtypeStruct((2, depth), f32),
        ],
        compiler_params=pltpu.CompilerParams(vmem_limit_bytes=VMEM),
        cost_estimate=pl.CostEstimate(
            flops=2 * count * depth * width,
            bytes_accessed=2 * (2 * count * depth + depth * width + count * width),
            transcendentals=count,
        ),
        name="project_back",
    )(*x_slots, grad, w)


def attend_kernel(masked, *refs):
    if masked:
        q_ref, k_ref, v_ref, qmask_ref, kmask_ref, o_ref, lse_ref, keys, values_t = refs
    else:
        q_ref, k_ref, v_ref, o_ref, lse_ref, keys, values_t = refs

    @pl.when(pl.program_id(1) == 0)
    def _():
        keys[:, :PAIR] = k_ref[...]
        if masked:
            keys[:, PAIR:] = kmask_ref[...]
        values_t[...] = v_ref[...].astype(f32).T.astype(bf16)

    queries = q_ref[...].astype(f32) * 0.125
    mixed = []
    for head in range(2):
        query = head_lanes(queries, head).astype(bf16)
        if masked:
            query = jnp.concatenate([query, qmask_ref[...]], axis=1)
        scores = dot_nt(keys[...], query)
        top = jnp.max(scores, axis=0, keepdims=True)
        shifted = jnp.exp(scores - top)
        total = jnp.sum(shifted, axis=0, keepdims=True)
        own = values_t[head * HEAD_DIM : (head + 1) * HEAD_DIM, :]
        mixed.append(dot_nn(own, shifted.astype(bf16)) / total)
        lse_ref[0, head : head + 1, :] = top + jnp.log(total)
    o_ref[...] = jnp.concatenate(mixed, axis=0).T.astype(bf16)


def attend(q, k, v, q_col, k_col, v_col, pairs, block, masks=None):
    count, keys = q.shape[0], k.shape[0]
    masked = masks is not None
    in_specs = [
        pl.BlockSpec((block, PAIR), lambda p, i: (i, q_col + p)),
        pl.BlockSpec((keys, PAIR), lambda p, i: (0, k_col + p)),
        pl.BlockSpec((keys, PAIR), lambda p, i: (0, v_col + p)),
    ]
    if masked:
        in_specs += [
            pl.BlockSpec((block, PAIR), lambda p, i: (i, 0)),
            pl.BlockSpec((keys, PAIR), lambda p, i: (0, 0)),
        ]
    return pl.pallas_call(
        functools.partial(attend_kernel, masked),
        grid=(pairs, count // block),
        in_specs=in_specs,
        out_specs=[
            pl.BlockSpec((block, PAIR), lambda p, i: (i, p)),
            pl.BlockSpec((1, 2, block), lambda p, i: (p, 0, i)),
        ],
        out_shape=[
            jax.ShapeDtypeStruct((count, pairs * PAIR), bf16),
            jax.ShapeDtypeStruct((pairs, 2, count), f32),
        ],
        scratch_shapes=[
            pltpu.VMEM((keys, (2 if masked else 1) * PAIR), bf16),
            pltpu.VMEM((PAIR, keys), bf16),
        ],
        compiler_params=pltpu.CompilerParams(vmem_limit_bytes=VMEM),
        cost_estimate=pl.CostEstimate(
            flops=16 * pairs * PAIR * count * keys,
            bytes_accessed=2 * pairs * PAIR * (2 * count + 2 * keys),
            transcendentals=2 * pairs * count * keys,
        ),
        name="attend",
    )(q, k, v, *(masks or ()))


def attend_back_kernel(masked, chunk, *refs):
    if masked:
        (q_ref, k_ref, v_ref, do_ref, o_ref, lse_ref, qmask_ref, kmask_ref, qcos_ref, qsin_ref,
         kcos_ref, ksin_ref, dq_ref, dk_ref, dv_ref, keys, keys_t, dk_sum, dv_sum) = refs
    else:
        (q_ref, k_ref, v_ref, do_ref, o_ref, lse_ref,
         dq_ref, dk_ref, dv_ref, keys, keys_t, dk_sum, dv_sum) = refs
    step = pl.program_id(1)
    count = k_ref.shape[0]

    @pl.when(step == 0)
    def _():
        keys[:, :PAIR] = k_ref[...]
        if masked:
            keys[:, PAIR:] = kmask_ref[...]
        keys_t[...] = k_ref[...].astype(f32).T.astype(bf16)
        dk_sum[...] = jnp.zeros_like(dk_sum)
        dv_sum[...] = jnp.zeros_like(dv_sum)

    queries = q_ref[...].astype(f32) * 0.125
    grads = do_ref[...].astype(f32)
    rows_t = (grads * o_ref[...].astype(f32)).T
    parts = []
    for head in range(2):
        lanes = slice(head * HEAD_DIM, (head + 1) * HEAD_DIM)
        delta = jnp.sum(rows_t[lanes, :], axis=0, keepdims=True)
        log_row = lse_ref[0, head : head + 1, :]
        query = head_lanes(queries, head).astype(bf16)
        grad = head_lanes(grads, head).astype(bf16)
        full = jnp.concatenate([query, qmask_ref[...]], axis=1) if masked else query
        total = None
        for start in range(0, count, chunk):
            here = slice(start, start + chunk)
            soft = jnp.exp(dot_nt(keys[here, :], full) - log_row)
            grad_soft = dot_nt(v_ref[here, :], grad)
            grad_scores = (soft * (grad_soft - delta)).astype(bf16)
            dv_sum[here, :] += dot_nn(soft.astype(bf16), grad)
            dk_sum[here, :] += dot_nn(grad_scores, query)
            part = dot_nn(keys_t[lanes, here], grad_scores)
            total = part if total is None else total + part
        parts.append(total)
    dq = jnp.concatenate(parts, axis=0).T * 0.125
    if masked:
        dq = dq * qcos_ref[...] - swap_halves(dq) * qsin_ref[...]
    dq_ref[...] = dq.astype(dq_ref.dtype)

    @pl.when(step == pl.num_programs(1) - 1)
    def _():
        dk = dk_sum[...]
        if masked:
            dk = dk * kcos_ref[...] - swap_halves(dk) * ksin_ref[...]
        dk_ref[...] = dk.astype(dk_ref.dtype)
        dv_ref[...] = dv_sum[...].astype(dv_ref.dtype)


def attend_back(q, k, v, do, o, lse, q_col, k_col, v_col, pairs, block, chunk, masks=None, tables=None):
    count, keys = q.shape[0], k.shape[0]
    masked = masks is not None
    out_type = bf16 if masked else f32
    rows = lambda col: pl.BlockSpec((block, PAIR), lambda p, i: (i, col + p))
    whole = lambda col: pl.BlockSpec((keys, PAIR), lambda p, i: (0, col + p))
    in_specs = [
        rows(q_col), whole(k_col), whole(v_col), rows(0), rows(0),
        pl.BlockSpec((1, 2, block), lambda p, i: (p, 0, i)),
    ]
    operands = [q, k, v, do, o, lse]
    if masked:
        rows_fixed = pl.BlockSpec((block, PAIR), lambda p, i: (i, 0))
        whole_fixed = pl.BlockSpec((keys, PAIR), lambda p, i: (0, 0))
        in_specs += [rows_fixed, whole_fixed, rows_fixed, rows_fixed, whole_fixed, whole_fixed]
        operands += [masks[0], masks[1], tables[0], tables[1], tables[0], tables[1]]
    return pl.pallas_call(
        functools.partial(attend_back_kernel, masked, chunk),
        grid=(pairs, count // block),
        in_specs=in_specs,
        out_specs=[rows(0), whole(0), whole(0)],
        out_shape=[
            jax.ShapeDtypeStruct((count, pairs * PAIR), bf16),
            jax.ShapeDtypeStruct((keys, pairs * PAIR), out_type),
            jax.ShapeDtypeStruct((keys, pairs * PAIR), out_type),
        ],
        scratch_shapes=[
            pltpu.VMEM((keys, (2 if masked else 1) * PAIR), bf16),
            pltpu.VMEM((PAIR, keys), bf16),
            pltpu.VMEM((keys, PAIR), f32),
            pltpu.VMEM((keys, PAIR), f32),
        ],
        compiler_params=pltpu.CompilerParams(vmem_limit_bytes=VMEM),
        cost_estimate=pl.CostEstimate(
            flops=40 * pairs * PAIR * count * keys,
            bytes_accessed=2 * pairs * PAIR * (4 * count + 4 * keys),
            transcendentals=2 * pairs * count * keys,
        ),
        name="attend_back",
    )(*operands)
def split_units_kernel(seqs, part, w_ref, out_ref):
    block = seqs * part
    for pair in range(w_ref.shape[1] // (2 * block)):
        groups = [
            w_ref[:, (2 * pair + k) * block : (2 * pair + k + 1) * block].astype(f32) for k in range(2)
        ]
        for t in range(seqs):
            both = [g[:, t * part : (t + 1) * part] for g in groups]
            out_ref[t, :, 2 * pair * part : 2 * (pair + 1) * part] = jnp.concatenate(both, axis=1).astype(bf16)


def split_units(w, seqs, part):
    depth, width = w.shape
    return pl.pallas_call(
        functools.partial(split_units_kernel, seqs, part),
        out_shape=jax.ShapeDtypeStruct((seqs, depth, width // seqs), bf16),
        compiler_params=pltpu.CompilerParams(vmem_limit_bytes=VMEM),
        cost_estimate=pl.CostEstimate(flops=0, bytes_accessed=4 * depth * width, transcendentals=0),
        name="split_units",
    )(w)


def join_units_kernel(seqs, part, in_ref, out_ref):
    block = seqs * part
    for pair in range(out_ref.shape[1] // (2 * block)):
        both = [in_ref[t, :, 2 * pair * part : 2 * (pair + 1) * part].astype(f32) for t in range(seqs)]
        for k in range(2):
            group = [b[:, k * part : (k + 1) * part] for b in both]
            out_ref[:, (2 * pair + k) * block : (2 * pair + k + 1) * block] = jnp.concatenate(group, axis=1)


def join_units(stack, part):
    seqs, depth, width = stack.shape
    return pl.pallas_call(
        functools.partial(join_units_kernel, seqs, part),
        out_shape=jax.ShapeDtypeStruct((depth, width * seqs), f32),
        compiler_params=pltpu.CompilerParams(vmem_limit_bytes=VMEM),
        cost_estimate=pl.CostEstimate(flops=0, bytes_accessed=6 * depth * width * seqs, transcendentals=0),
        name="join_units",
    )(stack)


highest = lax.Precision.HIGHEST


def matmul(left, right):
    return jnp.einsum("...i,ij->...j", left, right, preferred_element_type=jnp.float32)


def matmul_t(left, right):
    return jnp.einsum("...j,ij->...i", left, right, preferred_element_type=jnp.float32)


def outer_sum(left, right):
    return jnp.einsum("rfi,rfj->ij", left, right, preferred_element_type=jnp.float32)


def layer_stats(values):
    center = values - jnp.mean(values, axis=-1, keepdims=True)
    inv_std = lax.rsqrt(jnp.mean(center * center, axis=-1, keepdims=True) + 1e-05)
    return (center * inv_std, inv_std)


def norm_back(grad_normed, normed, inv_std):
    return inv_std * (
        grad_normed
        - jnp.mean(grad_normed, axis=-1, keepdims=True)
        - normed * jnp.mean(grad_normed * normed, axis=-1, keepdims=True)
    )


def silu_slope(values):
    sigmoid_part = jax.nn.sigmoid(values)
    return sigmoid_part * (1.0 + values * (1.0 - sigmoid_part))


def angle_tables(positions):
    half_dim = HEAD_DIM // 2
    inverse = jnp.exp(-math.log(10000.0) * jnp.arange(half_dim, dtype=jnp.float32) / half_dim)
    angles = positions[:, None] * inverse[None, :]
    return (jnp.cos(angles)[:, None, :], jnp.sin(angles)[:, None, :])


def rotate(values, cosine, sine_table):
    half_dim = values.shape[-1] // 2
    first_half = values[..., :half_dim]
    second_half = values[..., half_dim:]
    return jnp.concatenate(
        [
            first_half * cosine - second_half * sine_table,
            second_half * cosine + first_half * sine_table,
        ],
        axis=-1,
    )


def time_features(times):
    half_dim = TFREQ // 2
    freqs = jnp.exp(-math.log(10000.0) * jnp.arange(half_dim, dtype=jnp.float32) / half_dim)
    angles = times[:, None] * freqs[None, :]
    return jnp.concatenate([jnp.cos(angles), jnp.sin(angles)], axis=-1)


def stamp_rows(times, time_in, time_out, modul):
    features = time_features(times).astype(jnp.bfloat16)
    pre_hidden = jnp.dot(features, time_in, preferred_element_type=jnp.float32)
    time_hidden = jax.nn.silu(pre_hidden).astype(jnp.bfloat16)
    time_token = jnp.dot(time_hidden, time_out, preferred_element_type=jnp.float32)
    token_act = jax.nn.silu(time_token).astype(jnp.bfloat16)
    modulation = jnp.dot(token_act, modul, preferred_element_type=jnp.float32)
    return (features, pre_hidden, time_hidden, time_token, token_act, modulation)


def self_forward(row_inputs):
    query_row, key_row, value_row, local_row, whole_row = row_inputs
    allowed = local_row[:, None] == whole_row[None, :]
    scores = (
        jnp.einsum("qhd,khd->hqk", query_row, key_row, preferred_element_type=jnp.float32) * 0.125
    )
    scores = jnp.where(allowed[None], scores, -1e30)
    row_max = jnp.max(scores, axis=-1, keepdims=True)
    shifted = jnp.exp(scores - row_max)
    denominator = jnp.sum(shifted, axis=-1, keepdims=True)
    soft_weights = (shifted / denominator).astype(jnp.bfloat16)
    mixed = jnp.einsum("hqk,khd->qhd", soft_weights, value_row, preferred_element_type=jnp.float32)
    return (mixed.astype(jnp.bfloat16), row_max + jnp.log(denominator))


def self_backward(row_inputs):
    query_row, key_row, value_row, grad_row, log_row, local_row, whole_row = row_inputs
    allowed = local_row[:, None] == whole_row[None, :]
    scores = (
        jnp.einsum("qhd,khd->hqk", query_row, key_row, preferred_element_type=jnp.float32) * 0.125
    )
    soft_again = jnp.exp(jnp.where(allowed[None], scores, -1e30) - log_row)
    grad_soft = jnp.einsum("qhd,khd->hqk", grad_row, value_row, preferred_element_type=jnp.float32)
    grad_scores = (
        soft_again * (grad_soft - jnp.sum(soft_again * grad_soft, axis=-1, keepdims=True))
    ).astype(jnp.bfloat16)
    grad_query = (
        jnp.einsum("hqk,khd->qhd", grad_scores, key_row, preferred_element_type=jnp.float32) * 0.125
    )
    key_part = (
        jnp.einsum("hqk,qhd->khd", grad_scores, query_row, preferred_element_type=jnp.float32)
        * 0.125
    )
    value_part = jnp.einsum(
        "hqk,qhd->khd",
        soft_again.astype(jnp.bfloat16),
        grad_row,
        preferred_element_type=jnp.float32,
    )
    return (grad_query, key_part, value_part)


def on_device(
    frames,
    context,
    seg_lengths,
    bucket_ids,
    timesteps,
    bucket_weights,
    w_time_in,
    w_time_out,
    w_mod,
    w_qkv,
    w_attn_out,
    cross_gain,
    w_cross_q,
    w_cross_kv,
    w_cross_out,
    w_glu,
    w_down,
    cotangent,
):
    fwd_weights = (
        lax.all_gather(w_time_in, ("row", "seq"), axis=0, tiled=True),
        lax.all_gather(w_time_out, ("row", "seq"), axis=0, tiled=True),
        lax.all_gather(w_mod, ("row", "seq"), axis=0, tiled=True),
        lax.all_gather(w_qkv, ("row", "seq"), axis=0, tiled=True),
        lax.all_gather(w_attn_out, ("row", "seq"), axis=0, tiled=True),
        lax.all_gather(cross_gain, ("row", "seq"), axis=0, tiled=True),
        lax.all_gather(w_cross_q, ("row", "seq"), axis=0, tiled=True),
        lax.all_gather(w_cross_kv, ("row", "seq"), axis=0, tiled=True),
        lax.all_gather(w_cross_out, ("row", "seq"), axis=0, tiled=True),
        lax.all_gather(w_glu, ("row", "seq"), axis=0, tiled=True),
        lax.all_gather(w_down, ("row", "seq"), axis=0, tiled=True),
    )
    (
        time_in,
        time_out,
        modul,
        qkv_w,
        attn_w,
        gain_w,
        crossq_w,
        crosskv_w,
        crossout_w,
        glu_w,
        down_w,
    ) = fwd_weights
    rows_here = frames.shape[0]
    frames_here = frames.shape[1]
    text_len = context.shape[1]
    row_start = lax.axis_index("row") * rows_here
    seq_start = lax.axis_index("seq") * frames_here
    my_buckets = lax.dynamic_slice_in_dim(bucket_ids, row_start, rows_here)
    onehot = (my_buckets[:, None] == jnp.arange(BUCKETS, dtype=jnp.int32)[None, :]).astype(
        jnp.float32
    )
    my_times = jnp.dot(onehot, timesteps.astype(jnp.float32), precision=highest)
    features, pre_hidden, time_hidden, time_token, token_act, modulation = stamp_rows(
        my_times, time_in, time_out, modul
    )
    shift_attn = modulation[:, None, 0:D]
    scale_attn = modulation[:, None, D : 2 * D]
    gate_attn = modulation[:, None, 2 * D : 3 * D]
    shift_ffn = modulation[:, None, 3 * D : 4 * D]
    scale_ffn = modulation[:, None, 4 * D : 5 * D]
    gate_ffn = modulation[:, None, 5 * D : 6 * D]
    bounds = jnp.cumsum(seg_lengths, axis=-1)
    all_positions = jnp.arange(LENGTH, dtype=jnp.int32)
    all_ids = jnp.sum(
        (all_positions[None, :, None] >= bounds[:, None, :]).astype(jnp.int32), axis=-1
    )
    local_ids = lax.dynamic_slice_in_dim(all_ids, seq_start, frames_here, 1)
    cosine, sine_table = angle_tables(
        (seq_start + jnp.arange(frames_here, dtype=jnp.int32)).astype(jnp.float32)
    )
    inputs = frames.astype(jnp.float32)
    normed_a, inv_a = layer_stats(inputs)
    attn_in = (normed_a * (1.0 + scale_attn) + shift_attn).astype(jnp.bfloat16)
    projected = matmul(attn_in, qkv_w)
    query_pre = projected[..., :D].reshape(rows_here, frames_here, HEADS, HEAD_DIM)
    key_pre = projected[..., D : 2 * D].reshape(rows_here, frames_here, HEADS, HEAD_DIM)
    value_pre = projected[..., 2 * D :].reshape(rows_here, frames_here, HEADS, HEAD_DIM)
    queries = rotate(query_pre, cosine, sine_table).astype(jnp.bfloat16)
    key_local = rotate(key_pre, cosine, sine_table).astype(jnp.bfloat16)
    value_local = value_pre.astype(jnp.bfloat16)
    key_rows, value_rows = (
        lax.all_gather(key_local, "seq", axis=1, tiled=True),
        lax.all_gather(value_local, "seq", axis=1, tiled=True),
    )
    mixed_rows, log_total = lax.map(
        self_forward, (queries, key_rows, value_rows, local_ids, all_ids)
    )
    attn_mixed = mixed_rows.reshape(rows_here, frames_here, D)
    attn_out = matmul(attn_mixed, attn_w)
    after_attn = inputs + gate_attn * attn_out
    normed_c, inv_c = layer_stats(after_attn)
    gain_values = gain_w.astype(jnp.float32)
    cross_in = (normed_c * gain_values).astype(jnp.bfloat16)
    cross_q = (
        matmul(cross_in, crossq_w)
        .astype(jnp.bfloat16)
        .reshape(rows_here, frames_here, HEADS, HEAD_DIM)
    )
    cross_kv = jnp.einsum(
        "rcm,me->rce", context, crosskv_w, preferred_element_type=jnp.float32
    ).astype(jnp.bfloat16)
    cross_k = cross_kv[..., :D].reshape(rows_here, text_len, HEADS, HEAD_DIM)
    cross_v = cross_kv[..., D:].reshape(rows_here, text_len, HEADS, HEAD_DIM)
    cross_scores = (
        jnp.einsum("rqhd,rchd->rhqc", cross_q, cross_k, preferred_element_type=jnp.float32) * 0.125
    )
    cross_shift = jnp.exp(cross_scores - jnp.max(cross_scores, axis=-1, keepdims=True))
    cross_soft = cross_shift / jnp.sum(cross_shift, axis=-1, keepdims=True)
    cross_soft_low = cross_soft.astype(jnp.bfloat16)
    cross_mixed = (
        jnp.einsum("rhqc,rchd->rqhd", cross_soft_low, cross_v, preferred_element_type=jnp.float32)
        .reshape(rows_here, frames_here, D)
        .astype(jnp.bfloat16)
    )
    cross_out = matmul(cross_mixed, crossout_w)
    after_cross = after_attn + cross_out
    normed_f, inv_f = layer_stats(after_cross)
    ffn_in = (normed_f * (1.0 + scale_ffn) + shift_ffn).astype(jnp.bfloat16)
    gate_up = matmul(ffn_in, glu_w)
    gate_pre = gate_up[..., :FF]
    up_pre = gate_up[..., FF:]
    gate_act = jax.nn.silu(gate_pre)
    hidden = (gate_act * up_pre).astype(jnp.bfloat16)
    ffn_out = matmul(hidden, down_w)
    result = (after_cross + gate_ffn * ffn_out).astype(jnp.bfloat16)
    bwd_weights = (
        lax.all_gather(w_time_in, ("row", "seq"), axis=0, tiled=True),
        lax.all_gather(w_time_out, ("row", "seq"), axis=0, tiled=True),
        lax.all_gather(w_mod, ("row", "seq"), axis=0, tiled=True),
        lax.all_gather(w_qkv, ("row", "seq"), axis=0, tiled=True),
        lax.all_gather(w_attn_out, ("row", "seq"), axis=0, tiled=True),
        lax.all_gather(cross_gain, ("row", "seq"), axis=0, tiled=True),
        lax.all_gather(w_cross_q, ("row", "seq"), axis=0, tiled=True),
        lax.all_gather(w_cross_kv, ("row", "seq"), axis=0, tiled=True),
        lax.all_gather(w_cross_out, ("row", "seq"), axis=0, tiled=True),
        lax.all_gather(w_glu, ("row", "seq"), axis=0, tiled=True),
        lax.all_gather(w_down, ("row", "seq"), axis=0, tiled=True),
    )
    (
        time_in,
        time_out,
        modul,
        qkv_w,
        attn_w,
        gain_w,
        crossq_w,
        crosskv_w,
        crossout_w,
        glu_w,
        down_w,
    ) = bwd_weights
    row_scale = jnp.dot(onehot, bucket_weights, precision=highest)
    grad_out = cotangent.astype(jnp.float32) * row_scale[:, None, None]
    grad_ffn_low = (gate_ffn * grad_out).astype(jnp.bfloat16)
    dgate_ffn = jnp.sum(grad_out * ffn_out, axis=1)
    grad_down = outer_sum(hidden, grad_ffn_low)
    grad_hidden = matmul_t(grad_ffn_low, down_w)
    grad_gate_up = jnp.concatenate(
        [grad_hidden * up_pre * silu_slope(gate_pre), grad_hidden * gate_act], axis=-1
    ).astype(jnp.bfloat16)
    grad_glu = outer_sum(ffn_in, grad_gate_up)
    grad_ffn_in = matmul_t(grad_gate_up, glu_w)
    dshift_ffn = jnp.sum(grad_ffn_in, axis=1)
    dscale_ffn = jnp.sum(grad_ffn_in * normed_f, axis=1)
    grad_cross = grad_out + norm_back(grad_ffn_in * (1.0 + scale_ffn), normed_f, inv_f)
    ffn_grads = (
        lax.psum_scatter(grad_glu, ("row", "seq"), scatter_dimension=0, tiled=True),
        lax.psum_scatter(grad_down, ("row", "seq"), scatter_dimension=0, tiled=True),
    )
    grad_cross_low = grad_cross.astype(jnp.bfloat16)
    grad_crossout = outer_sum(cross_mixed, grad_cross_low)
    grad_cmixed = (
        matmul_t(grad_cross_low, crossout_w)
        .astype(jnp.bfloat16)
        .reshape(rows_here, frames_here, HEADS, HEAD_DIM)
    )
    grad_csoft = jnp.einsum(
        "rqhd,rchd->rhqc", grad_cmixed, cross_v, preferred_element_type=jnp.float32
    )
    grad_cvalue = jnp.einsum(
        "rhqc,rqhd->rchd", cross_soft_low, grad_cmixed, preferred_element_type=jnp.float32
    )
    grad_cscores = (
        cross_soft * (grad_csoft - jnp.sum(cross_soft * grad_csoft, axis=-1, keepdims=True))
    ).astype(jnp.bfloat16)
    grad_cquery = (
        (
            jnp.einsum("rhqc,rchd->rqhd", grad_cscores, cross_k, preferred_element_type=jnp.float32)
            * 0.125
        )
        .reshape(rows_here, frames_here, D)
        .astype(jnp.bfloat16)
    )
    grad_ckey = (
        jnp.einsum("rhqc,rqhd->rchd", grad_cscores, cross_q, preferred_element_type=jnp.float32)
        * 0.125
    )
    grad_ckv = jnp.concatenate(
        [grad_ckey.reshape(rows_here, text_len, D), grad_cvalue.reshape(rows_here, text_len, D)],
        axis=-1,
    )
    grad_crosskv = jnp.einsum(
        "rcm,rce->me", context.astype(jnp.float32), grad_ckv, precision=highest
    )
    grad_crossq = outer_sum(cross_in, grad_cquery)
    grad_cross_in = matmul_t(grad_cquery, crossq_w)
    grad_gain = jnp.sum(grad_cross_in * normed_c, axis=(0, 1))
    grad_attn = grad_cross + norm_back(grad_cross_in * gain_values, normed_c, inv_c)
    grad_attn_low = (gate_attn * grad_attn).astype(jnp.bfloat16)
    dgate_attn = jnp.sum(grad_attn * attn_out, axis=1)
    grad_attnout = outer_sum(attn_mixed, grad_attn_low)
    grad_amixed = (
        matmul_t(grad_attn_low, attn_w)
        .astype(jnp.bfloat16)
        .reshape(rows_here, frames_here, HEADS, HEAD_DIM)
    )
    grad_query, key_part, value_part = lax.map(
        self_backward, (queries, key_rows, value_rows, grad_amixed, log_total, local_ids, all_ids)
    )
    grad_key, grad_value = (
        lax.psum_scatter(
            key_part.astype(jnp.bfloat16), "seq", scatter_dimension=1, tiled=True
        ).astype(jnp.float32),
        lax.psum_scatter(
            value_part.astype(jnp.bfloat16), "seq", scatter_dimension=1, tiled=True
        ).astype(jnp.float32),
    )
    grad_projected = jnp.concatenate(
        [
            rotate(grad_query, cosine, -sine_table).reshape(rows_here, frames_here, D),
            rotate(grad_key, cosine, -sine_table).reshape(rows_here, frames_here, D),
            grad_value.reshape(rows_here, frames_here, D),
        ],
        axis=-1,
    ).astype(jnp.bfloat16)
    grad_qkv = outer_sum(attn_in, grad_projected)
    grad_attn_in = matmul_t(grad_projected, qkv_w)
    dshift_attn = jnp.sum(grad_attn_in, axis=1)
    dscale_attn = jnp.sum(grad_attn_in * normed_a, axis=1)
    grad_frames = grad_attn + norm_back(grad_attn_in * (1.0 + scale_attn), normed_a, inv_a)
    grad_rows = jnp.concatenate(
        [dshift_attn, dscale_attn, dgate_attn, dshift_ffn, dscale_ffn, dgate_ffn], axis=-1
    )
    grad_modul = jnp.dot(token_act.astype(jnp.float32).T, grad_rows, precision=highest)
    grad_token = jnp.dot(grad_rows, modul.astype(jnp.float32).T, precision=highest) * silu_slope(
        time_token
    )
    grad_timeout = jnp.dot(time_hidden.astype(jnp.float32).T, grad_token, precision=highest)
    grad_pre = jnp.dot(grad_token, time_out.astype(jnp.float32).T, precision=highest) * silu_slope(
        pre_hidden
    )
    grad_timein = jnp.dot(features.astype(jnp.float32).T, grad_pre, precision=highest)
    rest_grads = (
        lax.psum_scatter(grad_timein, ("row", "seq"), scatter_dimension=0, tiled=True),
        lax.psum_scatter(grad_timeout, ("row", "seq"), scatter_dimension=0, tiled=True),
        lax.psum_scatter(grad_modul, ("row", "seq"), scatter_dimension=0, tiled=True),
        lax.psum_scatter(grad_qkv, ("row", "seq"), scatter_dimension=0, tiled=True),
        lax.psum_scatter(grad_attnout, ("row", "seq"), scatter_dimension=0, tiled=True),
        lax.psum_scatter(grad_gain, ("row", "seq"), scatter_dimension=0, tiled=True),
        lax.psum_scatter(grad_crossq, ("row", "seq"), scatter_dimension=0, tiled=True),
        lax.psum_scatter(grad_crosskv, ("row", "seq"), scatter_dimension=0, tiled=True),
        lax.psum_scatter(grad_crossout, ("row", "seq"), scatter_dimension=0, tiled=True),
    )
    shard_timein, shard_timeout, shard_modul = (rest_grads[0], rest_grads[1], rest_grads[2])
    block_grads = rest_grads[3:]
    return (
        result,
        grad_frames,
        shard_timein,
        shard_timeout,
        shard_modul,
        block_grads[0],
        block_grads[1],
        block_grads[2],
        block_grads[3],
        block_grads[4],
        block_grads[5],
        ffn_grads[0],
        ffn_grads[1],
    )


def can_split(rows, seqs):
    power = lambda n: n & (n - 1) == 0
    return (
        power(rows)
        and power(seqs)
        and HEADS % (2 * seqs) == 0
        and D % (rows * seqs) == 0
        and FF % (rows * seqs) == 0
        and LENGTH % (seqs * 512) == 0
    )


def on_device_split(
    rows,
    seqs,
    frames,
    context,
    seg_lengths,
    bucket_ids,
    timesteps,
    bucket_weights,
    w_time_in,
    w_time_out,
    w_mod,
    w_qkv,
    w_attn_out,
    cross_gain,
    w_cross_q,
    w_cross_kv,
    w_cross_out,
    w_glu,
    w_down,
    cotangent,
):
    my_row = lax.axis_index("row")
    my_seq = lax.axis_index("seq")
    flat = my_row * seqs + my_seq
    sizes = {"row": rows, "seq": seqs}

    def swap(value, axis, j):
        return lax.ppermute(value, axis, [(i, i ^ j) for i in range(sizes[axis])])

    def sum_over(value, axis):
        j = 1
        while j < sizes[axis]:
            value = value + swap(value, axis, j)
            j *= 2
        return value

    def sum_all(value):
        return sum_over(sum_over(value, "seq"), "row")

    def pick(stack, axis_name, j, dim=0):
        me = my_row if axis_name == "row" else my_seq
        return lax.dynamic_index_in_dim(stack, me ^ j, dim, keepdims=False)

    def natural(slots, axis_name="seq"):
        stack = jnp.stack(slots)
        return jnp.stack([pick(stack, axis_name, t) for t in range(len(slots))])

    def exchange_lines(stack, dim):
        pieces = [
            lax.dynamic_index_in_dim(stack, (my_row // 2) ^ j, dim, keepdims=False)
            for j in range(rows // 2)
        ]
        return [pieces[0]] + [swap(p, "row", 2 * j) for j, p in enumerate(pieces) if j]

    def exchange(stack, dim=0, axis_name="seq"):
        pieces = [pick(stack, axis_name, j, dim) for j in range(sizes[axis_name])]
        return [pieces[0]] + [swap(p, axis_name, j) for j, p in enumerate(pieces) if j]

    def spread(value, axis_name="seq"):
        return [value] + [swap(value, axis_name, j) for j in range(1, sizes[axis_name])]

    def after(value, *others):
        return lax.optimization_barrier((value,) + others)[0]

    def spread_two(value):
        if seqs != 4:
            return spread(value), None
        near = [swap(value, "seq", 1), swap(value, "seq", 2)]
        return [value] + near, near

    def opposite(near):
        half = near[0].shape[0] // 2
        return jnp.concatenate([swap(near[1][:half], "seq", 1), swap(near[0][half:], "seq", 2)])

    def columns(values, axis_name, j, width, start=0):
        me = my_row if axis_name == "row" else my_seq
        return lax.dynamic_slice_in_dim(values, start + (me ^ j) * width, width, 1)

    def side_by_side(slots):
        stack = jnp.stack(slots)
        return jnp.concatenate([pick(stack, "seq", t) for t in range(seqs)], axis=1)

    def mine(values, width):
        return lax.dynamic_slice_in_dim(values, flat * width, width, values.ndim - 1)

    def dot(left, right):
        return jnp.dot(left, right, preferred_element_type=jnp.float32)

    def dot_right_t(left, right):
        return jnp.einsum("fj,ij->fi", left, right, preferred_element_type=jnp.float32)

    def dot_left_t(left, right):
        return jnp.einsum("fi,fj->ij", left, right, preferred_element_type=jnp.float32)

    low = jnp.bfloat16
    frames_here = frames.shape[1]
    text_len, ctx_dim = context.shape[1:]
    local_heads = D // seqs
    depth = w_qkv.shape[0]
    part = FF // (rows * seqs)
    x_own = frames[0]

    kv_width = 2 * D // seqs
    first_pieces = [
        jnp.concatenate(
            [columns(w_qkv, "seq", j, local_heads, k * D) for k in range(3)]
            + [
                jnp.concatenate(
                    [
                        columns(w_cross_kv, "seq", j, kv_width)[:, : kv_width // 2],
                        columns(w_cross_kv, "seq", j, kv_width)[:, kv_width // 2 :],
                    ]
                )
            ],
            axis=1,
        )
        for j in range(seqs)
    ]
    first_slots = [first_pieces[0]] + [swap(p, "seq", j) for j, p in enumerate(first_pieces) if j]
    first_w = natural(first_slots).reshape(seqs * depth, -1)
    first_w = lax.all_gather(first_w, "row", axis=0, tiled=True)
    kv_w = first_w[:, 3 * local_heads :].reshape(rows * seqs, 2, depth // 2, -1)
    kv_w = jnp.concatenate([kv_w[:, h].reshape(ctx_dim, -1) for h in range(2)], axis=1)

    features = time_features(timesteps.astype(jnp.float32)).astype(low)
    pre_part = dot(mine(features, w_time_in.shape[0]), w_time_in)
    gain_part = lax.dynamic_update_slice(
        jnp.zeros((1, D), jnp.float32), cross_gain.astype(jnp.float32)[None], (0, flat * depth)
    )
    pre_hidden = sum_over(after(jnp.concatenate([pre_part, gain_part]), *first_slots), "seq")
    x_slots, near = spread_two(after(x_own, pre_hidden))
    pre_hidden = sum_over(pre_hidden, "row")
    gain_values = pre_hidden[BUCKETS:]
    pre_hidden = pre_hidden[:BUCKETS]
    time_hidden = jax.nn.silu(pre_hidden).astype(low)
    time_token = sum_over(dot(mine(time_hidden, depth), w_time_out), "row")
    if near is not None:
        time_token, *near = lax.optimization_barrier((time_token, *near))
        x_slots = [x_own, *near, opposite(near)]
    time_token = sum_over(time_token, "seq")
    token_act = jax.nn.silu(time_token).astype(low)
    mod_part = dot(mine(token_act, depth), w_mod)
    mod_part, *x_slots = lax.optimization_barrier((mod_part, *x_slots))
    row_part = lambda j: lax.dynamic_index_in_dim(mod_part, bucket_ids[my_row ^ j], 0)
    modulation = row_part(0)
    for j in range(1, rows):
        modulation = modulation + swap(row_part(j), "row", j)
    modulation = sum_over(modulation, "seq")
    wide_w = lax.all_gather(
        after(jnp.concatenate([w_attn_out, w_cross_q, w_cross_out], axis=1), time_token), ("row", "seq"), axis=0, tiled=True
    )
    attn_w, crossq_w, crossout_w = wide_w[:, :D], wide_w[:, D : 2 * D], wide_w[:, 2 * D :]

    shift_attn, scale_attn, gate_attn, shift_ffn, scale_ffn, gate_ffn = jnp.split(modulation, 6, axis=1)

    bounds = jnp.cumsum(seg_lengths[0])
    slot_seq = my_seq ^ jnp.arange(seqs, dtype=jnp.int32)
    positions = (slot_seq[:, None] * frames_here + jnp.arange(frames_here, dtype=jnp.int32)).reshape(-1)
    ids = jnp.sum((positions[:, None] >= bounds[None, :]).astype(jnp.int32), axis=-1)
    lane = jnp.arange(PAIR, dtype=jnp.int32)[None, :]
    same = ids[:, None] == lane
    key_mask = same.astype(low)
    query_mask = jnp.where((lane < seg_lengths.shape[1]) & ~same, -1e30, 0.0).astype(low)
    half_dim = HEAD_DIM // 2
    inverse = jnp.exp(-math.log(10000.0) * jnp.arange(half_dim, dtype=jnp.float32) / half_dim)
    angles = positions.astype(jnp.float32)[:, None] * inverse[None, :]
    cosine = jnp.tile(jnp.cos(angles), (1, PAIR // half_dim))
    sine = jnp.tile(jnp.concatenate([-jnp.sin(angles), jnp.sin(angles)], axis=1), (1, 2))
    masks, tables = (query_mask, key_mask), (cosine, sine)

    pairs = local_heads // PAIR
    slots = lambda values: values.reshape(seqs, frames_here, -1)
    attn_in, qkv = project(x_slots, 1.0 + scale_attn, shift_attn, first_w, 3 * local_heads, cosine, sine)
    row_scale = lax.dynamic_index_in_dim(bucket_weights, bucket_ids[my_row], 0)
    grad_out = cotangent[0].astype(jnp.float32) * row_scale
    w_glu, w_down, grad_ffn_own, qkv = lax.optimization_barrier(
        (w_glu, w_down, (gate_ffn * grad_out).astype(low), qkv)
    )
    glu_slots = exchange(split_units(w_glu, seqs, part))
    down_lines = [w_down] + [swap(w_down, "row", 2 * j) for j in range(1, rows // 2)]
    grad_ffn_slots, near = spread_two(grad_ffn_own)
    mixed_heads, lse = attend(qkv, qkv, qkv, 0, pairs, 2 * pairs, pairs, 512, masks)
    mixed_heads, *got = lax.optimization_barrier(
        (mixed_heads, *grad_ffn_slots, *glu_slots, *down_lines)
    )
    grad_ffn_slots = got[: len(grad_ffn_slots)]
    glu_slots, down_lines = got[len(grad_ffn_slots) : -len(down_lines)], got[-len(down_lines) :]
    glu_w = lax.all_gather(natural(glu_slots).reshape(seqs * depth, -1), "row", axis=0, tiled=True)
    down_other = swap(jnp.stack(down_lines), "row", 1)
    down_w = [w for j in range(rows // 2) for w in (down_lines[j], down_other[j])]
    down_w = jnp.concatenate(natural(down_w, "row"))
    mixed_slots = slots(mixed_heads)
    mixed_got = [mixed_slots[0]] + [swap(mixed_slots[j], "seq", j) for j in range(1, seqs)]
    attn_mixed = side_by_side(mixed_got)
    attn_out = dot(attn_mixed, attn_w)
    inputs = x_own.astype(jnp.float32)
    after_attn = inputs + gate_attn * attn_out

    normed_c, inv_c = layer_stats(after_attn)
    cross_in = (normed_c * gain_values).astype(low)
    cross_q = dot(cross_in, crossq_w).astype(low)
    kv_mine = dot(context[0], kv_w).astype(low)
    cross_kv = side_by_side(spread(kv_mine))
    all_pairs = D // PAIR
    cross_mixed, cross_lse = attend(cross_q, cross_kv, cross_kv, 0, 0, all_pairs, all_pairs, frames_here)
    after_cross = after_attn + dot(cross_mixed, crossout_w)

    normed_f, inv_f = layer_stats(after_cross)
    ffn_in = (normed_f * (1.0 + scale_ffn) + shift_ffn).astype(low)
    units = FF // seqs
    ffn_slots, near = spread_two(ffn_in)
    if near is not None:
        ffn_slots.append(opposite(near))
        grad_ffn_slots = lax.optimization_barrier((*grad_ffn_slots, ffn_in))[:-1]
        grad_ffn_slots = [*grad_ffn_slots, opposite(grad_ffn_slots[1:])]
    gate_up = [dot(values, glu_w) for values in ffn_slots]
    gate_pre = [values[:, :units] for values in gate_up]
    up_pre = [values[:, units:] for values in gate_up]
    gate_act = [jax.nn.silu(values) for values in gate_pre]
    hidden = [(a * u).astype(low) for a, u in zip(gate_act, up_pre)]

    grad_hidden = [dot_right_t(values, down_w) for values in grad_ffn_slots]
    grad_gate_up = [
        jnp.concatenate([g * u * silu_slope(p), g * a], axis=-1).astype(low)
        for g, u, p, a in zip(grad_hidden, up_pre, gate_pre, gate_act)
    ]
    far_first = list(range(seqs - 1, -1, -1))

    def returned_near(parts):
        if seqs != 4:
            return [parts[0]] + [swap(parts[j], "seq", j) for j in range(1, seqs)]
        half = frames_here // 2
        return [
            swap(parts[3][:half], "seq", 1),
            swap(parts[3][half:], "seq", 2),
            swap(parts[1][:half], "seq", 1),
            swap(parts[2][half:], "seq", 2),
        ]

    def returned_far(parts, near):
        if seqs != 4:
            return near[1:], near[:1]
        half = frames_here // 2
        both = lambda left, right: left.astype(jnp.float32) + right.astype(jnp.float32)
        far = [
            swap(both(parts[2][:half], near[0]).astype(low), "seq", 2),
            swap(both(parts[1][half:], near[1]).astype(low), "seq", 1),
        ]
        return far, [both(parts[0][:half], near[2]), both(parts[0][half:], near[3])]

    def returned_total(far, near):
        if seqs != 4:
            return sum(term.astype(jnp.float32) for term in near + far)
        return jnp.concatenate([n + f.astype(jnp.float32) for n, f in zip(near, far)])

    ffn_back = {j: dot_right_t(grad_gate_up[j], glu_w).astype(low) for j in far_first}
    ffn_back_near = returned_near(ffn_back)
    ffn_all, hidden_all = jnp.concatenate(ffn_slots), jnp.concatenate(hidden)
    grad_glu = dot_left_t(ffn_all, jnp.concatenate(grad_gate_up)).astype(low)
    grad_down = dot_left_t(hidden_all, jnp.concatenate(grad_ffn_slots)).astype(low)
    ffn_parts = [dot(values, down_w).astype(low) for values in hidden]
    grad_glu, *ffn_back_near = lax.optimization_barrier((grad_glu, *ffn_back_near))
    ffn_back_far = returned_far(ffn_back, ffn_back_near)
    grad_ffn_in, grad_glu, grad_down, *ffn_parts = lax.optimization_barrier(
        (returned_total(*ffn_back_far), grad_glu, grad_down, *ffn_parts)
    )
    grad_glu = lax.psum_scatter(grad_glu, "row", scatter_dimension=0, tiled=True)
    grad_down = lax.psum_scatter(grad_down, "row", scatter_dimension=0, tiled=True)
    ffn_near = returned_near(ffn_parts)
    dshift_ffn = jnp.sum(grad_ffn_in, axis=0, keepdims=True)
    dscale_ffn = jnp.sum(grad_ffn_in * normed_f, axis=0, keepdims=True)
    grad_cross = grad_out + norm_back(grad_ffn_in * (1.0 + scale_ffn), normed_f, inv_f)

    grad_cross_low = grad_cross.astype(low)
    grad_cmixed = dot_right_t(grad_cross_low, crossout_w).astype(low)
    grad_cquery, grad_ckey, grad_cvalue = attend_back(
        cross_q, cross_kv, cross_kv, grad_cmixed, cross_mixed, cross_lse,
        0, 0, all_pairs, all_pairs, frames_here, text_len,
    )
    grad_cross_in = dot_right_t(grad_cquery, crossq_w)
    grad_gain = jnp.sum(grad_cross_in * normed_c, axis=0, keepdims=True)
    grad_attn = grad_cross + norm_back(grad_cross_in * gain_values, normed_c, inv_c)

    grad_attn_low = (gate_attn * grad_attn).astype(low)
    dgate_attn = jnp.sum(grad_attn * attn_out, axis=0, keepdims=True)
    grad_amixed = dot_right_t(grad_attn_low, attn_w).astype(low)
    grad_amixed, *ffn_near = lax.optimization_barrier((grad_amixed, *ffn_near))
    head_pieces = [columns(grad_amixed, "seq", j, local_heads) for j in range(seqs)]
    grad_heads = jnp.concatenate(
        [head_pieces[0]] + [swap(p, "seq", j) for j, p in enumerate(head_pieces) if j]
    )
    cross_mixed, cross_in, attn_mixed, grad_ckey, grad_amixed = lax.optimization_barrier(
        (cross_mixed, cross_in, attn_mixed, grad_ckey, grad_amixed)
    )

    core = my_row % 2
    wide_own = [
        dot_left_t(left, right).astype(low).reshape(rows // 2, 2, seqs, depth, D)
        for left, right in (
            (attn_mixed, grad_attn_low),
            (cross_in, grad_cquery),
            (cross_mixed, grad_cross_low),
        )
    ]
    half_of = lambda g, c: lax.dynamic_index_in_dim(g, c, 1, keepdims=False)
    wide_got = [swap(half_of(g, 1 - core), "row", 1) for g in wide_own]
    ffn_out = returned_total(*returned_far(ffn_parts, ffn_near))

    grad_ckv = jnp.concatenate([grad_ckey, grad_cvalue], axis=1)
    ckv_pieces = [columns(grad_ckv, "seq", j, kv_width) for j in range(seqs)]
    grad_ckv = ckv_pieces[0] + sum(swap(p, "seq", j) for j, p in enumerate(ckv_pieces) if j)
    grad_kv = dot_left_t(context[0], grad_ckv.astype(low)).astype(low)
    result = (after_cross + gate_ffn * ffn_out).astype(low)
    dgate_ffn = jnp.sum(grad_out * ffn_out, axis=0, keepdims=True)
    grad_heads, grad_kv, result, dgate_ffn, grad_glu, *wide_got = lax.optimization_barrier(
        (grad_heads, grad_kv, result, dgate_ffn, grad_glu, *wide_got)
    )
    glu_got = exchange(grad_glu.reshape(seqs, depth, -1))
    grad_kv = lax.psum_scatter(grad_kv, "row", scatter_dimension=0, tiled=True)
    wide_both = [(half_of(own, core), got) for own, got in zip(wide_own, wide_got)]

    def wide_piece(j):
        both = [
            pick(own, "seq", j, 1).astype(jnp.float32) + pick(got, "seq", j, 1).astype(jnp.float32)
            for own, got in wide_both
        ]
        return jnp.stack(both, axis=1).astype(low)

    wide_got = [wide_piece(j) for j in range(seqs)]
    wide_got = [wide_got[0]] + [swap(piece, "seq", j) for j, piece in enumerate(wide_got) if j]
    grad_projected = jnp.concatenate(
        attend_back(
            qkv, qkv, qkv, grad_heads, mixed_heads, lse,
            0, pairs, 2 * pairs, pairs, 512, 512, masks, tables,
        ),
        axis=1,
    )
    grad_projected, grad_down, grad_kv, *got = lax.optimization_barrier(
        (grad_projected, grad_down, grad_kv, *glu_got, *wide_got)
    )
    glu_got, wide_got = got[:seqs], got[seqs:]
    wide = sum(g.astype(jnp.float32) for g in wide_got).astype(low)
    grad_wide = lax.psum_scatter(
        wide,
        "row",
        scatter_dimension=0,
        axis_index_groups=[list(range(c, rows, 2)) for c in range(2)],
        tiled=True,
    )[0].astype(jnp.float32)
    grad_qkv = dot_left_t(attn_in, grad_projected).astype(low)
    grad_projected, grad_qkv = lax.optimization_barrier((grad_projected, grad_qkv))
    grad_qkv = lax.psum_scatter(grad_qkv, "row", scatter_dimension=0, tiled=True)
    attn_back, attn_sums = project_back(grad_projected, first_w, x_slots)
    own_sums = jnp.concatenate([attn_sums, dgate_attn, dshift_ffn, dscale_ffn, dgate_ffn, grad_gain])
    own_sums = sum_over(own_sums, "seq")
    attn_back = slots(after(attn_back, own_sums))
    attn_near = returned_near(attn_back)

    bucket_list = jnp.arange(BUCKETS, dtype=jnp.int32)
    grad_mods = jnp.zeros((BUCKETS, 6 * D), jnp.float32)
    gain_total = jnp.zeros((D,), jnp.float32)
    for j, sums in enumerate(spread(own_sums, "row")):
        hit = (bucket_list == bucket_ids[my_row ^ j]).astype(jnp.float32)
        grad_mods = grad_mods + hit[:, None] * sums[:6].reshape(1, 6 * D)
        gain_total = gain_total + sums[6]

    def outer(left, right):
        return sum(left[b][:, None] * right[b][None, :] for b in range(BUCKETS))

    def gather_row(own):
        return natural(spread(own, "row"), "row").transpose(1, 0, 2).reshape(BUCKETS, -1)

    def gather_seq(own):
        return natural(spread(own)).transpose(1, 0, 2).reshape(BUCKETS, -1)

    grad_modul = outer(mine(token_act, depth).astype(jnp.float32), grad_mods)
    token_own = jnp.dot(grad_mods, w_mod.astype(jnp.float32).T, precision=highest)
    token_own = token_own * silu_slope(mine(time_token, depth))
    token_own, *attn_near = lax.optimization_barrier((token_own, *attn_near))
    token_seq = gather_seq(token_own)
    token_seq, *attn_near = lax.optimization_barrier((token_seq, *attn_near))
    attn_far, attn_own = returned_far(attn_back, attn_near)
    grad_token = gather_row(token_seq)
    grad_timeout = outer(mine(time_hidden, depth).astype(jnp.float32), grad_token)
    hidden_own = jnp.dot(grad_token, w_time_out.astype(jnp.float32).T, precision=highest)
    hidden_own = hidden_own * silu_slope(mine(pre_hidden, depth))
    hidden_own, grad_qkv, *attn_far = lax.optimization_barrier((hidden_own, grad_qkv, *attn_far))
    qkv_got = exchange(grad_qkv.reshape(seqs, depth, -1))
    grad_attn_in = returned_total(attn_far, attn_own)
    hidden_seq, *qkv_got = lax.optimization_barrier((gather_seq(hidden_own), *qkv_got))
    grad_pre = gather_row(hidden_seq)
    grad_timein = outer(mine(features, w_time_in.shape[0]).astype(jnp.float32), grad_pre)
    normed_a, inv_a = layer_stats(inputs)
    grad_frames = grad_attn + norm_back(grad_attn_in * (1.0 + scale_attn), normed_a, inv_a)

    qkv_got = jnp.stack(qkv_got)
    grad_qkv = jnp.concatenate(
        [
            pick(qkv_got, "seq", t)[:, k * local_heads : (k + 1) * local_heads]
            for k in range(3)
            for t in range(seqs)
        ],
        axis=1,
    )
    grad_glu = join_units(natural(glu_got), part)
    grad_crosskv = side_by_side(exchange(grad_kv.reshape(seqs, ctx_dim // (rows * seqs), -1)))

    return (
        result[None],
        grad_frames[None],
        grad_timein,
        grad_timeout,
        grad_modul,
        grad_qkv.astype(jnp.float32),
        grad_wide[0],
        mine(gain_total, depth),
        grad_wide[1],
        grad_crosskv.astype(jnp.float32),
        grad_wide[2],
        grad_glu,
        grad_down.astype(jnp.float32),
    )


def solution(mesh):
    placed = (
        P("row", "seq", None),
        P("row", None, None),
        P("row", None),
        P(),
        P(),
        P(),
        P(("row", "seq"), None),
        P(("row", "seq"), None),
        P(("row", "seq"), None),
        P(("row", "seq"), None),
        P(("row", "seq"), None),
        P(("row", "seq")),
        P(("row", "seq"), None),
        P(("row", "seq"), None),
        P(("row", "seq"), None),
        P(("row", "seq"), None),
        P(("row", "seq"), None),
        P("row", "seq", None),
    )
    rows, seqs = mesh.shape["row"], mesh.shape["seq"]
    plan = functools.partial(on_device_split, rows, seqs) if can_split(rows, seqs) else on_device
    return jax.shard_map(
        plan,
        mesh=mesh,
        in_specs=placed,
        out_specs=(
            P("row", "seq", None),
            P("row", "seq", None),
            P(("row", "seq"), None),
            P(("row", "seq"), None),
            P(("row", "seq"), None),
            P(("row", "seq"), None),
            P(("row", "seq"), None),
            P(("row", "seq")),
            P(("row", "seq"), None),
            P(("row", "seq"), None),
            P(("row", "seq"), None),
            P(("row", "seq"), None),
            P(("row", "seq"), None),
        ),
        check_vma=False,
    )
```

```python
import functools
import math

import jax
import jax.numpy as jnp
from jax import lax
from jax.experimental import pallas as pl
from jax.experimental.pallas import tpu as pltpu
from jax.sharding import PartitionSpec as P

D = 1536
HEADS = 24
HEAD_DIM = 64
FF = 6144
TFREQ = 256
LENGTH = 2048
BUCKETS = 5
PAIR = 2 * HEAD_DIM
VMEM = 50 * 1024 * 1024
f32 = jnp.float32
bf16 = jnp.bfloat16


def dot_nt(left, right):
    return lax.dot_general(left, right, (((1,), (1,)), ((), ())), preferred_element_type=f32)


def dot_nn(left, right):
    return lax.dot_general(left, right, (((1,), (0,)), ((), ())), preferred_element_type=f32)


def swap_halves(values):
    lane = lax.broadcasted_iota(jnp.int32, values.shape, 1)
    ahead = pltpu.roll(values, PAIR - HEAD_DIM // 2, 1)
    behind = pltpu.roll(values, HEAD_DIM // 2, 1)
    return jnp.where((lane & (HEAD_DIM // 2)) == 0, ahead, behind)


def head_lanes(values, head):
    lane = lax.broadcasted_iota(jnp.int32, values.shape, 1)
    return jnp.where((lane // HEAD_DIM) == head, values, 0.0)


def norm_block(x_ref):
    values = x_ref[...].astype(f32)
    center = values - jnp.mean(values, axis=-1, keepdims=True)
    return center * lax.rsqrt(jnp.mean(center * center, axis=-1, keepdims=True) + 1e-05)


def joined(blocks):
    return blocks.reshape(blocks.shape[0] * blocks.shape[1], blocks.shape[2])


def gathered_spec(w, part, rows, width, **kwargs):
    return pl.BlockSpec((w.shape[0], rows, width), lambda i: (0, part, 0), **kwargs)


def project_kernel(per_slot, *refs):
    x_refs, (scale_ref, shift_ref, w_ref, cos_ref, sin_ref, in_ref, out_ref) = refs[:-7], refs[-7:]

    def run(x_ref):
        modulated = (norm_block(x_ref) * scale_ref[...] + shift_ref[...]).astype(bf16)
        in_ref[...] = modulated
        projected = dot_nn(modulated, joined(w_ref[...]))
        cosine = cos_ref[...]
        sine = sin_ref[...]
        width = out_ref.shape[1]
        for start in range(0, width, PAIR):
            part = projected[:, start : start + PAIR]
            if start < 2 * width // 3:
                part = part * cosine + swap_halves(part) * sine
            out_ref[:, start : start + PAIR] = part.astype(bf16)

    for slot, x_ref in enumerate(x_refs):
        pl.when(pl.program_id(0) // per_slot == slot)(functools.partial(run, x_ref))


def slot_specs(x_slots, block):
    per_slot, depth = x_slots[0].shape[0] // block, x_slots[0].shape[1]

    def one(slot):
        return pl.BlockSpec((block, depth), lambda i: (jnp.clip(i - slot * per_slot, 0, per_slot - 1), 0))

    return per_slot, [one(slot) for slot in range(len(x_slots))]


def project(x_slots, scale, shift, w, width, cosine, sine, block=256):
    per_slot, x_specs = slot_specs(x_slots, block)
    depth = x_slots[0].shape[1]
    count = len(x_slots) * x_slots[0].shape[0]
    row_spec = lambda cols: pl.BlockSpec((block, cols), lambda i: (i, 0))
    whole = lambda a: pl.BlockSpec(a.shape, lambda i: (0, 0))

    return pl.pallas_call(
        functools.partial(project_kernel, per_slot),
        grid=(count // block,),
        in_specs=x_specs
        + [
            whole(scale),
            whole(shift),
            gathered_spec(w, 0, depth // w.shape[0], width),
            row_spec(PAIR),
            row_spec(PAIR),
        ],
        out_specs=[row_spec(depth), row_spec(width)],
        out_shape=[
            jax.ShapeDtypeStruct((count, depth), bf16),
            jax.ShapeDtypeStruct((count, width), bf16),
        ],
        compiler_params=pltpu.CompilerParams(vmem_limit_bytes=VMEM),
        cost_estimate=pl.CostEstimate(
            flops=2 * count * depth * width,
            bytes_accessed=2 * (2 * count * depth + depth * width + count * width),
            transcendentals=count,
        ),
        name="project",
    )(*x_slots, scale, shift, w, cosine, sine)


def project_back_kernel(per_slot, *refs):
    x_refs, (grad_ref, w_ref, out_ref, sums_ref) = refs[:-4], refs[-4:]

    @pl.when(pl.program_id(0) == 0)
    def _():
        sums_ref[...] = jnp.zeros_like(sums_ref)

    def run(x_ref):
        part = dot_nt(grad_ref[...], joined(w_ref[...]))
        out_ref[...] = part.astype(bf16)
        sums_ref[0:1, :] += jnp.sum(part, axis=0, keepdims=True)
        sums_ref[1:2, :] += jnp.sum(part * norm_block(x_ref), axis=0, keepdims=True)

    for slot, x_ref in enumerate(x_refs):
        pl.when(pl.program_id(0) // per_slot == slot)(functools.partial(run, x_ref))


def project_back(grad, w, x_slots, block=256):
    per_slot, x_specs = slot_specs(x_slots, block)
    count, width = grad.shape
    depth = x_slots[0].shape[1]
    return pl.pallas_call(
        functools.partial(project_back_kernel, per_slot),
        grid=(count // block,),
        in_specs=x_specs
        + [
            pl.BlockSpec((block, width), lambda i: (i, 0)),
            gathered_spec(w, 0, depth // w.shape[0], width),
        ],
        out_specs=[
            pl.BlockSpec((block, depth), lambda i: (i, 0)),
            pl.BlockSpec((2, depth), lambda i: (0, 0)),
        ],
        out_shape=[
            jax.ShapeDtypeStruct((count, depth), bf16),
            jax.ShapeDtypeStruct((2, depth), f32),
        ],
        compiler_params=pltpu.CompilerParams(vmem_limit_bytes=VMEM),
        cost_estimate=pl.CostEstimate(
            flops=2 * count * depth * width,
            bytes_accessed=2 * (2 * count * depth + depth * width + count * width),
            transcendentals=count,
        ),
        name="project_back",
    )(*x_slots, grad, w)


def attend_kernel(masked, *refs):
    if masked:
        q_ref, k_ref, v_ref, qmask_ref, kmask_ref, o_ref, lse_ref, keys, values_t = refs
    else:
        q_ref, k_ref, v_ref, o_ref, lse_ref, keys, values_t = refs

    @pl.when(pl.program_id(1) == 0)
    def _():
        keys[:, :PAIR] = k_ref[...]
        if masked:
            keys[:, PAIR:] = kmask_ref[...]
        values_t[...] = v_ref[...].astype(f32).T.astype(bf16)

    queries = q_ref[...].astype(f32) * 0.125
    mixed = []
    for head in range(2):
        query = head_lanes(queries, head).astype(bf16)
        if masked:
            query = jnp.concatenate([query, qmask_ref[...]], axis=1)
        scores = dot_nt(keys[...], query)
        top = jnp.max(scores, axis=0, keepdims=True)
        shifted = jnp.exp(scores - top)
        total = jnp.sum(shifted, axis=0, keepdims=True)
        own = values_t[head * HEAD_DIM : (head + 1) * HEAD_DIM, :]
        mixed.append(dot_nn(own, shifted.astype(bf16)) / total)
        lse_ref[0, head : head + 1, :] = top + jnp.log(total)
    o_ref[...] = jnp.concatenate(mixed, axis=0).T.astype(bf16)


def attend(q, k, v, q_col, k_col, v_col, pairs, block, masks=None):
    count, keys = q.shape[0], k.shape[0]
    masked = masks is not None
    in_specs = [
        pl.BlockSpec((block, PAIR), lambda p, i: (i, q_col + p)),
        pl.BlockSpec((keys, PAIR), lambda p, i: (0, k_col + p)),
        pl.BlockSpec((keys, PAIR), lambda p, i: (0, v_col + p)),
    ]
    if masked:
        in_specs += [
            pl.BlockSpec((block, PAIR), lambda p, i: (i, 0)),
            pl.BlockSpec((keys, PAIR), lambda p, i: (0, 0)),
        ]
    return pl.pallas_call(
        functools.partial(attend_kernel, masked),
        grid=(pairs, count // block),
        in_specs=in_specs,
        out_specs=[
            pl.BlockSpec((block, PAIR), lambda p, i: (i, p)),
            pl.BlockSpec((1, 2, block), lambda p, i: (p, 0, i)),
        ],
        out_shape=[
            jax.ShapeDtypeStruct((count, pairs * PAIR), bf16),
            jax.ShapeDtypeStruct((pairs, 2, count), f32),
        ],
        scratch_shapes=[
            pltpu.VMEM((keys, (2 if masked else 1) * PAIR), bf16),
            pltpu.VMEM((PAIR, keys), bf16),
        ],
        compiler_params=pltpu.CompilerParams(vmem_limit_bytes=VMEM),
        cost_estimate=pl.CostEstimate(
            flops=16 * pairs * PAIR * count * keys,
            bytes_accessed=2 * pairs * PAIR * (2 * count + 2 * keys),
            transcendentals=2 * pairs * count * keys,
        ),
        name="attend",
    )(q, k, v, *(masks or ()))


def attend_back_kernel(masked, chunk, *refs):
    if masked:
        (q_ref, k_ref, v_ref, do_ref, o_ref, lse_ref, qmask_ref, kmask_ref, qcos_ref, qsin_ref,
         kcos_ref, ksin_ref, dq_ref, dk_ref, dv_ref, keys, keys_t, dk_sum, dv_sum) = refs
    else:
        (q_ref, k_ref, v_ref, do_ref, o_ref, lse_ref,
         dq_ref, dk_ref, dv_ref, keys, keys_t, dk_sum, dv_sum) = refs
    step = pl.program_id(1)
    count = k_ref.shape[0]

    @pl.when(step == 0)
    def _():
        keys[:, :PAIR] = k_ref[...]
        if masked:
            keys[:, PAIR:] = kmask_ref[...]
        keys_t[...] = k_ref[...].astype(f32).T.astype(bf16)
        dk_sum[...] = jnp.zeros_like(dk_sum)
        dv_sum[...] = jnp.zeros_like(dv_sum)

    queries = q_ref[...].astype(f32) * 0.125
    grads = do_ref[...].astype(f32)
    rows_t = (grads * o_ref[...].astype(f32)).T
    parts = []
    for head in range(2):
        lanes = slice(head * HEAD_DIM, (head + 1) * HEAD_DIM)
        delta = jnp.sum(rows_t[lanes, :], axis=0, keepdims=True)
        log_row = lse_ref[0, head : head + 1, :]
        query = head_lanes(queries, head).astype(bf16)
        grad = head_lanes(grads, head).astype(bf16)
        full = jnp.concatenate([query, qmask_ref[...]], axis=1) if masked else query
        total = None
        for start in range(0, count, chunk):
            here = slice(start, start + chunk)
            soft = jnp.exp(dot_nt(keys[here, :], full) - log_row)
            grad_soft = dot_nt(v_ref[here, :], grad)
            grad_scores = (soft * (grad_soft - delta)).astype(bf16)
            dv_sum[here, :] += dot_nn(soft.astype(bf16), grad)
            dk_sum[here, :] += dot_nn(grad_scores, query)
            part = dot_nn(keys_t[lanes, here], grad_scores)
            total = part if total is None else total + part
        parts.append(total)
    dq = jnp.concatenate(parts, axis=0).T * 0.125
    if masked:
        dq = dq * qcos_ref[...] - swap_halves(dq) * qsin_ref[...]
    dq_ref[...] = dq.astype(dq_ref.dtype)

    @pl.when(step == pl.num_programs(1) - 1)
    def _():
        dk = dk_sum[...]
        if masked:
            dk = dk * kcos_ref[...] - swap_halves(dk) * ksin_ref[...]
        dk_ref[...] = dk.astype(dk_ref.dtype)
        dv_ref[...] = dv_sum[...].astype(dv_ref.dtype)


def attend_back(q, k, v, do, o, lse, q_col, k_col, v_col, pairs, block, chunk, masks=None, tables=None):
    count, keys = q.shape[0], k.shape[0]
    masked = masks is not None
    out_type = bf16 if masked else f32
    rows = lambda col: pl.BlockSpec((block, PAIR), lambda p, i: (i, col + p))
    whole = lambda col: pl.BlockSpec((keys, PAIR), lambda p, i: (0, col + p))
    in_specs = [
        rows(q_col), whole(k_col), whole(v_col), rows(0), rows(0),
        pl.BlockSpec((1, 2, block), lambda p, i: (p, 0, i)),
    ]
    operands = [q, k, v, do, o, lse]
    if masked:
        rows_fixed = pl.BlockSpec((block, PAIR), lambda p, i: (i, 0))
        whole_fixed = pl.BlockSpec((keys, PAIR), lambda p, i: (0, 0))
        in_specs += [rows_fixed, whole_fixed, rows_fixed, rows_fixed, whole_fixed, whole_fixed]
        operands += [masks[0], masks[1], tables[0], tables[1], tables[0], tables[1]]
    return pl.pallas_call(
        functools.partial(attend_back_kernel, masked, chunk),
        grid=(pairs, count // block),
        in_specs=in_specs,
        out_specs=[rows(0), whole(0), whole(0)],
        out_shape=[
            jax.ShapeDtypeStruct((count, pairs * PAIR), bf16),
            jax.ShapeDtypeStruct((keys, pairs * PAIR), out_type),
            jax.ShapeDtypeStruct((keys, pairs * PAIR), out_type),
        ],
        scratch_shapes=[
            pltpu.VMEM((keys, (2 if masked else 1) * PAIR), bf16),
            pltpu.VMEM((PAIR, keys), bf16),
            pltpu.VMEM((keys, PAIR), f32),
            pltpu.VMEM((keys, PAIR), f32),
        ],
        compiler_params=pltpu.CompilerParams(vmem_limit_bytes=VMEM),
        cost_estimate=pl.CostEstimate(
            flops=40 * pairs * PAIR * count * keys,
            bytes_accessed=2 * pairs * PAIR * (4 * count + 4 * keys),
            transcendentals=2 * pairs * count * keys,
        ),
        name="attend_back",
    )(*operands)
def split_units_kernel(seqs, part, w_ref, out_ref):
    block = seqs * part
    for pair in range(w_ref.shape[1] // (2 * block)):
        groups = [
            w_ref[:, (2 * pair + k) * block : (2 * pair + k + 1) * block].astype(f32) for k in range(2)
        ]
        for t in range(seqs):
            both = [g[:, t * part : (t + 1) * part] for g in groups]
            out_ref[t, :, 2 * pair * part : 2 * (pair + 1) * part] = jnp.concatenate(both, axis=1).astype(bf16)


def split_units(w, seqs, part):
    depth, width = w.shape
    return pl.pallas_call(
        functools.partial(split_units_kernel, seqs, part),
        out_shape=jax.ShapeDtypeStruct((seqs, depth, width // seqs), bf16),
        compiler_params=pltpu.CompilerParams(vmem_limit_bytes=VMEM),
        cost_estimate=pl.CostEstimate(flops=0, bytes_accessed=4 * depth * width, transcendentals=0),
        name="split_units",
    )(w)


def join_units_kernel(seqs, part, in_ref, out_ref):
    block = seqs * part
    for pair in range(out_ref.shape[1] // (2 * block)):
        both = [in_ref[t, :, 2 * pair * part : 2 * (pair + 1) * part].astype(f32) for t in range(seqs)]
        for k in range(2):
            group = [b[:, k * part : (k + 1) * part] for b in both]
            out_ref[:, (2 * pair + k) * block : (2 * pair + k + 1) * block] = jnp.concatenate(group, axis=1)


def join_units(stack, part):
    seqs, depth, width = stack.shape
    return pl.pallas_call(
        functools.partial(join_units_kernel, seqs, part),
        out_shape=jax.ShapeDtypeStruct((depth, width * seqs), f32),
        compiler_params=pltpu.CompilerParams(vmem_limit_bytes=VMEM),
        cost_estimate=pl.CostEstimate(flops=0, bytes_accessed=6 * depth * width * seqs, transcendentals=0),
        name="join_units",
    )(stack)


def feed_kernel(per_slot, slots, chunk, chained, *refs):
    x_refs, g_refs = refs[:slots], refs[slots : 2 * slots]
    gate_ref, scale_ref, glu_ref, down_ref = refs[2 * slots : 2 * slots + 4]
    outs = refs[2 * slots + 4 + (4 if chained else 0) :]
    x_out, g_out, hidden_ref, grads_ref, back_ref, out_ref, dgate_ref, back_sum, out_sum = outs
    blocks, block_units = down_ref.shape[:2]
    units = blocks * block_units
    taken = chunk // block_units

    def run(x_ref, g_ref):
        x = x_ref[...]
        grad_out = g_ref[...].astype(f32) * scale_ref[...]
        g = (gate_ref[...] * grad_out).astype(bf16)
        x_out[...] = x
        g_out[...] = g
        for start in range(0, units, chunk):
            gate_cols, up_cols = slice(start, start + chunk), slice(units + start, units + start + chunk)
            gate = dot_nn(x, glu_ref[:, gate_cols])
            up = dot_nn(x, glu_ref[:, up_cols])
            down = joined(down_ref[start // block_units : start // block_units + taken])
            grad_hidden = dot_nt(g, down)
            opened = 1.0 / (1.0 + jnp.exp(-gate))
            act = gate * opened
            hidden = (act * up).astype(bf16)
            grad_gate = (grad_hidden * up * (opened * (1.0 + gate * (1.0 - opened)))).astype(bf16)
            grad_up = (grad_hidden * act).astype(bf16)
            hidden_ref[:, gate_cols] = hidden
            grads_ref[:, gate_cols] = grad_gate
            grads_ref[:, up_cols] = grad_up
            back = dot_nt(grad_gate, glu_ref[:, gate_cols]) + dot_nt(grad_up, glu_ref[:, up_cols])
            out = dot_nn(hidden, down)
            if start == 0:
                back_sum[...] = back
                out_sum[...] = out
            else:
                back_sum[...] += back
                out_sum[...] += out
        back_ref[...] = back_sum[...].astype(bf16)
        out_ref[...] = out_sum[...].astype(bf16)
        dgate_ref[...] += jnp.sum(grad_out * out_sum[...], axis=0, keepdims=True)

    @pl.when(pl.program_id(0) == 0)
    def _():
        dgate_ref[...] = jnp.zeros_like(dgate_ref)

    for slot in range(slots):
        pl.when(pl.program_id(0) // per_slot == slot)(functools.partial(run, x_refs[slot], g_refs[slot]))


def feed(x_slots, g_slots, gate, scale, glu, down, first, total, kept=None, block=256):
    per_slot, x_specs = slot_specs(x_slots, block)
    slots, (frames, depth) = len(x_slots), x_slots[0].shape
    count, units = slots * frames, glu.shape[1] // 2
    chunk = units // 2
    own_units = units // down.shape[0]
    offset = first * per_slot
    own_rows = lambda cols: pl.BlockSpec((block, cols), lambda i: (i, 0))
    all_rows = lambda cols: pl.BlockSpec((block, cols), lambda i: (i + offset, 0))
    whole = lambda a: pl.BlockSpec(a.shape, lambda i: (0, 0), pipeline_mode=pl.Buffered(1))
    everywhere = [depth, depth, units, 2 * units]
    return pl.pallas_call(
        functools.partial(feed_kernel, per_slot, slots, chunk, kept is not None),
        grid=(count // block,),
        in_specs=x_specs
        + slot_specs(g_slots, block)[1]
        + [
            whole(gate),
            whole(scale),
            whole(glu),
            gathered_spec(
                down, down.shape[1] // own_units - 1, own_units, depth, pipeline_mode=pl.Buffered(1)
            ),
        ]
        + [pl.BlockSpec(memory_space=pl.ANY)] * (4 if kept is not None else 0),
        out_specs=[all_rows(cols) for cols in everywhere] + [own_rows(depth), own_rows(depth), pl.BlockSpec((1, depth), lambda i: (0, 0))],
        out_shape=[jax.ShapeDtypeStruct((total * frames, cols), bf16) for cols in everywhere]
        + [jax.ShapeDtypeStruct((count, depth), bf16)] * 2
        + [jax.ShapeDtypeStruct((1, depth), f32)],
        scratch_shapes=[pltpu.VMEM((block, depth), f32), pltpu.VMEM((block, depth), f32)],
        input_output_aliases={2 * slots + 4 + k: k for k in range(4)} if kept is not None else {},
        compiler_params=pltpu.CompilerParams(vmem_limit_bytes=VMEM),
        cost_estimate=pl.CostEstimate(
            flops=12 * count * depth * units,
            bytes_accessed=2 * (3 * depth * units + count * (6 * depth + 3 * units)),
            transcendentals=count * units,
        ),
        name="feed",
    )(*x_slots, *g_slots, gate, scale, glu, down, *(kept or ()))


def outer_kernel(left_ref, right_ref, out_ref):
    left = left_ref[...].T
    height = out_ref.shape[0]
    total = left[:height, 0:1] * right_ref[0:1, :]
    for b in range(1, right_ref.shape[0]):
        total += left[:height, b : b + 1] * right_ref[b : b + 1, :]
    out_ref[...] = total


def outer(left, right):
    buckets, height = left.shape
    width = right.shape[1]
    left = jnp.pad(left.astype(f32), ((0, -buckets % 8), (0, -height % 128)))
    return pl.pallas_call(
        outer_kernel,
        out_shape=jax.ShapeDtypeStruct((height, width), f32),
        compiler_params=pltpu.CompilerParams(vmem_limit_bytes=VMEM),
        cost_estimate=pl.CostEstimate(
            flops=2 * buckets * height * width, bytes_accessed=4 * height * width, transcendentals=0
        ),
        name="outer",
    )(left, right)


def text_product_kernel(left_ref, right_ref, out_ref):
    left = left_ref[...].astype(f32).T.astype(bf16)
    out_ref[...] = dot_nn(left, right_ref[...]).astype(bf16)


def text_product(left, right, block=1024):
    tokens, height = left.shape
    width = right.shape[1]
    return pl.pallas_call(
        text_product_kernel,
        grid=(width // block,),
        in_specs=[
            pl.BlockSpec((tokens, height), lambda i: (0, 0)),
            pl.BlockSpec((tokens, block), lambda i: (0, i)),
        ],
        out_specs=pl.BlockSpec((height, block), lambda i: (0, i)),
        out_shape=jax.ShapeDtypeStruct((height, width), bf16),
        compiler_params=pltpu.CompilerParams(vmem_limit_bytes=VMEM),
        cost_estimate=pl.CostEstimate(
            flops=2 * tokens * height * width, bytes_accessed=2 * height * width, transcendentals=0
        ),
        name="text_product",
    )(left, right)


highest = lax.Precision.HIGHEST


def matmul(left, right):
    return jnp.einsum("...i,ij->...j", left, right, preferred_element_type=jnp.float32)


def matmul_t(left, right):
    return jnp.einsum("...j,ij->...i", left, right, preferred_element_type=jnp.float32)


def outer_sum(left, right):
    return jnp.einsum("rfi,rfj->ij", left, right, preferred_element_type=jnp.float32)


def layer_stats(values):
    center = values - jnp.mean(values, axis=-1, keepdims=True)
    inv_std = lax.rsqrt(jnp.mean(center * center, axis=-1, keepdims=True) + 1e-05)
    return (center * inv_std, inv_std)


def norm_back(grad_normed, normed, inv_std):
    return inv_std * (
        grad_normed
        - jnp.mean(grad_normed, axis=-1, keepdims=True)
        - normed * jnp.mean(grad_normed * normed, axis=-1, keepdims=True)
    )


def silu_slope(values):
    sigmoid_part = jax.nn.sigmoid(values)
    return sigmoid_part * (1.0 + values * (1.0 - sigmoid_part))


def angle_tables(positions):
    half_dim = HEAD_DIM // 2
    inverse = jnp.exp(-math.log(10000.0) * jnp.arange(half_dim, dtype=jnp.float32) / half_dim)
    angles = positions[:, None] * inverse[None, :]
    return (jnp.cos(angles)[:, None, :], jnp.sin(angles)[:, None, :])


def rotate(values, cosine, sine_table):
    half_dim = values.shape[-1] // 2
    first_half = values[..., :half_dim]
    second_half = values[..., half_dim:]
    return jnp.concatenate(
        [
            first_half * cosine - second_half * sine_table,
            second_half * cosine + first_half * sine_table,
        ],
        axis=-1,
    )


def time_features(times):
    half_dim = TFREQ // 2
    freqs = jnp.exp(-math.log(10000.0) * jnp.arange(half_dim, dtype=jnp.float32) / half_dim)
    angles = times[:, None] * freqs[None, :]
    return jnp.concatenate([jnp.cos(angles), jnp.sin(angles)], axis=-1)


def stamp_rows(times, time_in, time_out, modul):
    features = time_features(times).astype(jnp.bfloat16)
    pre_hidden = jnp.dot(features, time_in, preferred_element_type=jnp.float32)
    time_hidden = jax.nn.silu(pre_hidden).astype(jnp.bfloat16)
    time_token = jnp.dot(time_hidden, time_out, preferred_element_type=jnp.float32)
    token_act = jax.nn.silu(time_token).astype(jnp.bfloat16)
    modulation = jnp.dot(token_act, modul, preferred_element_type=jnp.float32)
    return (features, pre_hidden, time_hidden, time_token, token_act, modulation)


def self_forward(row_inputs):
    query_row, key_row, value_row, local_row, whole_row = row_inputs
    allowed = local_row[:, None] == whole_row[None, :]
    scores = (
        jnp.einsum("qhd,khd->hqk", query_row, key_row, preferred_element_type=jnp.float32) * 0.125
    )
    scores = jnp.where(allowed[None], scores, -1e30)
    row_max = jnp.max(scores, axis=-1, keepdims=True)
    shifted = jnp.exp(scores - row_max)
    denominator = jnp.sum(shifted, axis=-1, keepdims=True)
    soft_weights = (shifted / denominator).astype(jnp.bfloat16)
    mixed = jnp.einsum("hqk,khd->qhd", soft_weights, value_row, preferred_element_type=jnp.float32)
    return (mixed.astype(jnp.bfloat16), row_max + jnp.log(denominator))


def self_backward(row_inputs):
    query_row, key_row, value_row, grad_row, log_row, local_row, whole_row = row_inputs
    allowed = local_row[:, None] == whole_row[None, :]
    scores = (
        jnp.einsum("qhd,khd->hqk", query_row, key_row, preferred_element_type=jnp.float32) * 0.125
    )
    soft_again = jnp.exp(jnp.where(allowed[None], scores, -1e30) - log_row)
    grad_soft = jnp.einsum("qhd,khd->hqk", grad_row, value_row, preferred_element_type=jnp.float32)
    grad_scores = (
        soft_again * (grad_soft - jnp.sum(soft_again * grad_soft, axis=-1, keepdims=True))
    ).astype(jnp.bfloat16)
    grad_query = (
        jnp.einsum("hqk,khd->qhd", grad_scores, key_row, preferred_element_type=jnp.float32) * 0.125
    )
    key_part = (
        jnp.einsum("hqk,qhd->khd", grad_scores, query_row, preferred_element_type=jnp.float32)
        * 0.125
    )
    value_part = jnp.einsum(
        "hqk,qhd->khd",
        soft_again.astype(jnp.bfloat16),
        grad_row,
        preferred_element_type=jnp.float32,
    )
    return (grad_query, key_part, value_part)


def on_device(
    frames,
    context,
    seg_lengths,
    bucket_ids,
    timesteps,
    bucket_weights,
    w_time_in,
    w_time_out,
    w_mod,
    w_qkv,
    w_attn_out,
    cross_gain,
    w_cross_q,
    w_cross_kv,
    w_cross_out,
    w_glu,
    w_down,
    cotangent,
):
    fwd_weights = (
        lax.all_gather(w_time_in, ("row", "seq"), axis=0, tiled=True),
        lax.all_gather(w_time_out, ("row", "seq"), axis=0, tiled=True),
        lax.all_gather(w_mod, ("row", "seq"), axis=0, tiled=True),
        lax.all_gather(w_qkv, ("row", "seq"), axis=0, tiled=True),
        lax.all_gather(w_attn_out, ("row", "seq"), axis=0, tiled=True),
        lax.all_gather(cross_gain, ("row", "seq"), axis=0, tiled=True),
        lax.all_gather(w_cross_q, ("row", "seq"), axis=0, tiled=True),
        lax.all_gather(w_cross_kv, ("row", "seq"), axis=0, tiled=True),
        lax.all_gather(w_cross_out, ("row", "seq"), axis=0, tiled=True),
        lax.all_gather(w_glu, ("row", "seq"), axis=0, tiled=True),
        lax.all_gather(w_down, ("row", "seq"), axis=0, tiled=True),
    )
    (
        time_in,
        time_out,
        modul,
        qkv_w,
        attn_w,
        gain_w,
        crossq_w,
        crosskv_w,
        crossout_w,
        glu_w,
        down_w,
    ) = fwd_weights
    rows_here = frames.shape[0]
    frames_here = frames.shape[1]
    text_len = context.shape[1]
    row_start = lax.axis_index("row") * rows_here
    seq_start = lax.axis_index("seq") * frames_here
    my_buckets = lax.dynamic_slice_in_dim(bucket_ids, row_start, rows_here)
    onehot = (my_buckets[:, None] == jnp.arange(BUCKETS, dtype=jnp.int32)[None, :]).astype(
        jnp.float32
    )
    my_times = jnp.dot(onehot, timesteps.astype(jnp.float32), precision=highest)
    features, pre_hidden, time_hidden, time_token, token_act, modulation = stamp_rows(
        my_times, time_in, time_out, modul
    )
    shift_attn = modulation[:, None, 0:D]
    scale_attn = modulation[:, None, D : 2 * D]
    gate_attn = modulation[:, None, 2 * D : 3 * D]
    shift_ffn = modulation[:, None, 3 * D : 4 * D]
    scale_ffn = modulation[:, None, 4 * D : 5 * D]
    gate_ffn = modulation[:, None, 5 * D : 6 * D]
    bounds = jnp.cumsum(seg_lengths, axis=-1)
    all_positions = jnp.arange(LENGTH, dtype=jnp.int32)
    all_ids = jnp.sum(
        (all_positions[None, :, None] >= bounds[:, None, :]).astype(jnp.int32), axis=-1
    )
    local_ids = lax.dynamic_slice_in_dim(all_ids, seq_start, frames_here, 1)
    cosine, sine_table = angle_tables(
        (seq_start + jnp.arange(frames_here, dtype=jnp.int32)).astype(jnp.float32)
    )
    inputs = frames.astype(jnp.float32)
    normed_a, inv_a = layer_stats(inputs)
    attn_in = (normed_a * (1.0 + scale_attn) + shift_attn).astype(jnp.bfloat16)
    projected = matmul(attn_in, qkv_w)
    query_pre = projected[..., :D].reshape(rows_here, frames_here, HEADS, HEAD_DIM)
    key_pre = projected[..., D : 2 * D].reshape(rows_here, frames_here, HEADS, HEAD_DIM)
    value_pre = projected[..., 2 * D :].reshape(rows_here, frames_here, HEADS, HEAD_DIM)
    queries = rotate(query_pre, cosine, sine_table).astype(jnp.bfloat16)
    key_local = rotate(key_pre, cosine, sine_table).astype(jnp.bfloat16)
    value_local = value_pre.astype(jnp.bfloat16)
    key_rows, value_rows = (
        lax.all_gather(key_local, "seq", axis=1, tiled=True),
        lax.all_gather(value_local, "seq", axis=1, tiled=True),
    )
    mixed_rows, log_total = lax.map(
        self_forward, (queries, key_rows, value_rows, local_ids, all_ids)
    )
    attn_mixed = mixed_rows.reshape(rows_here, frames_here, D)
    attn_out = matmul(attn_mixed, attn_w)
    after_attn = inputs + gate_attn * attn_out
    normed_c, inv_c = layer_stats(after_attn)
    gain_values = gain_w.astype(jnp.float32)
    cross_in = (normed_c * gain_values).astype(jnp.bfloat16)
    cross_q = (
        matmul(cross_in, crossq_w)
        .astype(jnp.bfloat16)
        .reshape(rows_here, frames_here, HEADS, HEAD_DIM)
    )
    cross_kv = jnp.einsum(
        "rcm,me->rce", context, crosskv_w, preferred_element_type=jnp.float32
    ).astype(jnp.bfloat16)
    cross_k = cross_kv[..., :D].reshape(rows_here, text_len, HEADS, HEAD_DIM)
    cross_v = cross_kv[..., D:].reshape(rows_here, text_len, HEADS, HEAD_DIM)
    cross_scores = (
        jnp.einsum("rqhd,rchd->rhqc", cross_q, cross_k, preferred_element_type=jnp.float32) * 0.125
    )
    cross_shift = jnp.exp(cross_scores - jnp.max(cross_scores, axis=-1, keepdims=True))
    cross_soft = cross_shift / jnp.sum(cross_shift, axis=-1, keepdims=True)
    cross_soft_low = cross_soft.astype(jnp.bfloat16)
    cross_mixed = (
        jnp.einsum("rhqc,rchd->rqhd", cross_soft_low, cross_v, preferred_element_type=jnp.float32)
        .reshape(rows_here, frames_here, D)
        .astype(jnp.bfloat16)
    )
    cross_out = matmul(cross_mixed, crossout_w)
    after_cross = after_attn + cross_out
    normed_f, inv_f = layer_stats(after_cross)
    ffn_in = (normed_f * (1.0 + scale_ffn) + shift_ffn).astype(jnp.bfloat16)
    gate_up = matmul(ffn_in, glu_w)
    gate_pre = gate_up[..., :FF]
    up_pre = gate_up[..., FF:]
    gate_act = jax.nn.silu(gate_pre)
    hidden = (gate_act * up_pre).astype(jnp.bfloat16)
    ffn_out = matmul(hidden, down_w)
    result = (after_cross + gate_ffn * ffn_out).astype(jnp.bfloat16)
    bwd_weights = (
        lax.all_gather(w_time_in, ("row", "seq"), axis=0, tiled=True),
        lax.all_gather(w_time_out, ("row", "seq"), axis=0, tiled=True),
        lax.all_gather(w_mod, ("row", "seq"), axis=0, tiled=True),
        lax.all_gather(w_qkv, ("row", "seq"), axis=0, tiled=True),
        lax.all_gather(w_attn_out, ("row", "seq"), axis=0, tiled=True),
        lax.all_gather(cross_gain, ("row", "seq"), axis=0, tiled=True),
        lax.all_gather(w_cross_q, ("row", "seq"), axis=0, tiled=True),
        lax.all_gather(w_cross_kv, ("row", "seq"), axis=0, tiled=True),
        lax.all_gather(w_cross_out, ("row", "seq"), axis=0, tiled=True),
        lax.all_gather(w_glu, ("row", "seq"), axis=0, tiled=True),
        lax.all_gather(w_down, ("row", "seq"), axis=0, tiled=True),
    )
    (
        time_in,
        time_out,
        modul,
        qkv_w,
        attn_w,
        gain_w,
        crossq_w,
        crosskv_w,
        crossout_w,
        glu_w,
        down_w,
    ) = bwd_weights
    row_scale = jnp.dot(onehot, bucket_weights, precision=highest)
    grad_out = cotangent.astype(jnp.float32) * row_scale[:, None, None]
    grad_ffn_low = (gate_ffn * grad_out).astype(jnp.bfloat16)
    dgate_ffn = jnp.sum(grad_out * ffn_out, axis=1)
    grad_down = outer_sum(hidden, grad_ffn_low)
    grad_hidden = matmul_t(grad_ffn_low, down_w)
    grad_gate_up = jnp.concatenate(
        [grad_hidden * up_pre * silu_slope(gate_pre), grad_hidden * gate_act], axis=-1
    ).astype(jnp.bfloat16)
    grad_glu = outer_sum(ffn_in, grad_gate_up)
    grad_ffn_in = matmul_t(grad_gate_up, glu_w)
    dshift_ffn = jnp.sum(grad_ffn_in, axis=1)
    dscale_ffn = jnp.sum(grad_ffn_in * normed_f, axis=1)
    grad_cross = grad_out + norm_back(grad_ffn_in * (1.0 + scale_ffn), normed_f, inv_f)
    ffn_grads = (
        lax.psum_scatter(grad_glu, ("row", "seq"), scatter_dimension=0, tiled=True),
        lax.psum_scatter(grad_down, ("row", "seq"), scatter_dimension=0, tiled=True),
    )
    grad_cross_low = grad_cross.astype(jnp.bfloat16)
    grad_crossout = outer_sum(cross_mixed, grad_cross_low)
    grad_cmixed = (
        matmul_t(grad_cross_low, crossout_w)
        .astype(jnp.bfloat16)
        .reshape(rows_here, frames_here, HEADS, HEAD_DIM)
    )
    grad_csoft = jnp.einsum(
        "rqhd,rchd->rhqc", grad_cmixed, cross_v, preferred_element_type=jnp.float32
    )
    grad_cvalue = jnp.einsum(
        "rhqc,rqhd->rchd", cross_soft_low, grad_cmixed, preferred_element_type=jnp.float32
    )
    grad_cscores = (
        cross_soft * (grad_csoft - jnp.sum(cross_soft * grad_csoft, axis=-1, keepdims=True))
    ).astype(jnp.bfloat16)
    grad_cquery = (
        (
            jnp.einsum("rhqc,rchd->rqhd", grad_cscores, cross_k, preferred_element_type=jnp.float32)
            * 0.125
        )
        .reshape(rows_here, frames_here, D)
        .astype(jnp.bfloat16)
    )
    grad_ckey = (
        jnp.einsum("rhqc,rqhd->rchd", grad_cscores, cross_q, preferred_element_type=jnp.float32)
        * 0.125
    )
    grad_ckv = jnp.concatenate(
        [grad_ckey.reshape(rows_here, text_len, D), grad_cvalue.reshape(rows_here, text_len, D)],
        axis=-1,
    )
    grad_crosskv = jnp.einsum(
        "rcm,rce->me", context.astype(jnp.float32), grad_ckv, precision=highest
    )
    grad_crossq = outer_sum(cross_in, grad_cquery)
    grad_cross_in = matmul_t(grad_cquery, crossq_w)
    grad_gain = jnp.sum(grad_cross_in * normed_c, axis=(0, 1))
    grad_attn = grad_cross + norm_back(grad_cross_in * gain_values, normed_c, inv_c)
    grad_attn_low = (gate_attn * grad_attn).astype(jnp.bfloat16)
    dgate_attn = jnp.sum(grad_attn * attn_out, axis=1)
    grad_attnout = outer_sum(attn_mixed, grad_attn_low)
    grad_amixed = (
        matmul_t(grad_attn_low, attn_w)
        .astype(jnp.bfloat16)
        .reshape(rows_here, frames_here, HEADS, HEAD_DIM)
    )
    grad_query, key_part, value_part = lax.map(
        self_backward, (queries, key_rows, value_rows, grad_amixed, log_total, local_ids, all_ids)
    )
    grad_key, grad_value = (
        lax.psum_scatter(
            key_part.astype(jnp.bfloat16), "seq", scatter_dimension=1, tiled=True
        ).astype(jnp.float32),
        lax.psum_scatter(
            value_part.astype(jnp.bfloat16), "seq", scatter_dimension=1, tiled=True
        ).astype(jnp.float32),
    )
    grad_projected = jnp.concatenate(
        [
            rotate(grad_query, cosine, -sine_table).reshape(rows_here, frames_here, D),
            rotate(grad_key, cosine, -sine_table).reshape(rows_here, frames_here, D),
            grad_value.reshape(rows_here, frames_here, D),
        ],
        axis=-1,
    ).astype(jnp.bfloat16)
    grad_qkv = outer_sum(attn_in, grad_projected)
    grad_attn_in = matmul_t(grad_projected, qkv_w)
    dshift_attn = jnp.sum(grad_attn_in, axis=1)
    dscale_attn = jnp.sum(grad_attn_in * normed_a, axis=1)
    grad_frames = grad_attn + norm_back(grad_attn_in * (1.0 + scale_attn), normed_a, inv_a)
    grad_rows = jnp.concatenate(
        [dshift_attn, dscale_attn, dgate_attn, dshift_ffn, dscale_ffn, dgate_ffn], axis=-1
    )
    grad_modul = jnp.dot(token_act.astype(jnp.float32).T, grad_rows, precision=highest)
    grad_token = jnp.dot(grad_rows, modul.astype(jnp.float32).T, precision=highest) * silu_slope(
        time_token
    )
    grad_timeout = jnp.dot(time_hidden.astype(jnp.float32).T, grad_token, precision=highest)
    grad_pre = jnp.dot(grad_token, time_out.astype(jnp.float32).T, precision=highest) * silu_slope(
        pre_hidden
    )
    grad_timein = jnp.dot(features.astype(jnp.float32).T, grad_pre, precision=highest)
    rest_grads = (
        lax.psum_scatter(grad_timein, ("row", "seq"), scatter_dimension=0, tiled=True),
        lax.psum_scatter(grad_timeout, ("row", "seq"), scatter_dimension=0, tiled=True),
        lax.psum_scatter(grad_modul, ("row", "seq"), scatter_dimension=0, tiled=True),
        lax.psum_scatter(grad_qkv, ("row", "seq"), scatter_dimension=0, tiled=True),
        lax.psum_scatter(grad_attnout, ("row", "seq"), scatter_dimension=0, tiled=True),
        lax.psum_scatter(grad_gain, ("row", "seq"), scatter_dimension=0, tiled=True),
        lax.psum_scatter(grad_crossq, ("row", "seq"), scatter_dimension=0, tiled=True),
        lax.psum_scatter(grad_crosskv, ("row", "seq"), scatter_dimension=0, tiled=True),
        lax.psum_scatter(grad_crossout, ("row", "seq"), scatter_dimension=0, tiled=True),
    )
    shard_timein, shard_timeout, shard_modul = (rest_grads[0], rest_grads[1], rest_grads[2])
    block_grads = rest_grads[3:]
    return (
        result,
        grad_frames,
        shard_timein,
        shard_timeout,
        shard_modul,
        block_grads[0],
        block_grads[1],
        block_grads[2],
        block_grads[3],
        block_grads[4],
        block_grads[5],
        ffn_grads[0],
        ffn_grads[1],
    )


def can_split(rows, seqs):
    power = lambda n: n & (n - 1) == 0
    return (
        power(rows)
        and power(seqs)
        and HEADS % (2 * seqs) == 0
        and D % (rows * seqs) == 0
        and FF % (rows * seqs) == 0
        and LENGTH % (seqs * 512) == 0
    )


def on_device_split(
    rows,
    seqs,
    frames,
    context,
    seg_lengths,
    bucket_ids,
    timesteps,
    bucket_weights,
    w_time_in,
    w_time_out,
    w_mod,
    w_qkv,
    w_attn_out,
    cross_gain,
    w_cross_q,
    w_cross_kv,
    w_cross_out,
    w_glu,
    w_down,
    cotangent,
):
    my_row = lax.axis_index("row")
    row_order = my_row ^ jnp.arange(rows, dtype=jnp.int32)
    hits = jnp.arange(BUCKETS, dtype=jnp.int32)[:, None] == bucket_ids[row_order][None, :]
    hits = hits.astype(jnp.float32)
    my_seq = lax.axis_index("seq")
    flat = my_row * seqs + my_seq
    sizes = {"row": rows, "seq": seqs}

    def swap(value, axis, j):
        return lax.ppermute(value, axis, [(i, i ^ j) for i in range(sizes[axis])])

    def sum_over(value, axis):
        j = 1
        while j < sizes[axis]:
            value = value + swap(value, axis, j)
            j *= 2
        return value

    def sum_all(value):
        return sum_over(sum_over(value, "seq"), "row")

    def pick(stack, axis_name, j, dim=0):
        me = my_row if axis_name == "row" else my_seq
        return lax.dynamic_index_in_dim(stack, me ^ j, dim, keepdims=False)

    def natural(slots, axis_name="seq"):
        stack = jnp.stack(slots)
        return jnp.stack([pick(stack, axis_name, t) for t in range(len(slots))])

    def exchange_lines(stack, dim):
        pieces = [
            lax.dynamic_index_in_dim(stack, (my_row // 2) ^ j, dim, keepdims=False)
            for j in range(rows // 2)
        ]
        return [pieces[0]] + [swap(p, "row", 2 * j) for j, p in enumerate(pieces) if j]

    def exchange(stack, dim=0, axis_name="seq"):
        pieces = [pick(stack, axis_name, j, dim) for j in range(sizes[axis_name])]
        return [pieces[0]] + [swap(p, axis_name, j) for j, p in enumerate(pieces) if j]

    def spread(value, axis_name="seq"):
        return [value] + [swap(value, axis_name, j) for j in range(1, sizes[axis_name])]

    def after(value, *others):
        return lax.optimization_barrier((value,) + others)[0]

    def spread_two(value):
        if seqs != 4:
            return spread(value), None
        near = [swap(value, "seq", 1), swap(value, "seq", 2)]
        return [value] + near, near

    def opposite(near):
        half = near[0].shape[0] // 2
        return jnp.concatenate([swap(near[1][:half], "seq", 1), swap(near[0][half:], "seq", 2)])

    def spread_row(value):
        both = jnp.stack([value, swap(value, "row", 1)])
        lines = [both] + [swap(both, "row", 2 * j) for j in range(1, rows // 2)]
        return [line[c] for line in lines for c in range(2)]

    def columns(values, axis_name, j, width, start=0):
        me = my_row if axis_name == "row" else my_seq
        return lax.dynamic_slice_in_dim(values, start + (me ^ j) * width, width, 1)

    def side_by_side(slots):
        stack = jnp.stack(slots)
        return jnp.concatenate([pick(stack, "seq", t) for t in range(seqs)], axis=1)

    def mine(values, width):
        return lax.dynamic_slice_in_dim(values, flat * width, width, values.ndim - 1)

    def dot(left, right):
        return jnp.dot(left, right, preferred_element_type=jnp.float32)

    def dot_right_t(left, right):
        return jnp.einsum("fj,ij->fi", left, right, preferred_element_type=jnp.float32)

    def dot_left_t(left, right):
        return jnp.einsum("fi,fj->ij", left, right, preferred_element_type=jnp.float32)

    low = jnp.bfloat16
    frames_here = frames.shape[1]
    text_len, ctx_dim = context.shape[1:]
    local_heads = D // seqs
    depth = w_qkv.shape[0]
    part = FF // (rows * seqs)
    x_own = frames[0]

    kv_width = 2 * D // seqs
    first_pieces = [
        jnp.concatenate(
            [columns(w_qkv, "seq", j, local_heads, k * D) for k in range(3)]
            + [
                jnp.concatenate(
                    [
                        columns(w_cross_kv, "seq", j, kv_width)[:, : kv_width // 2],
                        columns(w_cross_kv, "seq", j, kv_width)[:, kv_width // 2 :],
                    ]
                )
            ],
            axis=1,
        )
        for j in range(seqs)
    ]
    first_slots = [first_pieces[0]] + [swap(p, "seq", j) for j, p in enumerate(first_pieces) if j]
    first_w = natural(first_slots).reshape(seqs * depth, -1)
    first_w = jnp.concatenate([first_w, w_down])
    first_w = lax.all_gather(first_w, "row", axis=0, tiled=True).reshape(rows, -1, D)
    kv_w = first_w[:, : seqs * depth, 3 * local_heads :].reshape(rows * seqs, 2, depth // 2, -1)
    kv_w = jnp.concatenate([kv_w[:, h].reshape(ctx_dim, -1) for h in range(2)], axis=1)

    features = time_features(timesteps.astype(jnp.float32)).astype(low)
    pre_part = dot(mine(features, w_time_in.shape[0]), w_time_in)
    gain_part = lax.dynamic_update_slice(
        jnp.zeros((1, D), jnp.float32), cross_gain.astype(jnp.float32)[None], (0, flat * depth)
    )
    pre_hidden = sum_over(after(jnp.concatenate([pre_part, gain_part]), *first_slots), "seq")
    x_slots, near = spread_two(after(x_own, pre_hidden))
    pre_hidden = sum_over(pre_hidden, "row")
    gain_values = pre_hidden[BUCKETS:]
    pre_hidden = pre_hidden[:BUCKETS]
    time_hidden = jax.nn.silu(pre_hidden).astype(low)
    time_token = sum_over(dot(mine(time_hidden, depth), w_time_out), "row")
    if near is not None:
        time_token, *near = lax.optimization_barrier((time_token, *near))
    wide_w = jnp.concatenate([w_attn_out, w_cross_q, w_cross_out], axis=1)
    wide_w = lax.all_gather(after(wide_w, time_token), ("row", "seq"), axis=0, tiled=True)
    attn_w, crossq_w, crossout_w = wide_w[:, :D], wide_w[:, D : 2 * D], wide_w[:, 2 * D :]
    time_token = sum_over(time_token, "seq")
    if near is not None:
        time_token, *near = lax.optimization_barrier((time_token, *near))
        x_slots = [x_own, *near, opposite(near)]
    token_act = jax.nn.silu(time_token).astype(low)
    mod_part = dot(mine(token_act, depth), w_mod)
    mod_part, *x_slots = lax.optimization_barrier((mod_part, *x_slots))
    glu_slots = exchange(split_units(after(w_glu, x_slots[-1]), seqs, part))
    row_part = lambda j: lax.dynamic_index_in_dim(mod_part, bucket_ids[my_row ^ j], 0)
    modulation = row_part(0)
    for j in range(1, rows):
        modulation = modulation + swap(row_part(j), "row", j)
    modulation = sum_over(modulation, "seq")
    shift_attn, scale_attn, gate_attn, shift_ffn, scale_ffn, gate_ffn = jnp.split(modulation, 6, axis=1)

    bounds = jnp.cumsum(seg_lengths[0])
    slot_seq = my_seq ^ jnp.arange(seqs, dtype=jnp.int32)
    positions = (slot_seq[:, None] * frames_here + jnp.arange(frames_here, dtype=jnp.int32)).reshape(-1)
    ids = jnp.sum((positions[:, None] >= bounds[None, :]).astype(jnp.int32), axis=-1)
    lane = jnp.arange(PAIR, dtype=jnp.int32)[None, :]
    same = ids[:, None] == lane
    key_mask = same.astype(low)
    query_mask = jnp.where((lane < seg_lengths.shape[1]) & ~same, -1e30, 0.0).astype(low)
    half_dim = HEAD_DIM // 2
    inverse = jnp.exp(-math.log(10000.0) * jnp.arange(half_dim, dtype=jnp.float32) / half_dim)
    angles = positions.astype(jnp.float32)[:, None] * inverse[None, :]
    cosine = jnp.tile(jnp.cos(angles), (1, PAIR // half_dim))
    sine = jnp.tile(jnp.concatenate([-jnp.sin(angles), jnp.sin(angles)], axis=1), (1, 2))
    masks, tables = (query_mask, key_mask), (cosine, sine)

    pairs = local_heads // PAIR
    slots = lambda values: values.reshape(seqs, frames_here, -1)
    attn_in, qkv = project(x_slots, 1.0 + scale_attn, shift_attn, first_w, 3 * local_heads, cosine, sine)
    row_scale = lax.dynamic_index_in_dim(bucket_weights, bucket_ids[my_row], 0)
    grad_out = cotangent[0].astype(jnp.float32) * row_scale
    kv_slots = spread(dot(context[0], kv_w).astype(low))
    qkv, *got = lax.optimization_barrier((qkv, *kv_slots, *glu_slots))
    kv_slots, glu_slots = got[:seqs], got[seqs:]
    glu_w = lax.all_gather(natural(glu_slots).reshape(seqs * depth, -1), "row", axis=0, tiled=True)
    mixed_heads, lse = attend(qkv, qkv, qkv, 0, pairs, 2 * pairs, pairs, 512, masks)
    mixed_slots = slots(mixed_heads)
    mixed_got = [mixed_slots[0]] + [swap(mixed_slots[j], "seq", j) for j in range(1, seqs)]
    attn_mixed = side_by_side(mixed_got)
    attn_out = dot(attn_mixed, attn_w)
    cot_slots, _ = spread_two(after(cotangent[0], attn_out))
    inputs = x_own.astype(jnp.float32)
    after_attn = inputs + gate_attn * attn_out

    normed_c, inv_c = layer_stats(after_attn)
    cross_in = (normed_c * gain_values).astype(low)
    cross_q = dot(cross_in, crossq_w).astype(low)
    cross_kv = side_by_side(kv_slots)
    all_pairs = D // PAIR
    cross_mixed, cross_lse = attend(cross_q, cross_kv, cross_kv, 0, 0, all_pairs, all_pairs, frames_here)
    after_cross = after_attn + dot(cross_mixed, crossout_w)

    normed_f, inv_f = layer_stats(after_cross)
    ffn_in = (normed_f * (1.0 + scale_ffn) + shift_ffn).astype(low)
    units = FF // seqs
    ffn_slots, near = spread_two(ffn_in)
    calls = [slice(0, 1), slice(1, 3), slice(3, 4)] if seqs == 4 else [slice(0, seqs)]
    kept, ffn_back, ffn_parts, dgate_ffn = None, [], [], 0.0
    scale_row = jnp.broadcast_to(row_scale[None], (1, D))
    for call in calls:
        if call.start == 1:
            near, kept = lax.optimization_barrier((near, kept))
            cot_near, near = lax.optimization_barrier((cot_slots[1:], near))
            ffn_slots = [ffn_in, *near, opposite(near)]
            cot_slots = [*cot_slots, opposite(cot_near)]
        *kept, back, out, dgate = feed(
            ffn_slots[call], cot_slots[call], gate_ffn, scale_row, glu_w, first_w, call.start, seqs, kept
        )
        dgate_ffn = dgate_ffn + dgate
        ffn_back += [back[i : i + frames_here] for i in range(0, back.shape[0], frames_here)]
        ffn_parts += [out[i : i + frames_here] for i in range(0, out.shape[0], frames_here)]
    ffn_all, grad_ffn_all, hidden_all, grad_gate_up = kept

    def returned_near(parts):
        if seqs != 4:
            return [parts[0]] + [swap(parts[j], "seq", j) for j in range(1, seqs)]
        half = frames_here // 2
        return [
            swap(parts[3][:half], "seq", 1),
            swap(parts[3][half:], "seq", 2),
            swap(parts[1][:half], "seq", 1),
            swap(parts[2][half:], "seq", 2),
        ]

    def returned_far(parts, near):
        if seqs != 4:
            return near[1:], near[:1]
        half = frames_here // 2
        both = lambda left, right: left.astype(jnp.float32) + right.astype(jnp.float32)
        far = [
            swap(both(parts[2][:half], near[0]).astype(low), "seq", 2),
            swap(both(parts[1][half:], near[1]).astype(low), "seq", 1),
        ]
        return far, [both(parts[0][:half], near[2]), both(parts[0][half:], near[3])]

    def returned_total(far, near):
        if seqs != 4:
            return sum(term.astype(jnp.float32) for term in near + far)
        return jnp.concatenate([n + f.astype(jnp.float32) for n, f in zip(near, far)])

    ffn_back_near = returned_near(ffn_back)
    grad_glu = dot_left_t(ffn_all, grad_gate_up).astype(low)
    grad_down = dot_left_t(hidden_all, grad_ffn_all).astype(low)
    grad_glu, *ffn_back_near = lax.optimization_barrier((grad_glu, *ffn_back_near))
    ffn_back_far = returned_far(ffn_back, ffn_back_near)
    grad_ffn_in, grad_glu, grad_down, *ffn_parts = lax.optimization_barrier(
        (returned_total(*ffn_back_far), grad_glu, grad_down, *ffn_parts)
    )
    grad_glu = lax.psum_scatter(grad_glu, "row", scatter_dimension=0, tiled=True)
    grad_down = lax.psum_scatter(grad_down, "row", scatter_dimension=0, tiled=True)
    ffn_near = returned_near(ffn_parts)
    dshift_ffn = jnp.sum(grad_ffn_in, axis=0, keepdims=True)
    dscale_ffn = jnp.sum(grad_ffn_in * normed_f, axis=0, keepdims=True)
    grad_cross = grad_out + norm_back(grad_ffn_in * (1.0 + scale_ffn), normed_f, inv_f)

    grad_cross_low = grad_cross.astype(low)
    grad_cmixed = dot_right_t(grad_cross_low, crossout_w).astype(low)
    grad_cquery, grad_ckey, grad_cvalue = attend_back(
        cross_q, cross_kv, cross_kv, grad_cmixed, cross_mixed, cross_lse,
        0, 0, all_pairs, all_pairs, frames_here, text_len,
    )
    grad_cquery, *ffn_near = lax.optimization_barrier((grad_cquery, *ffn_near))
    grad_cross_in = dot_right_t(grad_cquery, crossq_w)
    grad_gain = jnp.sum(grad_cross_in * normed_c, axis=0, keepdims=True)
    grad_attn = grad_cross + norm_back(grad_cross_in * gain_values, normed_c, inv_c)

    grad_attn_low = (gate_attn * grad_attn).astype(low)
    dgate_attn = jnp.sum(grad_attn * attn_out, axis=0, keepdims=True)
    grad_amixed = dot_right_t(grad_attn_low, attn_w).astype(low)
    head_pieces = [columns(grad_amixed, "seq", j, local_heads) for j in range(seqs)]
    head_pieces = [head_pieces[0]] + [swap(p, "seq", j) for j, p in enumerate(head_pieces) if j]
    wide_left = [cross_mixed, cross_in, attn_mixed]
    for j in range(1, min(seqs, 4)):
        wide_left[j - 1], head_pieces[j] = lax.optimization_barrier((wide_left[j - 1], head_pieces[j]))
    cross_mixed, cross_in, attn_mixed = wide_left
    grad_heads = jnp.concatenate(head_pieces)

    core = my_row % 2
    wide_own = [
        dot_left_t(left, right).astype(low).reshape(rows // 2, 2, seqs, depth, D)
        for left, right in (
            (attn_mixed, grad_attn_low),
            (cross_in, grad_cquery),
            (cross_mixed, grad_cross_low),
        )
    ]
    half_of = lambda g, c: lax.dynamic_index_in_dim(g, c, 1, keepdims=False)
    wide_got = [swap(half_of(g, 1 - core), "row", 1) for g in wide_own]

    grad_ckv = jnp.concatenate([grad_ckey, grad_cvalue], axis=1).astype(low)
    grad_kv = text_product(context[0], grad_ckv)
    grad_heads, grad_kv, grad_down, *wide_got = lax.optimization_barrier(
        (grad_heads, grad_kv, grad_down, *wide_got)
    )
    grad_kv = lax.psum_scatter(grad_kv, "row", scatter_dimension=0, tiled=True)
    ffn_far, ffn_near = returned_far(ffn_parts, ffn_near)
    wide_both = [(half_of(own, core), got) for own, got in zip(wide_own, wide_got)]

    def wide_piece(j):
        both = [
            pick(own, "seq", j, 1).astype(jnp.float32) + pick(got, "seq", j, 1).astype(jnp.float32)
            for own, got in wide_both
        ]
        return jnp.stack(both, axis=1).astype(low)

    wide_got = [wide_piece(j) for j in range(seqs)]
    wide_got = [wide_got[0]] + [swap(piece, "seq", j) for j, piece in enumerate(wide_got) if j]
    grad_projected = jnp.concatenate(
        attend_back(
            qkv, qkv, qkv, grad_heads, mixed_heads, lse,
            0, pairs, 2 * pairs, pairs, 512, 512, masks, tables,
        ),
        axis=1,
    )
    grad_projected, grad_glu, wide_got, ffn_far = lax.optimization_barrier(
        (grad_projected, grad_glu, wide_got, ffn_far)
    )
    glu_got = exchange(after(grad_glu, grad_projected).reshape(seqs, depth, -1))
    grad_qkv = dot_left_t(attn_in, grad_projected).astype(low)
    grad_projected, grad_qkv = lax.optimization_barrier((grad_projected, grad_qkv))
    grad_qkv = lax.psum_scatter(grad_qkv, "row", scatter_dimension=0, tiled=True)
    attn_back, attn_sums = project_back(grad_projected, first_w, x_slots)
    attn_sums, attn_back, grad_down, grad_kv, glu_got = lax.optimization_barrier(
        (attn_sums, attn_back, grad_down, grad_kv, glu_got)
    )
    own_sums = jnp.concatenate([attn_sums, dgate_attn, dshift_ffn, dscale_ffn, dgate_ffn, grad_gain])
    own_sums = sum_over(own_sums, "seq")
    own_sums, attn_back = lax.optimization_barrier((own_sums, attn_back))
    attn_back = slots(attn_back)
    attn_near = returned_near(attn_back)

    sums_list, attn_near, grad_qkv = lax.optimization_barrier(
        (spread_row(own_sums), attn_near, grad_qkv)
    )
    wide = sum(g.astype(jnp.float32) for g in after(tuple(wide_got), grad_qkv)).astype(low)
    grad_wide = lax.psum_scatter(
        wide,
        "row",
        scatter_dimension=0,
        axis_index_groups=[list(range(c, rows, 2)) for c in range(2)],
        tiled=True,
    )[0].astype(jnp.float32)
    total = sum(hits[:, j, None, None] * sums for j, sums in enumerate(sums_list))
    grad_mods = total[:, :6].reshape(BUCKETS, 6 * D)
    gain_total = jnp.sum(total[:, 6], axis=0)

    def gather_row(slots):
        return natural(slots, "row").transpose(1, 0, 2).reshape(BUCKETS, -1)

    def gather_seq(own):
        return natural(spread(own)).transpose(1, 0, 2).reshape(BUCKETS, -1)

    grad_modul = outer(mine(token_act, depth).astype(jnp.float32), grad_mods)
    token_own = jnp.dot(grad_mods, w_mod.astype(jnp.float32).T, precision=highest)
    token_own = token_own * silu_slope(mine(time_token, depth))
    token_seq = gather_seq(token_own)
    token_seq, *attn_near = lax.optimization_barrier((token_seq, *attn_near))
    attn_far, attn_own = returned_far(attn_back, attn_near)
    token_slots, attn_far = lax.optimization_barrier((spread_row(token_seq), attn_far))
    result = (after_cross + gate_ffn * returned_total(ffn_far, ffn_near)).astype(low)
    grad_token = gather_row(token_slots)
    grad_timeout = outer(mine(time_hidden, depth).astype(jnp.float32), grad_token)
    hidden_own = jnp.dot(grad_token, w_time_out.astype(jnp.float32).T, precision=highest)
    hidden_own = hidden_own * silu_slope(mine(pre_hidden, depth))
    grad_attn_in = returned_total(attn_far, attn_own)
    kv_stack = grad_kv.reshape(seqs, depth // 2, 2 * D)
    kv_stack = jnp.concatenate([kv_stack[..., :D], kv_stack[..., D:]], axis=1)
    qkv_stack = jnp.concatenate([grad_qkv.reshape(seqs, depth, -1), kv_stack], axis=2)
    qkv_stack, hidden_own = lax.optimization_barrier((qkv_stack, hidden_own))
    qkv_got = exchange(qkv_stack)
    hidden_seq, *qkv_got = lax.optimization_barrier((gather_seq(hidden_own), *qkv_got))
    grad_pre = gather_row(spread_row(hidden_seq))
    grad_timein = outer(mine(features, w_time_in.shape[0]).astype(jnp.float32), grad_pre)
    normed_a, inv_a = layer_stats(inputs)
    grad_frames = grad_attn + norm_back(grad_attn_in * (1.0 + scale_attn), normed_a, inv_a)

    qkv_list = qkv_got
    qkv_got = jnp.stack(qkv_got)
    grad_qkv = jnp.concatenate(
        [
            pick(qkv_got, "seq", t)[:, k * local_heads : (k + 1) * local_heads]
            for k in range(3)
            for t in range(seqs)
        ],
        axis=1,
    )
    grad_glu = join_units(natural(glu_got), part)
    grad_crosskv = sum(piece[:, 3 * local_heads :].astype(jnp.float32) for piece in qkv_list)
    grad_crosskv = jnp.concatenate([grad_crosskv[: depth // 2], grad_crosskv[depth // 2 :]], axis=1)

    return (
        result[None],
        grad_frames[None],
        grad_timein,
        grad_timeout,
        grad_modul,
        grad_qkv.astype(jnp.float32),
        grad_wide[0],
        mine(gain_total, depth),
        grad_wide[1],
        grad_crosskv,
        grad_wide[2],
        grad_glu,
        grad_down.astype(jnp.float32),
    )


def solution(mesh):
    placed = (
        P("row", "seq", None),
        P("row", None, None),
        P("row", None),
        P(),
        P(),
        P(),
        P(("row", "seq"), None),
        P(("row", "seq"), None),
        P(("row", "seq"), None),
        P(("row", "seq"), None),
        P(("row", "seq"), None),
        P(("row", "seq")),
        P(("row", "seq"), None),
        P(("row", "seq"), None),
        P(("row", "seq"), None),
        P(("row", "seq"), None),
        P(("row", "seq"), None),
        P("row", "seq", None),
    )
    rows, seqs = mesh.shape["row"], mesh.shape["seq"]
    plan = functools.partial(on_device_split, rows, seqs) if can_split(rows, seqs) else on_device
    return jax.shard_map(
        plan,
        mesh=mesh,
        in_specs=placed,
        out_specs=(
            P("row", "seq", None),
            P("row", "seq", None),
            P(("row", "seq"), None),
            P(("row", "seq"), None),
            P(("row", "seq"), None),
            P(("row", "seq"), None),
            P(("row", "seq"), None),
            P(("row", "seq")),
            P(("row", "seq"), None),
            P(("row", "seq"), None),
            P(("row", "seq"), None),
            P(("row", "seq"), None),
            P(("row", "seq"), None),
        ),
        check_vma=False,
    )
```

```python
import functools
import math

import jax
import jax.numpy as jnp
from jax import lax
from jax.experimental import pallas as pl
from jax.experimental.pallas import tpu as pltpu
from jax.sharding import PartitionSpec as P

D = 1536
HEADS = 24
HEAD_DIM = 64
FF = 6144
TFREQ = 256
LENGTH = 2048
BUCKETS = 5
PAIR = 2 * HEAD_DIM
VMEM = 50 * 1024 * 1024
f32 = jnp.float32
bf16 = jnp.bfloat16


def dot_nt(left, right):
    return lax.dot_general(left, right, (((1,), (1,)), ((), ())), preferred_element_type=f32)


def dot_nn(left, right):
    return lax.dot_general(left, right, (((1,), (0,)), ((), ())), preferred_element_type=f32)


def swap_halves(values):
    lane = lax.broadcasted_iota(jnp.int32, values.shape, 1)
    ahead = pltpu.roll(values, PAIR - HEAD_DIM // 2, 1)
    behind = pltpu.roll(values, HEAD_DIM // 2, 1)
    return jnp.where((lane & (HEAD_DIM // 2)) == 0, ahead, behind)


def head_lanes(values, head):
    lane = lax.broadcasted_iota(jnp.int32, values.shape, 1)
    return jnp.where((lane // HEAD_DIM) == head, values, 0.0)


def norm_block(x_ref):
    values = x_ref[...].astype(f32)
    center = values - jnp.mean(values, axis=-1, keepdims=True)
    return center * lax.rsqrt(jnp.mean(center * center, axis=-1, keepdims=True) + 1e-05)


def joined(blocks):
    return blocks.reshape(blocks.shape[0] * blocks.shape[1], blocks.shape[2])


def gathered_spec(w, part, rows, width, **kwargs):
    return pl.BlockSpec((w.shape[0], rows, width), lambda i: (0, part, 0), **kwargs)


def project_kernel(per_slot, *refs):
    x_refs, (scale_ref, shift_ref, w_ref, cos_ref, sin_ref, in_ref, out_ref) = refs[:-7], refs[-7:]

    def run(x_ref):
        modulated = (norm_block(x_ref) * scale_ref[...] + shift_ref[...]).astype(bf16)
        in_ref[...] = modulated
        projected = dot_nn(modulated, joined(w_ref[...]))
        cosine = cos_ref[...]
        sine = sin_ref[...]
        width = out_ref.shape[1]
        for start in range(0, width, PAIR):
            part = projected[:, start : start + PAIR]
            if start < 2 * width // 3:
                part = part * cosine + swap_halves(part) * sine
            out_ref[:, start : start + PAIR] = part.astype(bf16)

    for slot, x_ref in enumerate(x_refs):
        pl.when(pl.program_id(0) // per_slot == slot)(functools.partial(run, x_ref))


def slot_specs(x_slots, block):
    per_slot, depth = x_slots[0].shape[0] // block, x_slots[0].shape[1]

    def one(slot):
        return pl.BlockSpec((block, depth), lambda i: (jnp.clip(i - slot * per_slot, 0, per_slot - 1), 0))

    return per_slot, [one(slot) for slot in range(len(x_slots))]


def project(x_slots, scale, shift, w, width, cosine, sine, block=256):
    per_slot, x_specs = slot_specs(x_slots, block)
    depth = x_slots[0].shape[1]
    count = len(x_slots) * x_slots[0].shape[0]
    row_spec = lambda cols: pl.BlockSpec((block, cols), lambda i: (i, 0))
    whole = lambda a: pl.BlockSpec(a.shape, lambda i: (0, 0))

    return pl.pallas_call(
        functools.partial(project_kernel, per_slot),
        grid=(count // block,),
        in_specs=x_specs
        + [
            whole(scale),
            whole(shift),
            gathered_spec(w, 0, depth // w.shape[0], width),
            row_spec(PAIR),
            row_spec(PAIR),
        ],
        out_specs=[row_spec(depth), row_spec(width)],
        out_shape=[
            jax.ShapeDtypeStruct((count, depth), bf16),
            jax.ShapeDtypeStruct((count, width), bf16),
        ],
        compiler_params=pltpu.CompilerParams(vmem_limit_bytes=VMEM),
        cost_estimate=pl.CostEstimate(
            flops=2 * count * depth * width,
            bytes_accessed=2 * (2 * count * depth + depth * width + count * width),
            transcendentals=count,
        ),
        name="project",
    )(*x_slots, scale, shift, w, cosine, sine)


def project_back_kernel(per_slot, *refs):
    x_refs, (grad_ref, w_ref, out_ref, sums_ref) = refs[:-4], refs[-4:]

    @pl.when(pl.program_id(0) == 0)
    def _():
        sums_ref[...] = jnp.zeros_like(sums_ref)

    def run(x_ref):
        part = dot_nt(grad_ref[...], joined(w_ref[...]))
        out_ref[...] = part.astype(bf16)
        sums_ref[0:1, :] += jnp.sum(part, axis=0, keepdims=True)
        sums_ref[1:2, :] += jnp.sum(part * norm_block(x_ref), axis=0, keepdims=True)

    for slot, x_ref in enumerate(x_refs):
        pl.when(pl.program_id(0) // per_slot == slot)(functools.partial(run, x_ref))


def project_back(grad, w, x_slots, block=256):
    per_slot, x_specs = slot_specs(x_slots, block)
    count, width = grad.shape
    depth = x_slots[0].shape[1]
    return pl.pallas_call(
        functools.partial(project_back_kernel, per_slot),
        grid=(count // block,),
        in_specs=x_specs
        + [
            pl.BlockSpec((block, width), lambda i: (i, 0)),
            gathered_spec(w, 0, depth // w.shape[0], width),
        ],
        out_specs=[
            pl.BlockSpec((block, depth), lambda i: (i, 0)),
            pl.BlockSpec((2, depth), lambda i: (0, 0)),
        ],
        out_shape=[
            jax.ShapeDtypeStruct((count, depth), bf16),
            jax.ShapeDtypeStruct((2, depth), f32),
        ],
        compiler_params=pltpu.CompilerParams(vmem_limit_bytes=VMEM),
        cost_estimate=pl.CostEstimate(
            flops=2 * count * depth * width,
            bytes_accessed=2 * (2 * count * depth + depth * width + count * width),
            transcendentals=count,
        ),
        name="project_back",
    )(*x_slots, grad, w)


def attend_kernel(masked, *refs):
    if masked:
        q_ref, k_ref, v_ref, qmask_ref, kmask_ref, o_ref, lse_ref, keys, values_t = refs
    else:
        q_ref, k_ref, v_ref, o_ref, lse_ref, keys, values_t = refs

    @pl.when(pl.program_id(1) == 0)
    def _():
        keys[:, :PAIR] = k_ref[...]
        if masked:
            keys[:, PAIR:] = kmask_ref[...]
        values_t[...] = v_ref[...].astype(f32).T.astype(bf16)

    queries = q_ref[...].astype(f32) * 0.125
    mixed = []
    for head in range(2):
        query = head_lanes(queries, head).astype(bf16)
        if masked:
            query = jnp.concatenate([query, qmask_ref[...]], axis=1)
        scores = dot_nt(keys[...], query)
        top = jnp.max(scores, axis=0, keepdims=True)
        shifted = jnp.exp(scores - top)
        total = jnp.sum(shifted, axis=0, keepdims=True)
        own = values_t[head * HEAD_DIM : (head + 1) * HEAD_DIM, :]
        mixed.append(dot_nn(own, shifted.astype(bf16)) / total)
        lse_ref[0, head : head + 1, :] = top + jnp.log(total)
    o_ref[...] = jnp.concatenate(mixed, axis=0).T.astype(bf16)


def attend(q, k, v, q_col, k_col, v_col, pairs, block, masks=None):
    count, keys = q.shape[0], k.shape[0]
    masked = masks is not None
    in_specs = [
        pl.BlockSpec((block, PAIR), lambda p, i: (i, q_col + p)),
        pl.BlockSpec((keys, PAIR), lambda p, i: (0, k_col + p)),
        pl.BlockSpec((keys, PAIR), lambda p, i: (0, v_col + p)),
    ]
    if masked:
        in_specs += [
            pl.BlockSpec((block, PAIR), lambda p, i: (i, 0)),
            pl.BlockSpec((keys, PAIR), lambda p, i: (0, 0)),
        ]
    return pl.pallas_call(
        functools.partial(attend_kernel, masked),
        grid=(pairs, count // block),
        in_specs=in_specs,
        out_specs=[
            pl.BlockSpec((block, PAIR), lambda p, i: (i, p)),
            pl.BlockSpec((1, 2, block), lambda p, i: (p, 0, i)),
        ],
        out_shape=[
            jax.ShapeDtypeStruct((count, pairs * PAIR), bf16),
            jax.ShapeDtypeStruct((pairs, 2, count), f32),
        ],
        scratch_shapes=[
            pltpu.VMEM((keys, (2 if masked else 1) * PAIR), bf16),
            pltpu.VMEM((PAIR, keys), bf16),
        ],
        compiler_params=pltpu.CompilerParams(vmem_limit_bytes=VMEM),
        cost_estimate=pl.CostEstimate(
            flops=16 * pairs * PAIR * count * keys,
            bytes_accessed=2 * pairs * PAIR * (2 * count + 2 * keys),
            transcendentals=2 * pairs * count * keys,
        ),
        name="attend",
    )(q, k, v, *(masks or ()))


def attend_back_kernel(masked, chunk, *refs):
    if masked:
        (q_ref, k_ref, v_ref, do_ref, o_ref, lse_ref, qmask_ref, kmask_ref, qcos_ref, qsin_ref,
         kcos_ref, ksin_ref, dq_ref, dk_ref, dv_ref, keys, keys_t, dk_sum, dv_sum) = refs
    else:
        (q_ref, k_ref, v_ref, do_ref, o_ref, lse_ref,
         dq_ref, dk_ref, dv_ref, keys, keys_t, dk_sum, dv_sum) = refs
    step = pl.program_id(1)
    count = k_ref.shape[0]

    @pl.when(step == 0)
    def _():
        keys[:, :PAIR] = k_ref[...]
        if masked:
            keys[:, PAIR:] = kmask_ref[...]
        keys_t[...] = k_ref[...].astype(f32).T.astype(bf16)
        dk_sum[...] = jnp.zeros_like(dk_sum)
        dv_sum[...] = jnp.zeros_like(dv_sum)

    queries = q_ref[...].astype(f32) * 0.125
    grads = do_ref[...].astype(f32)
    rows_t = (grads * o_ref[...].astype(f32)).T
    parts = []
    for head in range(2):
        lanes = slice(head * HEAD_DIM, (head + 1) * HEAD_DIM)
        delta = jnp.sum(rows_t[lanes, :], axis=0, keepdims=True)
        log_row = lse_ref[0, head : head + 1, :]
        query = head_lanes(queries, head).astype(bf16)
        grad = head_lanes(grads, head).astype(bf16)
        full = jnp.concatenate([query, qmask_ref[...]], axis=1) if masked else query
        total = None
        for start in range(0, count, chunk):
            here = slice(start, start + chunk)
            soft = jnp.exp(dot_nt(keys[here, :], full) - log_row)
            grad_soft = dot_nt(v_ref[here, :], grad)
            grad_scores = (soft * (grad_soft - delta)).astype(bf16)
            dv_sum[here, :] += dot_nn(soft.astype(bf16), grad)
            dk_sum[here, :] += dot_nn(grad_scores, query)
            part = dot_nn(keys_t[lanes, here], grad_scores)
            total = part if total is None else total + part
        parts.append(total)
    dq = jnp.concatenate(parts, axis=0).T * 0.125
    if masked:
        dq = dq * qcos_ref[...] - swap_halves(dq) * qsin_ref[...]
    dq_ref[...] = dq.astype(dq_ref.dtype)

    @pl.when(step == pl.num_programs(1) - 1)
    def _():
        dk = dk_sum[...]
        if masked:
            dk = dk * kcos_ref[...] - swap_halves(dk) * ksin_ref[...]
        dk_ref[...] = dk.astype(dk_ref.dtype)
        dv_ref[...] = dv_sum[...].astype(dv_ref.dtype)


def attend_back(q, k, v, do, o, lse, q_col, k_col, v_col, pairs, block, chunk, masks=None, tables=None):
    count, keys = q.shape[0], k.shape[0]
    masked = masks is not None
    out_type = bf16 if masked else f32
    rows = lambda col: pl.BlockSpec((block, PAIR), lambda p, i: (i, col + p))
    whole = lambda col: pl.BlockSpec((keys, PAIR), lambda p, i: (0, col + p))
    in_specs = [
        rows(q_col), whole(k_col), whole(v_col), rows(0), rows(0),
        pl.BlockSpec((1, 2, block), lambda p, i: (p, 0, i)),
    ]
    operands = [q, k, v, do, o, lse]
    if masked:
        rows_fixed = pl.BlockSpec((block, PAIR), lambda p, i: (i, 0))
        whole_fixed = pl.BlockSpec((keys, PAIR), lambda p, i: (0, 0))
        in_specs += [rows_fixed, whole_fixed, rows_fixed, rows_fixed, whole_fixed, whole_fixed]
        operands += [masks[0], masks[1], tables[0], tables[1], tables[0], tables[1]]
    return pl.pallas_call(
        functools.partial(attend_back_kernel, masked, chunk),
        grid=(pairs, count // block),
        in_specs=in_specs,
        out_specs=[rows(0), whole(0), whole(0)],
        out_shape=[
            jax.ShapeDtypeStruct((count, pairs * PAIR), bf16),
            jax.ShapeDtypeStruct((keys, pairs * PAIR), out_type),
            jax.ShapeDtypeStruct((keys, pairs * PAIR), out_type),
        ],
        scratch_shapes=[
            pltpu.VMEM((keys, (2 if masked else 1) * PAIR), bf16),
            pltpu.VMEM((PAIR, keys), bf16),
            pltpu.VMEM((keys, PAIR), f32),
            pltpu.VMEM((keys, PAIR), f32),
        ],
        compiler_params=pltpu.CompilerParams(vmem_limit_bytes=VMEM),
        cost_estimate=pl.CostEstimate(
            flops=40 * pairs * PAIR * count * keys,
            bytes_accessed=2 * pairs * PAIR * (4 * count + 4 * keys),
            transcendentals=2 * pairs * count * keys,
        ),
        name="attend_back",
    )(*operands)
def split_units_kernel(seqs, part, w_ref, out_ref):
    block = seqs * part
    for pair in range(w_ref.shape[1] // (2 * block)):
        groups = [
            w_ref[:, (2 * pair + k) * block : (2 * pair + k + 1) * block].astype(f32) for k in range(2)
        ]
        for t in range(seqs):
            both = [g[:, t * part : (t + 1) * part] for g in groups]
            out_ref[t, :, 2 * pair * part : 2 * (pair + 1) * part] = jnp.concatenate(both, axis=1).astype(bf16)


def split_units(w, seqs, part):
    depth, width = w.shape
    return pl.pallas_call(
        functools.partial(split_units_kernel, seqs, part),
        out_shape=jax.ShapeDtypeStruct((seqs, depth, width // seqs), bf16),
        compiler_params=pltpu.CompilerParams(vmem_limit_bytes=VMEM),
        cost_estimate=pl.CostEstimate(flops=0, bytes_accessed=4 * depth * width, transcendentals=0),
        name="split_units",
    )(w)


def join_units_kernel(seqs, part, in_ref, out_ref):
    block = seqs * part
    for pair in range(out_ref.shape[1] // (2 * block)):
        both = [in_ref[t, :, 2 * pair * part : 2 * (pair + 1) * part].astype(f32) for t in range(seqs)]
        for k in range(2):
            group = [b[:, k * part : (k + 1) * part] for b in both]
            out_ref[:, (2 * pair + k) * block : (2 * pair + k + 1) * block] = jnp.concatenate(group, axis=1)


def join_units(stack, part):
    seqs, depth, width = stack.shape
    return pl.pallas_call(
        functools.partial(join_units_kernel, seqs, part),
        out_shape=jax.ShapeDtypeStruct((depth, width * seqs), f32),
        compiler_params=pltpu.CompilerParams(vmem_limit_bytes=VMEM),
        cost_estimate=pl.CostEstimate(flops=0, bytes_accessed=6 * depth * width * seqs, transcendentals=0),
        name="join_units",
    )(stack)


def feed_kernel(per_slot, slots, chunk, chained, *refs):
    x_refs, g_refs = refs[:slots], refs[slots : 2 * slots]
    gate_ref, scale_ref, glu_ref, down_ref = refs[2 * slots : 2 * slots + 4]
    outs = refs[2 * slots + 4 + (4 if chained else 0) :]
    x_out, g_out, hidden_ref, grads_ref, back_ref, out_ref, dgate_ref, back_sum, out_sum = outs
    blocks, block_units = down_ref.shape[:2]
    units = blocks * block_units
    taken = chunk // block_units

    def run(x_ref, g_ref):
        x = x_ref[...]
        grad_out = g_ref[...].astype(f32) * scale_ref[...]
        g = (gate_ref[...] * grad_out).astype(bf16)
        x_out[...] = x
        g_out[...] = g
        for start in range(0, units, chunk):
            gate_cols, up_cols = slice(start, start + chunk), slice(units + start, units + start + chunk)
            gate = dot_nn(x, glu_ref[:, gate_cols])
            up = dot_nn(x, glu_ref[:, up_cols])
            down = joined(down_ref[start // block_units : start // block_units + taken])
            grad_hidden = dot_nt(g, down)
            opened = 1.0 / (1.0 + jnp.exp(-gate))
            act = gate * opened
            hidden = (act * up).astype(bf16)
            grad_gate = (grad_hidden * up * (opened * (1.0 + gate * (1.0 - opened)))).astype(bf16)
            grad_up = (grad_hidden * act).astype(bf16)
            hidden_ref[:, gate_cols] = hidden
            grads_ref[:, gate_cols] = grad_gate
            grads_ref[:, up_cols] = grad_up
            back = dot_nt(grad_gate, glu_ref[:, gate_cols]) + dot_nt(grad_up, glu_ref[:, up_cols])
            out = dot_nn(hidden, down)
            if start == 0:
                back_sum[...] = back
                out_sum[...] = out
            else:
                back_sum[...] += back
                out_sum[...] += out
        back_ref[...] = back_sum[...].astype(bf16)
        out_ref[...] = out_sum[...].astype(bf16)
        dgate_ref[...] += jnp.sum(grad_out * out_sum[...], axis=0, keepdims=True)

    @pl.when(pl.program_id(0) == 0)
    def _():
        dgate_ref[...] = jnp.zeros_like(dgate_ref)

    for slot in range(slots):
        pl.when(pl.program_id(0) // per_slot == slot)(functools.partial(run, x_refs[slot], g_refs[slot]))


def feed(x_slots, g_slots, gate, scale, glu, down, first, total, kept=None, block=256):
    per_slot, x_specs = slot_specs(x_slots, block)
    slots, (frames, depth) = len(x_slots), x_slots[0].shape
    count, units = slots * frames, glu.shape[1] // 2
    chunk = units // 2
    own_units = units // down.shape[0]
    offset = first * per_slot
    own_rows = lambda cols: pl.BlockSpec((block, cols), lambda i: (i, 0))
    all_rows = lambda cols: pl.BlockSpec((block, cols), lambda i: (i + offset, 0))
    whole = lambda a: pl.BlockSpec(a.shape, lambda i: (0, 0), pipeline_mode=pl.Buffered(1))
    everywhere = [depth, depth, units, 2 * units]
    return pl.pallas_call(
        functools.partial(feed_kernel, per_slot, slots, chunk, kept is not None),
        grid=(count // block,),
        in_specs=x_specs
        + slot_specs(g_slots, block)[1]
        + [
            whole(gate),
            whole(scale),
            whole(glu),
            gathered_spec(
                down, down.shape[1] // own_units - 1, own_units, depth, pipeline_mode=pl.Buffered(1)
            ),
        ]
        + [pl.BlockSpec(memory_space=pl.ANY)] * (4 if kept is not None else 0),
        out_specs=[all_rows(cols) for cols in everywhere] + [own_rows(depth), own_rows(depth), pl.BlockSpec((1, depth), lambda i: (0, 0))],
        out_shape=[jax.ShapeDtypeStruct((total * frames, cols), bf16) for cols in everywhere]
        + [jax.ShapeDtypeStruct((count, depth), bf16)] * 2
        + [jax.ShapeDtypeStruct((1, depth), f32)],
        scratch_shapes=[pltpu.VMEM((block, depth), f32), pltpu.VMEM((block, depth), f32)],
        input_output_aliases={2 * slots + 4 + k: k for k in range(4)} if kept is not None else {},
        compiler_params=pltpu.CompilerParams(vmem_limit_bytes=VMEM),
        cost_estimate=pl.CostEstimate(
            flops=12 * count * depth * units,
            bytes_accessed=2 * (3 * depth * units + count * (6 * depth + 3 * units)),
            transcendentals=count * units,
        ),
        name="feed",
    )(*x_slots, *g_slots, gate, scale, glu, down, *(kept or ()))


def outer_kernel(left_ref, right_ref, out_ref):
    left = left_ref[...].T
    height = out_ref.shape[0]
    total = left[:height, 0:1] * right_ref[0:1, :]
    for b in range(1, right_ref.shape[0]):
        total += left[:height, b : b + 1] * right_ref[b : b + 1, :]
    out_ref[...] = total


def outer(left, right):
    buckets, height = left.shape
    width = right.shape[1]
    left = jnp.pad(left.astype(f32), ((0, -buckets % 8), (0, -height % 128)))
    return pl.pallas_call(
        outer_kernel,
        out_shape=jax.ShapeDtypeStruct((height, width), f32),
        compiler_params=pltpu.CompilerParams(vmem_limit_bytes=VMEM),
        cost_estimate=pl.CostEstimate(
            flops=2 * buckets * height * width, bytes_accessed=4 * height * width, transcendentals=0
        ),
        name="outer",
    )(left, right)


def text_product_kernel(left_ref, right_ref, out_ref):
    left = left_ref[...].astype(f32).T.astype(bf16)
    out_ref[...] = dot_nn(left, right_ref[...]).astype(bf16)


def text_product(left, right, block=1024):
    tokens, height = left.shape
    width = right.shape[1]
    return pl.pallas_call(
        text_product_kernel,
        grid=(width // block,),
        in_specs=[
            pl.BlockSpec((tokens, height), lambda i: (0, 0)),
            pl.BlockSpec((tokens, block), lambda i: (0, i)),
        ],
        out_specs=pl.BlockSpec((height, block), lambda i: (0, i)),
        out_shape=jax.ShapeDtypeStruct((height, width), bf16),
        compiler_params=pltpu.CompilerParams(vmem_limit_bytes=VMEM),
        cost_estimate=pl.CostEstimate(
            flops=2 * tokens * height * width, bytes_accessed=2 * height * width, transcendentals=0
        ),
        name="text_product",
    )(left, right)


highest = lax.Precision.HIGHEST


def matmul(left, right):
    return jnp.einsum("...i,ij->...j", left, right, preferred_element_type=jnp.float32)


def matmul_t(left, right):
    return jnp.einsum("...j,ij->...i", left, right, preferred_element_type=jnp.float32)


def outer_sum(left, right):
    return jnp.einsum("rfi,rfj->ij", left, right, preferred_element_type=jnp.float32)


def layer_stats(values):
    center = values - jnp.mean(values, axis=-1, keepdims=True)
    inv_std = lax.rsqrt(jnp.mean(center * center, axis=-1, keepdims=True) + 1e-05)
    return (center * inv_std, inv_std)


def norm_back(grad_normed, normed, inv_std):
    return inv_std * (
        grad_normed
        - jnp.mean(grad_normed, axis=-1, keepdims=True)
        - normed * jnp.mean(grad_normed * normed, axis=-1, keepdims=True)
    )


def silu_slope(values):
    sigmoid_part = jax.nn.sigmoid(values)
    return sigmoid_part * (1.0 + values * (1.0 - sigmoid_part))


def angle_tables(positions):
    half_dim = HEAD_DIM // 2
    inverse = jnp.exp(-math.log(10000.0) * jnp.arange(half_dim, dtype=jnp.float32) / half_dim)
    angles = positions[:, None] * inverse[None, :]
    return (jnp.cos(angles)[:, None, :], jnp.sin(angles)[:, None, :])


def rotate(values, cosine, sine_table):
    half_dim = values.shape[-1] // 2
    first_half = values[..., :half_dim]
    second_half = values[..., half_dim:]
    return jnp.concatenate(
        [
            first_half * cosine - second_half * sine_table,
            second_half * cosine + first_half * sine_table,
        ],
        axis=-1,
    )


def time_features(times):
    half_dim = TFREQ // 2
    freqs = jnp.exp(-math.log(10000.0) * jnp.arange(half_dim, dtype=jnp.float32) / half_dim)
    angles = times[:, None] * freqs[None, :]
    return jnp.concatenate([jnp.cos(angles), jnp.sin(angles)], axis=-1)


def stamp_rows(times, time_in, time_out, modul):
    features = time_features(times).astype(jnp.bfloat16)
    pre_hidden = jnp.dot(features, time_in, preferred_element_type=jnp.float32)
    time_hidden = jax.nn.silu(pre_hidden).astype(jnp.bfloat16)
    time_token = jnp.dot(time_hidden, time_out, preferred_element_type=jnp.float32)
    token_act = jax.nn.silu(time_token).astype(jnp.bfloat16)
    modulation = jnp.dot(token_act, modul, preferred_element_type=jnp.float32)
    return (features, pre_hidden, time_hidden, time_token, token_act, modulation)


def self_forward(row_inputs):
    query_row, key_row, value_row, local_row, whole_row = row_inputs
    allowed = local_row[:, None] == whole_row[None, :]
    scores = (
        jnp.einsum("qhd,khd->hqk", query_row, key_row, preferred_element_type=jnp.float32) * 0.125
    )
    scores = jnp.where(allowed[None], scores, -1e30)
    row_max = jnp.max(scores, axis=-1, keepdims=True)
    shifted = jnp.exp(scores - row_max)
    denominator = jnp.sum(shifted, axis=-1, keepdims=True)
    soft_weights = (shifted / denominator).astype(jnp.bfloat16)
    mixed = jnp.einsum("hqk,khd->qhd", soft_weights, value_row, preferred_element_type=jnp.float32)
    return (mixed.astype(jnp.bfloat16), row_max + jnp.log(denominator))


def self_backward(row_inputs):
    query_row, key_row, value_row, grad_row, log_row, local_row, whole_row = row_inputs
    allowed = local_row[:, None] == whole_row[None, :]
    scores = (
        jnp.einsum("qhd,khd->hqk", query_row, key_row, preferred_element_type=jnp.float32) * 0.125
    )
    soft_again = jnp.exp(jnp.where(allowed[None], scores, -1e30) - log_row)
    grad_soft = jnp.einsum("qhd,khd->hqk", grad_row, value_row, preferred_element_type=jnp.float32)
    grad_scores = (
        soft_again * (grad_soft - jnp.sum(soft_again * grad_soft, axis=-1, keepdims=True))
    ).astype(jnp.bfloat16)
    grad_query = (
        jnp.einsum("hqk,khd->qhd", grad_scores, key_row, preferred_element_type=jnp.float32) * 0.125
    )
    key_part = (
        jnp.einsum("hqk,qhd->khd", grad_scores, query_row, preferred_element_type=jnp.float32)
        * 0.125
    )
    value_part = jnp.einsum(
        "hqk,qhd->khd",
        soft_again.astype(jnp.bfloat16),
        grad_row,
        preferred_element_type=jnp.float32,
    )
    return (grad_query, key_part, value_part)


def on_device(
    frames,
    context,
    seg_lengths,
    bucket_ids,
    timesteps,
    bucket_weights,
    w_time_in,
    w_time_out,
    w_mod,
    w_qkv,
    w_attn_out,
    cross_gain,
    w_cross_q,
    w_cross_kv,
    w_cross_out,
    w_glu,
    w_down,
    cotangent,
):
    fwd_weights = (
        lax.all_gather(w_time_in, ("row", "seq"), axis=0, tiled=True),
        lax.all_gather(w_time_out, ("row", "seq"), axis=0, tiled=True),
        lax.all_gather(w_mod, ("row", "seq"), axis=0, tiled=True),
        lax.all_gather(w_qkv, ("row", "seq"), axis=0, tiled=True),
        lax.all_gather(w_attn_out, ("row", "seq"), axis=0, tiled=True),
        lax.all_gather(cross_gain, ("row", "seq"), axis=0, tiled=True),
        lax.all_gather(w_cross_q, ("row", "seq"), axis=0, tiled=True),
        lax.all_gather(w_cross_kv, ("row", "seq"), axis=0, tiled=True),
        lax.all_gather(w_cross_out, ("row", "seq"), axis=0, tiled=True),
        lax.all_gather(w_glu, ("row", "seq"), axis=0, tiled=True),
        lax.all_gather(w_down, ("row", "seq"), axis=0, tiled=True),
    )
    (
        time_in,
        time_out,
        modul,
        qkv_w,
        attn_w,
        gain_w,
        crossq_w,
        crosskv_w,
        crossout_w,
        glu_w,
        down_w,
    ) = fwd_weights
    rows_here = frames.shape[0]
    frames_here = frames.shape[1]
    text_len = context.shape[1]
    row_start = lax.axis_index("row") * rows_here
    seq_start = lax.axis_index("seq") * frames_here
    my_buckets = lax.dynamic_slice_in_dim(bucket_ids, row_start, rows_here)
    onehot = (my_buckets[:, None] == jnp.arange(BUCKETS, dtype=jnp.int32)[None, :]).astype(
        jnp.float32
    )
    my_times = jnp.dot(onehot, timesteps.astype(jnp.float32), precision=highest)
    features, pre_hidden, time_hidden, time_token, token_act, modulation = stamp_rows(
        my_times, time_in, time_out, modul
    )
    shift_attn = modulation[:, None, 0:D]
    scale_attn = modulation[:, None, D : 2 * D]
    gate_attn = modulation[:, None, 2 * D : 3 * D]
    shift_ffn = modulation[:, None, 3 * D : 4 * D]
    scale_ffn = modulation[:, None, 4 * D : 5 * D]
    gate_ffn = modulation[:, None, 5 * D : 6 * D]
    bounds = jnp.cumsum(seg_lengths, axis=-1)
    all_positions = jnp.arange(LENGTH, dtype=jnp.int32)
    all_ids = jnp.sum(
        (all_positions[None, :, None] >= bounds[:, None, :]).astype(jnp.int32), axis=-1
    )
    local_ids = lax.dynamic_slice_in_dim(all_ids, seq_start, frames_here, 1)
    cosine, sine_table = angle_tables(
        (seq_start + jnp.arange(frames_here, dtype=jnp.int32)).astype(jnp.float32)
    )
    inputs = frames.astype(jnp.float32)
    normed_a, inv_a = layer_stats(inputs)
    attn_in = (normed_a * (1.0 + scale_attn) + shift_attn).astype(jnp.bfloat16)
    projected = matmul(attn_in, qkv_w)
    query_pre = projected[..., :D].reshape(rows_here, frames_here, HEADS, HEAD_DIM)
    key_pre = projected[..., D : 2 * D].reshape(rows_here, frames_here, HEADS, HEAD_DIM)
    value_pre = projected[..., 2 * D :].reshape(rows_here, frames_here, HEADS, HEAD_DIM)
    queries = rotate(query_pre, cosine, sine_table).astype(jnp.bfloat16)
    key_local = rotate(key_pre, cosine, sine_table).astype(jnp.bfloat16)
    value_local = value_pre.astype(jnp.bfloat16)
    key_rows, value_rows = (
        lax.all_gather(key_local, "seq", axis=1, tiled=True),
        lax.all_gather(value_local, "seq", axis=1, tiled=True),
    )
    mixed_rows, log_total = lax.map(
        self_forward, (queries, key_rows, value_rows, local_ids, all_ids)
    )
    attn_mixed = mixed_rows.reshape(rows_here, frames_here, D)
    attn_out = matmul(attn_mixed, attn_w)
    after_attn = inputs + gate_attn * attn_out
    normed_c, inv_c = layer_stats(after_attn)
    gain_values = gain_w.astype(jnp.float32)
    cross_in = (normed_c * gain_values).astype(jnp.bfloat16)
    cross_q = (
        matmul(cross_in, crossq_w)
        .astype(jnp.bfloat16)
        .reshape(rows_here, frames_here, HEADS, HEAD_DIM)
    )
    cross_kv = jnp.einsum(
        "rcm,me->rce", context, crosskv_w, preferred_element_type=jnp.float32
    ).astype(jnp.bfloat16)
    cross_k = cross_kv[..., :D].reshape(rows_here, text_len, HEADS, HEAD_DIM)
    cross_v = cross_kv[..., D:].reshape(rows_here, text_len, HEADS, HEAD_DIM)
    cross_scores = (
        jnp.einsum("rqhd,rchd->rhqc", cross_q, cross_k, preferred_element_type=jnp.float32) * 0.125
    )
    cross_shift = jnp.exp(cross_scores - jnp.max(cross_scores, axis=-1, keepdims=True))
    cross_soft = cross_shift / jnp.sum(cross_shift, axis=-1, keepdims=True)
    cross_soft_low = cross_soft.astype(jnp.bfloat16)
    cross_mixed = (
        jnp.einsum("rhqc,rchd->rqhd", cross_soft_low, cross_v, preferred_element_type=jnp.float32)
        .reshape(rows_here, frames_here, D)
        .astype(jnp.bfloat16)
    )
    cross_out = matmul(cross_mixed, crossout_w)
    after_cross = after_attn + cross_out
    normed_f, inv_f = layer_stats(after_cross)
    ffn_in = (normed_f * (1.0 + scale_ffn) + shift_ffn).astype(jnp.bfloat16)
    gate_up = matmul(ffn_in, glu_w)
    gate_pre = gate_up[..., :FF]
    up_pre = gate_up[..., FF:]
    gate_act = jax.nn.silu(gate_pre)
    hidden = (gate_act * up_pre).astype(jnp.bfloat16)
    ffn_out = matmul(hidden, down_w)
    result = (after_cross + gate_ffn * ffn_out).astype(jnp.bfloat16)
    bwd_weights = (
        lax.all_gather(w_time_in, ("row", "seq"), axis=0, tiled=True),
        lax.all_gather(w_time_out, ("row", "seq"), axis=0, tiled=True),
        lax.all_gather(w_mod, ("row", "seq"), axis=0, tiled=True),
        lax.all_gather(w_qkv, ("row", "seq"), axis=0, tiled=True),
        lax.all_gather(w_attn_out, ("row", "seq"), axis=0, tiled=True),
        lax.all_gather(cross_gain, ("row", "seq"), axis=0, tiled=True),
        lax.all_gather(w_cross_q, ("row", "seq"), axis=0, tiled=True),
        lax.all_gather(w_cross_kv, ("row", "seq"), axis=0, tiled=True),
        lax.all_gather(w_cross_out, ("row", "seq"), axis=0, tiled=True),
        lax.all_gather(w_glu, ("row", "seq"), axis=0, tiled=True),
        lax.all_gather(w_down, ("row", "seq"), axis=0, tiled=True),
    )
    (
        time_in,
        time_out,
        modul,
        qkv_w,
        attn_w,
        gain_w,
        crossq_w,
        crosskv_w,
        crossout_w,
        glu_w,
        down_w,
    ) = bwd_weights
    row_scale = jnp.dot(onehot, bucket_weights, precision=highest)
    grad_out = cotangent.astype(jnp.float32) * row_scale[:, None, None]
    grad_ffn_low = (gate_ffn * grad_out).astype(jnp.bfloat16)
    dgate_ffn = jnp.sum(grad_out * ffn_out, axis=1)
    grad_down = outer_sum(hidden, grad_ffn_low)
    grad_hidden = matmul_t(grad_ffn_low, down_w)
    grad_gate_up = jnp.concatenate(
        [grad_hidden * up_pre * silu_slope(gate_pre), grad_hidden * gate_act], axis=-1
    ).astype(jnp.bfloat16)
    grad_glu = outer_sum(ffn_in, grad_gate_up)
    grad_ffn_in = matmul_t(grad_gate_up, glu_w)
    dshift_ffn = jnp.sum(grad_ffn_in, axis=1)
    dscale_ffn = jnp.sum(grad_ffn_in * normed_f, axis=1)
    grad_cross = grad_out + norm_back(grad_ffn_in * (1.0 + scale_ffn), normed_f, inv_f)
    ffn_grads = (
        lax.psum_scatter(grad_glu, ("row", "seq"), scatter_dimension=0, tiled=True),
        lax.psum_scatter(grad_down, ("row", "seq"), scatter_dimension=0, tiled=True),
    )
    grad_cross_low = grad_cross.astype(jnp.bfloat16)
    grad_crossout = outer_sum(cross_mixed, grad_cross_low)
    grad_cmixed = (
        matmul_t(grad_cross_low, crossout_w)
        .astype(jnp.bfloat16)
        .reshape(rows_here, frames_here, HEADS, HEAD_DIM)
    )
    grad_csoft = jnp.einsum(
        "rqhd,rchd->rhqc", grad_cmixed, cross_v, preferred_element_type=jnp.float32
    )
    grad_cvalue = jnp.einsum(
        "rhqc,rqhd->rchd", cross_soft_low, grad_cmixed, preferred_element_type=jnp.float32
    )
    grad_cscores = (
        cross_soft * (grad_csoft - jnp.sum(cross_soft * grad_csoft, axis=-1, keepdims=True))
    ).astype(jnp.bfloat16)
    grad_cquery = (
        (
            jnp.einsum("rhqc,rchd->rqhd", grad_cscores, cross_k, preferred_element_type=jnp.float32)
            * 0.125
        )
        .reshape(rows_here, frames_here, D)
        .astype(jnp.bfloat16)
    )
    grad_ckey = (
        jnp.einsum("rhqc,rqhd->rchd", grad_cscores, cross_q, preferred_element_type=jnp.float32)
        * 0.125
    )
    grad_ckv = jnp.concatenate(
        [grad_ckey.reshape(rows_here, text_len, D), grad_cvalue.reshape(rows_here, text_len, D)],
        axis=-1,
    )
    grad_crosskv = jnp.einsum(
        "rcm,rce->me", context.astype(jnp.float32), grad_ckv, precision=highest
    )
    grad_crossq = outer_sum(cross_in, grad_cquery)
    grad_cross_in = matmul_t(grad_cquery, crossq_w)
    grad_gain = jnp.sum(grad_cross_in * normed_c, axis=(0, 1))
    grad_attn = grad_cross + norm_back(grad_cross_in * gain_values, normed_c, inv_c)
    grad_attn_low = (gate_attn * grad_attn).astype(jnp.bfloat16)
    dgate_attn = jnp.sum(grad_attn * attn_out, axis=1)
    grad_attnout = outer_sum(attn_mixed, grad_attn_low)
    grad_amixed = (
        matmul_t(grad_attn_low, attn_w)
        .astype(jnp.bfloat16)
        .reshape(rows_here, frames_here, HEADS, HEAD_DIM)
    )
    grad_query, key_part, value_part = lax.map(
        self_backward, (queries, key_rows, value_rows, grad_amixed, log_total, local_ids, all_ids)
    )
    grad_key, grad_value = (
        lax.psum_scatter(
            key_part.astype(jnp.bfloat16), "seq", scatter_dimension=1, tiled=True
        ).astype(jnp.float32),
        lax.psum_scatter(
            value_part.astype(jnp.bfloat16), "seq", scatter_dimension=1, tiled=True
        ).astype(jnp.float32),
    )
    grad_projected = jnp.concatenate(
        [
            rotate(grad_query, cosine, -sine_table).reshape(rows_here, frames_here, D),
            rotate(grad_key, cosine, -sine_table).reshape(rows_here, frames_here, D),
            grad_value.reshape(rows_here, frames_here, D),
        ],
        axis=-1,
    ).astype(jnp.bfloat16)
    grad_qkv = outer_sum(attn_in, grad_projected)
    grad_attn_in = matmul_t(grad_projected, qkv_w)
    dshift_attn = jnp.sum(grad_attn_in, axis=1)
    dscale_attn = jnp.sum(grad_attn_in * normed_a, axis=1)
    grad_frames = grad_attn + norm_back(grad_attn_in * (1.0 + scale_attn), normed_a, inv_a)
    grad_rows = jnp.concatenate(
        [dshift_attn, dscale_attn, dgate_attn, dshift_ffn, dscale_ffn, dgate_ffn], axis=-1
    )
    grad_modul = jnp.dot(token_act.astype(jnp.float32).T, grad_rows, precision=highest)
    grad_token = jnp.dot(grad_rows, modul.astype(jnp.float32).T, precision=highest) * silu_slope(
        time_token
    )
    grad_timeout = jnp.dot(time_hidden.astype(jnp.float32).T, grad_token, precision=highest)
    grad_pre = jnp.dot(grad_token, time_out.astype(jnp.float32).T, precision=highest) * silu_slope(
        pre_hidden
    )
    grad_timein = jnp.dot(features.astype(jnp.float32).T, grad_pre, precision=highest)
    rest_grads = (
        lax.psum_scatter(grad_timein, ("row", "seq"), scatter_dimension=0, tiled=True),
        lax.psum_scatter(grad_timeout, ("row", "seq"), scatter_dimension=0, tiled=True),
        lax.psum_scatter(grad_modul, ("row", "seq"), scatter_dimension=0, tiled=True),
        lax.psum_scatter(grad_qkv, ("row", "seq"), scatter_dimension=0, tiled=True),
        lax.psum_scatter(grad_attnout, ("row", "seq"), scatter_dimension=0, tiled=True),
        lax.psum_scatter(grad_gain, ("row", "seq"), scatter_dimension=0, tiled=True),
        lax.psum_scatter(grad_crossq, ("row", "seq"), scatter_dimension=0, tiled=True),
        lax.psum_scatter(grad_crosskv, ("row", "seq"), scatter_dimension=0, tiled=True),
        lax.psum_scatter(grad_crossout, ("row", "seq"), scatter_dimension=0, tiled=True),
    )
    shard_timein, shard_timeout, shard_modul = (rest_grads[0], rest_grads[1], rest_grads[2])
    block_grads = rest_grads[3:]
    return (
        result,
        grad_frames,
        shard_timein,
        shard_timeout,
        shard_modul,
        block_grads[0],
        block_grads[1],
        block_grads[2],
        block_grads[3],
        block_grads[4],
        block_grads[5],
        ffn_grads[0],
        ffn_grads[1],
    )


def can_split(rows, seqs):
    power = lambda n: n & (n - 1) == 0
    return (
        power(rows)
        and power(seqs)
        and HEADS % (2 * seqs) == 0
        and D % (rows * seqs) == 0
        and FF % (rows * seqs) == 0
        and LENGTH % (seqs * 512) == 0
    )


def on_device_split(
    rows,
    seqs,
    frames,
    context,
    seg_lengths,
    bucket_ids,
    timesteps,
    bucket_weights,
    w_time_in,
    w_time_out,
    w_mod,
    w_qkv,
    w_attn_out,
    cross_gain,
    w_cross_q,
    w_cross_kv,
    w_cross_out,
    w_glu,
    w_down,
    cotangent,
):
    my_row = lax.axis_index("row")
    row_order = my_row ^ jnp.arange(rows, dtype=jnp.int32)
    hits = jnp.arange(BUCKETS, dtype=jnp.int32)[:, None] == bucket_ids[row_order][None, :]
    hits = hits.astype(jnp.float32)
    my_seq = lax.axis_index("seq")
    flat = my_row * seqs + my_seq
    sizes = {"row": rows, "seq": seqs}

    def swap(value, axis, j):
        return lax.ppermute(value, axis, [(i, i ^ j) for i in range(sizes[axis])])

    def sum_over(value, axis):
        j = 1
        while j < sizes[axis]:
            value = value + swap(value, axis, j)
            j *= 2
        return value

    def sum_all(value):
        return sum_over(sum_over(value, "seq"), "row")

    def pick(stack, axis_name, j, dim=0):
        me = my_row if axis_name == "row" else my_seq
        return lax.dynamic_index_in_dim(stack, me ^ j, dim, keepdims=False)

    def natural(slots, axis_name="seq"):
        stack = jnp.stack(slots)
        return jnp.stack([pick(stack, axis_name, t) for t in range(len(slots))])

    def exchange_lines(stack, dim):
        pieces = [
            lax.dynamic_index_in_dim(stack, (my_row // 2) ^ j, dim, keepdims=False)
            for j in range(rows // 2)
        ]
        return [pieces[0]] + [swap(p, "row", 2 * j) for j, p in enumerate(pieces) if j]

    def exchange(stack, dim=0, axis_name="seq"):
        pieces = [pick(stack, axis_name, j, dim) for j in range(sizes[axis_name])]
        return [pieces[0]] + [swap(p, axis_name, j) for j, p in enumerate(pieces) if j]

    def spread(value, axis_name="seq"):
        return [value] + [swap(value, axis_name, j) for j in range(1, sizes[axis_name])]

    def after(value, *others):
        return lax.optimization_barrier((value,) + others)[0]

    def spread_two(value):
        if seqs != 4:
            return spread(value), None
        near = [swap(value, "seq", 1), swap(value, "seq", 2)]
        return [value] + near, near

    def opposite_halves(near):
        half = near[0].shape[0] // 2
        return [swap(near[1][:half], "seq", 1), swap(near[0][half:], "seq", 2)]

    def opposite(near):
        return jnp.concatenate(opposite_halves(near))

    def spread_row(value):
        both = jnp.stack([value, swap(value, "row", 1)])
        lines = [both] + [swap(both, "row", 2 * j) for j in range(1, rows // 2)]
        return [line[c] for line in lines for c in range(2)]

    def columns(values, axis_name, j, width, start=0):
        me = my_row if axis_name == "row" else my_seq
        return lax.dynamic_slice_in_dim(values, start + (me ^ j) * width, width, 1)

    def side_by_side(slots):
        stack = jnp.stack(slots)
        return jnp.concatenate([pick(stack, "seq", t) for t in range(seqs)], axis=1)

    def mine(values, width):
        return lax.dynamic_slice_in_dim(values, flat * width, width, values.ndim - 1)

    def dot(left, right):
        return jnp.dot(left, right, preferred_element_type=jnp.float32)

    def dot_right_t(left, right):
        return jnp.einsum("fj,ij->fi", left, right, preferred_element_type=jnp.float32)

    def dot_left_t(left, right):
        return jnp.einsum("fi,fj->ij", left, right, preferred_element_type=jnp.float32)

    low = jnp.bfloat16
    frames_here = frames.shape[1]
    text_len, ctx_dim = context.shape[1:]
    local_heads = D // seqs
    depth = w_qkv.shape[0]
    part = FF // (rows * seqs)
    x_own = frames[0]

    kv_width = 2 * D // seqs
    first_pieces = [
        jnp.concatenate(
            [columns(w_qkv, "seq", j, local_heads, k * D) for k in range(3)]
            + [
                jnp.concatenate(
                    [
                        columns(w_cross_kv, "seq", j, kv_width)[:, : kv_width // 2],
                        columns(w_cross_kv, "seq", j, kv_width)[:, kv_width // 2 :],
                    ]
                )
            ],
            axis=1,
        )
        for j in range(seqs)
    ]
    first_slots = [first_pieces[0]] + [swap(p, "seq", j) for j, p in enumerate(first_pieces) if j]
    first_w = natural(first_slots).reshape(seqs * depth, -1)
    first_w = jnp.concatenate([first_w, w_down])
    first_w = lax.all_gather(first_w, "row", axis=0, tiled=True).reshape(rows, -1, D)
    kv_w = first_w[:, : seqs * depth, 3 * local_heads :].reshape(rows * seqs, 2, depth // 2, -1)
    kv_w = jnp.concatenate([kv_w[:, h].reshape(ctx_dim, -1) for h in range(2)], axis=1)

    features = time_features(timesteps.astype(jnp.float32)).astype(low)
    pre_part = dot(mine(features, w_time_in.shape[0]), w_time_in)
    gain_part = lax.dynamic_update_slice(
        jnp.zeros((1, D), jnp.float32), cross_gain.astype(jnp.float32)[None], (0, flat * depth)
    )
    pre_hidden = sum_over(after(jnp.concatenate([pre_part, gain_part]), *first_slots), "seq")
    x_slots, near = spread_two(after(x_own, pre_hidden))
    pre_hidden = sum_over(pre_hidden, "row")
    gain_values = pre_hidden[BUCKETS:]
    pre_hidden = pre_hidden[:BUCKETS]
    time_hidden = jax.nn.silu(pre_hidden).astype(low)
    time_token = sum_over(dot(mine(time_hidden, depth), w_time_out), "row")
    if near is not None:
        time_token, *near = lax.optimization_barrier((time_token, *near))
    wide_w = jnp.concatenate([w_attn_out, w_cross_q, w_cross_out], axis=1)
    wide_w = lax.all_gather(after(wide_w, time_token), ("row", "seq"), axis=0, tiled=True)
    attn_w, crossq_w, crossout_w = wide_w[:, :D], wide_w[:, D : 2 * D], wide_w[:, 2 * D :]
    time_token = sum_over(time_token, "seq")
    if near is not None:
        time_token, *near = lax.optimization_barrier((time_token, *near))
        x_slots = [x_own, *near, opposite(near)]
    token_act = jax.nn.silu(time_token).astype(low)
    mod_part = dot(mine(token_act, depth), w_mod)
    mod_part, *x_slots = lax.optimization_barrier((mod_part, *x_slots))
    glu_slots = exchange(split_units(after(w_glu, x_slots[-1]), seqs, part))
    row_part = lambda j: lax.dynamic_index_in_dim(mod_part, bucket_ids[my_row ^ j], 0)
    modulation = row_part(0)
    for j in range(1, rows):
        modulation = modulation + swap(row_part(j), "row", j)
    modulation = sum_over(modulation, "seq")
    shift_attn, scale_attn, gate_attn, shift_ffn, scale_ffn, gate_ffn = jnp.split(modulation, 6, axis=1)

    bounds = jnp.cumsum(seg_lengths[0])
    slot_seq = my_seq ^ jnp.arange(seqs, dtype=jnp.int32)
    positions = (slot_seq[:, None] * frames_here + jnp.arange(frames_here, dtype=jnp.int32)).reshape(-1)
    ids = jnp.sum((positions[:, None] >= bounds[None, :]).astype(jnp.int32), axis=-1)
    lane = jnp.arange(PAIR, dtype=jnp.int32)[None, :]
    same = ids[:, None] == lane
    key_mask = same.astype(low)
    query_mask = jnp.where((lane < seg_lengths.shape[1]) & ~same, -1e30, 0.0).astype(low)
    half_dim = HEAD_DIM // 2
    inverse = jnp.exp(-math.log(10000.0) * jnp.arange(half_dim, dtype=jnp.float32) / half_dim)
    angles = positions.astype(jnp.float32)[:, None] * inverse[None, :]
    cosine = jnp.tile(jnp.cos(angles), (1, PAIR // half_dim))
    sine = jnp.tile(jnp.concatenate([-jnp.sin(angles), jnp.sin(angles)], axis=1), (1, 2))
    masks, tables = (query_mask, key_mask), (cosine, sine)

    pairs = local_heads // PAIR
    slots = lambda values: values.reshape(seqs, frames_here, -1)
    attn_in, qkv = project(x_slots, 1.0 + scale_attn, shift_attn, first_w, 3 * local_heads, cosine, sine)
    row_scale = lax.dynamic_index_in_dim(bucket_weights, bucket_ids[my_row], 0)
    grad_out = cotangent[0].astype(jnp.float32) * row_scale
    kv_slots = spread(dot(context[0], kv_w).astype(low))
    qkv, *got = lax.optimization_barrier((qkv, *kv_slots, *glu_slots))
    kv_slots, glu_slots = got[:seqs], got[seqs:]
    glu_w = lax.all_gather(natural(glu_slots).reshape(seqs * depth, -1), "row", axis=0, tiled=True)
    mixed_heads, lse = attend(qkv, qkv, qkv, 0, pairs, 2 * pairs, pairs, LENGTH, masks)
    mixed_slots = slots(mixed_heads)
    mixed_got = [mixed_slots[0]] + [swap(mixed_slots[j], "seq", j) for j in range(1, seqs)]
    attn_mixed = side_by_side(mixed_got)
    attn_out = dot(attn_mixed, attn_w)
    cot_slots, _ = spread_two(after(cotangent[0], attn_out))
    inputs = x_own.astype(jnp.float32)
    after_attn = inputs + gate_attn * attn_out

    normed_c, inv_c = layer_stats(after_attn)
    cross_in = (normed_c * gain_values).astype(low)
    cross_q = dot(cross_in, crossq_w).astype(low)
    cross_kv = side_by_side(kv_slots)
    all_pairs = D // PAIR
    cross_mixed, cross_lse = attend(cross_q, cross_kv, cross_kv, 0, 0, all_pairs, all_pairs, frames_here)
    cross_mixed, cot_slots = lax.optimization_barrier((cross_mixed, cot_slots))
    after_cross = after_attn + dot(cross_mixed, crossout_w)

    normed_f, inv_f = layer_stats(after_cross)
    ffn_in = (normed_f * (1.0 + scale_ffn) + shift_ffn).astype(low)
    units = FF // seqs
    ffn_slots, near = spread_two(ffn_in)
    if near is not None:
        far_halves = (opposite_halves(near), opposite_halves(cot_slots[1:]))
    calls = [slice(0, 3), slice(3, 4)] if seqs == 4 else [slice(0, seqs)]
    kept, ffn_back, ffn_parts, dgate_ffn = None, [], [], 0.0
    scale_row = jnp.broadcast_to(row_scale[None], (1, D))
    for call in calls:
        if call.start == 3:
            far_halves, kept = lax.optimization_barrier((far_halves, kept))
            ffn_slots, cot_slots = [
                [*slots_here, jnp.concatenate(halves)]
                for slots_here, halves in zip((ffn_slots, cot_slots), far_halves)
            ]
        *kept, back, out, dgate = feed(
            ffn_slots[call], cot_slots[call], gate_ffn, scale_row, glu_w, first_w, call.start, seqs, kept
        )
        dgate_ffn = dgate_ffn + dgate
        ffn_back += [back[i : i + frames_here] for i in range(0, back.shape[0], frames_here)]
        ffn_parts += [out[i : i + frames_here] for i in range(0, out.shape[0], frames_here)]
    ffn_all, grad_ffn_all, hidden_all, grad_gate_up = kept

    def returned_near(parts):
        if seqs != 4:
            return [parts[0]] + [swap(parts[j], "seq", j) for j in range(1, seqs)]
        half = frames_here // 2
        return [
            swap(parts[3][:half], "seq", 1),
            swap(parts[3][half:], "seq", 2),
            swap(parts[1][:half], "seq", 1),
            swap(parts[2][half:], "seq", 2),
        ]

    def returned_far(parts, near):
        if seqs != 4:
            return near[1:], near[:1]
        half = frames_here // 2
        both = lambda left, right: left.astype(jnp.float32) + right.astype(jnp.float32)
        far = [
            swap(both(parts[2][:half], near[0]).astype(low), "seq", 2),
            swap(both(parts[1][half:], near[1]).astype(low), "seq", 1),
        ]
        return far, [both(parts[0][:half], near[2]), both(parts[0][half:], near[3])]

    def returned_total(far, near):
        if seqs != 4:
            return sum(term.astype(jnp.float32) for term in near + far)
        return jnp.concatenate([n + f.astype(jnp.float32) for n, f in zip(near, far)])

    ffn_back_near = returned_near(ffn_back)
    grad_glu = dot_left_t(ffn_all, grad_gate_up).astype(low)
    grad_down = dot_left_t(hidden_all, grad_ffn_all).astype(low)
    grad_glu, *ffn_back_near = lax.optimization_barrier((grad_glu, *ffn_back_near))
    ffn_back_far, ffn_back_own = returned_far(ffn_back, ffn_back_near)
    ffn_back_far, grad_down = lax.optimization_barrier((ffn_back_far, grad_down))
    grad_ffn_in, grad_glu, grad_down, *ffn_parts = lax.optimization_barrier(
        (returned_total(ffn_back_far, ffn_back_own), grad_glu, grad_down, *ffn_parts)
    )
    grad_glu = lax.psum_scatter(grad_glu, "row", scatter_dimension=0, tiled=True)
    grad_down = lax.psum_scatter(grad_down, "row", scatter_dimension=0, tiled=True)
    ffn_near = returned_near(ffn_parts)
    dshift_ffn = jnp.sum(grad_ffn_in, axis=0, keepdims=True)
    dscale_ffn = jnp.sum(grad_ffn_in * normed_f, axis=0, keepdims=True)
    grad_cross = grad_out + norm_back(grad_ffn_in * (1.0 + scale_ffn), normed_f, inv_f)

    grad_cross_low = grad_cross.astype(low)
    grad_cmixed = dot_right_t(grad_cross_low, crossout_w).astype(low)
    grad_cquery, grad_ckey, grad_cvalue = attend_back(
        cross_q, cross_kv, cross_kv, grad_cmixed, cross_mixed, cross_lse,
        0, 0, all_pairs, all_pairs, frames_here, text_len,
    )
    grad_cquery, *ffn_near = lax.optimization_barrier((grad_cquery, *ffn_near))
    grad_cross_in = dot_right_t(grad_cquery, crossq_w)
    grad_gain = jnp.sum(grad_cross_in * normed_c, axis=0, keepdims=True)
    grad_attn = grad_cross + norm_back(grad_cross_in * gain_values, normed_c, inv_c)

    grad_attn_low = (gate_attn * grad_attn).astype(low)
    dgate_attn = jnp.sum(grad_attn * attn_out, axis=0, keepdims=True)
    grad_amixed = dot_right_t(grad_attn_low, attn_w).astype(low)
    head_pieces = [columns(grad_amixed, "seq", j, local_heads) for j in range(seqs)]
    head_pieces = [head_pieces[0]] + [swap(p, "seq", j) for j, p in enumerate(head_pieces) if j]
    wide_left = [cross_mixed, cross_in, attn_mixed]
    for j in range(1, min(seqs, 4)):
        wide_left[j - 1], head_pieces[j] = lax.optimization_barrier((wide_left[j - 1], head_pieces[j]))
    cross_mixed, cross_in, attn_mixed = wide_left
    grad_heads = jnp.concatenate(head_pieces)

    core = my_row % 2
    wide_own = [
        dot_left_t(left, right).astype(low).reshape(rows // 2, 2, seqs, depth, D)
        for left, right in (
            (attn_mixed, grad_attn_low),
            (cross_in, grad_cquery),
            (cross_mixed, grad_cross_low),
        )
    ]
    half_of = lambda g, c: lax.dynamic_index_in_dim(g, c, 1, keepdims=False)
    wide_got = [swap(half_of(g, 1 - core), "row", 1) for g in wide_own]

    grad_ckv = jnp.concatenate([grad_ckey, grad_cvalue], axis=1).astype(low)
    grad_kv = text_product(context[0], grad_ckv)
    grad_heads, grad_kv, grad_down, *wide_got = lax.optimization_barrier(
        (grad_heads, grad_kv, grad_down, *wide_got)
    )
    grad_kv = lax.psum_scatter(grad_kv, "row", scatter_dimension=0, tiled=True)
    ffn_far, ffn_near = returned_far(ffn_parts, ffn_near)
    wide_both = [(half_of(own, core), got) for own, got in zip(wide_own, wide_got)]

    def wide_piece(j):
        both = [
            pick(own, "seq", j, 1).astype(jnp.float32) + pick(got, "seq", j, 1).astype(jnp.float32)
            for own, got in wide_both
        ]
        return jnp.stack(both, axis=1).astype(low)

    wide_got = [wide_piece(j) for j in range(seqs)]
    wide_got = [wide_got[0]] + [swap(piece, "seq", j) for j, piece in enumerate(wide_got) if j]
    grad_projected = jnp.concatenate(
        attend_back(
            qkv, qkv, qkv, grad_heads, mixed_heads, lse,
            0, pairs, 2 * pairs, pairs, LENGTH // 2, 512, masks, tables,
        ),
        axis=1,
    )
    grad_projected, grad_glu, wide_got, ffn_far = lax.optimization_barrier(
        (grad_projected, grad_glu, wide_got, ffn_far)
    )
    glu_got = exchange(after(grad_glu, grad_projected).reshape(seqs, depth, -1))
    grad_qkv = dot_left_t(attn_in, grad_projected).astype(low)
    grad_projected, grad_qkv = lax.optimization_barrier((grad_projected, grad_qkv))
    grad_qkv = lax.psum_scatter(grad_qkv, "row", scatter_dimension=0, tiled=True)
    attn_back, attn_sums = project_back(grad_projected, first_w, x_slots)
    attn_sums, attn_back, grad_down, grad_kv, glu_got = lax.optimization_barrier(
        (attn_sums, attn_back, grad_down, grad_kv, glu_got)
    )
    own_sums = jnp.concatenate([attn_sums, dgate_attn, dshift_ffn, dscale_ffn, dgate_ffn, grad_gain])
    own_sums = sum_over(own_sums, "seq")
    own_sums, attn_back = lax.optimization_barrier((own_sums, attn_back))
    attn_back = slots(attn_back)
    attn_near = returned_near(attn_back)

    sums_list = spread_row(own_sums)
    ffn_far, sums_list[1] = lax.optimization_barrier((ffn_far, sums_list[1]))
    sums_list, attn_near, grad_qkv = lax.optimization_barrier((sums_list, attn_near, grad_qkv))
    wide = sum(g.astype(jnp.float32) for g in after(tuple(wide_got), grad_qkv)).astype(low)
    grad_wide = lax.psum_scatter(
        wide,
        "row",
        scatter_dimension=0,
        axis_index_groups=[list(range(c, rows, 2)) for c in range(2)],
        tiled=True,
    )[0].astype(jnp.float32)
    total = sum(hits[:, j, None, None] * sums for j, sums in enumerate(sums_list))
    grad_mods = total[:, :6].reshape(BUCKETS, 6 * D)
    gain_total = jnp.sum(total[:, 6], axis=0)

    def gather_row(slots):
        return natural(slots, "row").transpose(1, 0, 2).reshape(BUCKETS, -1)

    def gather_seq(own):
        return natural(spread(own)).transpose(1, 0, 2).reshape(BUCKETS, -1)

    grad_modul = outer(mine(token_act, depth).astype(jnp.float32), grad_mods)
    token_own = jnp.dot(grad_mods, w_mod.astype(jnp.float32).T, precision=highest)
    token_own = token_own * silu_slope(mine(time_token, depth))
    token_seq = gather_seq(token_own)
    token_seq, *attn_near = lax.optimization_barrier((token_seq, *attn_near))
    attn_far, attn_own = returned_far(attn_back, attn_near)
    token_slots, attn_far = lax.optimization_barrier((spread_row(token_seq), attn_far))
    result = (after_cross + gate_ffn * returned_total(ffn_far, ffn_near)).astype(low)
    grad_token = gather_row(token_slots)
    grad_timeout = outer(mine(time_hidden, depth).astype(jnp.float32), grad_token)
    hidden_own = jnp.dot(grad_token, w_time_out.astype(jnp.float32).T, precision=highest)
    hidden_own = hidden_own * silu_slope(mine(pre_hidden, depth))
    grad_attn_in = returned_total(attn_far, attn_own)
    kv_stack = grad_kv.reshape(seqs, depth // 2, 2 * D)
    kv_stack = jnp.concatenate([kv_stack[..., :D], kv_stack[..., D:]], axis=1)
    qkv_stack = jnp.concatenate([grad_qkv.reshape(seqs, depth, -1), kv_stack], axis=2)
    qkv_stack, hidden_own = lax.optimization_barrier((qkv_stack, hidden_own))
    qkv_got = exchange(qkv_stack)
    hidden_seq, *qkv_got = lax.optimization_barrier((gather_seq(hidden_own), *qkv_got))
    grad_pre = gather_row(spread_row(hidden_seq))
    grad_timein = outer(mine(features, w_time_in.shape[0]).astype(jnp.float32), grad_pre)
    normed_a, inv_a = layer_stats(inputs)
    grad_frames = grad_attn + norm_back(grad_attn_in * (1.0 + scale_attn), normed_a, inv_a)

    qkv_list = qkv_got
    qkv_got = jnp.stack(qkv_got)
    grad_qkv = jnp.concatenate(
        [
            pick(qkv_got, "seq", t)[:, k * local_heads : (k + 1) * local_heads]
            for k in range(3)
            for t in range(seqs)
        ],
        axis=1,
    )
    grad_glu = join_units(natural(glu_got), part)
    grad_crosskv = sum(piece[:, 3 * local_heads :].astype(jnp.float32) for piece in qkv_list)
    grad_crosskv = jnp.concatenate([grad_crosskv[: depth // 2], grad_crosskv[depth // 2 :]], axis=1)

    return (
        result[None],
        grad_frames[None],
        grad_timein,
        grad_timeout,
        grad_modul,
        grad_qkv.astype(jnp.float32),
        grad_wide[0],
        mine(gain_total, depth),
        grad_wide[1],
        grad_crosskv,
        grad_wide[2],
        grad_glu,
        grad_down.astype(jnp.float32),
    )


def solution(mesh):
    placed = (
        P("row", "seq", None),
        P("row", None, None),
        P("row", None),
        P(),
        P(),
        P(),
        P(("row", "seq"), None),
        P(("row", "seq"), None),
        P(("row", "seq"), None),
        P(("row", "seq"), None),
        P(("row", "seq"), None),
        P(("row", "seq")),
        P(("row", "seq"), None),
        P(("row", "seq"), None),
        P(("row", "seq"), None),
        P(("row", "seq"), None),
        P(("row", "seq"), None),
        P("row", "seq", None),
    )
    rows, seqs = mesh.shape["row"], mesh.shape["seq"]
    plan = functools.partial(on_device_split, rows, seqs) if can_split(rows, seqs) else on_device
    return jax.shard_map(
        plan,
        mesh=mesh,
        in_specs=placed,
        out_specs=(
            P("row", "seq", None),
            P("row", "seq", None),
            P(("row", "seq"), None),
            P(("row", "seq"), None),
            P(("row", "seq"), None),
            P(("row", "seq"), None),
            P(("row", "seq"), None),
            P(("row", "seq")),
            P(("row", "seq"), None),
            P(("row", "seq"), None),
            P(("row", "seq"), None),
            P(("row", "seq"), None),
            P(("row", "seq"), None),
        ),
        check_vma=False,
    )
```
